32 devices in a mesh: roi: 8 (over z, x), col: 4 (over y, core).
Axes of the slice: x: 2, y: 2, z: 4, core: 2. Of those that a mesh axis runs over, the one named last changes fastest.
Arguments:
- p2: bfloat16 [8, 256, 65536], P('roi', 'col'), may hold values from -120 to 120
- p3: bfloat16 [8, 256, 16384], P('roi', 'col'), may hold values from -120 to 120
- p4: bfloat16 [8, 256, 4096], P('roi', 'col'), may hold values from -120 to 120
- p5: bfloat16 [8, 256, 1024], P('roi', 'col'), may hold values from -120 to 120
- norm_gain: float32 [256], P('col'), may hold values from 0.5 to 1.5
- norm_bias: float32 [256], P('col'), may hold values from -3 to 3
- fc6_weight: bfloat16 [12544, 1024], P('roi', 'col'), may hold values from -0.0546875 to 0.0546875
- fc6_bias: float32 [1024], P('col'), may hold values from -3 to 3
- fc7_weight: bfloat16 [1024, 1024], P('roi', 'col'), may hold values from -0.1875 to 0.1875
- fc7_bias: bfloat16 [1024], P(('roi', 'col')), may hold values from -3 to 3
- cls_weight: bfloat16 [1024, 81], P(('roi', 'col')), may hold values from -0.59765625 to 0.59765625
- cls_bias: float32 [81], replicated, may hold values from -4 to 4
- box_weight: bfloat16 [1024, 4], P(('roi', 'col')), may hold values from -0.1875 to 0.1875
- box_bias: float32 [4], replicated, may hold values from -3 to 3
- roi_boxes: int32 [4, 3072], P(None, 'roi'), may hold values from 0 to 512, as said below
- roi_level: int32 [3072], P('roi'), may hold values from 0 to 3
- roi_image: int32 [3072], P('roi'), may hold values from 0 to 3
- canvas_offsets: int32 [2, 32], P(None, 'roi'), may hold values from 0 to 544, as said below
- labels: int32 [3072], P('roi'), may hold values from 0 to 80
- target_boxes: int32 [4, 3072], P(None, 'roi'), may hold values from -128 to 640, as said below
- valid: int32 [3072], P('roi'), may hold values from 0 to 1, as said below
Outputs:
- cls_loss: float32 [], replicated
- box_loss: float32 [], replicated
- decoded_boxes: float32 [4, 3072], P(None, ('roi', 'col'))
- p2_grad: float32 [8, 256, 65536], P('roi', 'col')
- p3_grad: float32 [8, 256, 16384], P('roi', 'col')
- p4_grad: float32 [8, 256, 4096], P('roi', 'col')
- p5_grad: float32 [8, 256, 1024], P('roi', 'col')
- norm_gain_grad: float32 [256], P('col')
- norm_bias_grad: float32 [256], P('col')
- fc6_weight_grad: float32 [12544, 1024], P('roi', 'col')
- fc6_bias_grad: float32 [1024], P('col')
- fc7_weight_grad: float32 [1024, 1024], P('roi', 'col')
- fc7_bias_grad: float32 [1024], P(('roi', 'col'))
- cls_weight_grad: float32 [1024, 81], P(('roi', 'col'))
- cls_bias_grad: float32 [81], replicated
- box_weight_grad: float32 [1024, 4], P(('roi', 'col'))
- box_bias_grad: float32 [4], replicated
The draws below stay inside these ranges and needn't reach their ends.
Inputs may be any that keep to these rules, and one draw needn't show every extreme that they name: `roi_boxes`: each box has positive width and height and lies inside its image, whose content spans 480 pixels; the box side grows with the level. `canvas_offsets`: image g sits in quadrant g mod 4 of its canvas. `target_boxes`: each target box has positive width and height. The first region of each canvas is valid.
All inputs are finite; a program needn't handle non-finite values.
Results may differ from the reference program's by a relative error of at most 0.018.
Values may be sent and summed in bfloat16 or wider, within the bound.
A program may use at most 256 MiB of HBM per device.

```python
import math
import jax
import jax.numpy as jnp
from jax import lax

C = 256
FC = 1024
CLASSES = 81
R_DEV = 384
CANVAS = 1024
FLAT = 12544
CANVASES = 8
IMAGES = 32
ROIS = 3072


def region_table(key):
    base = jax.random.fold_in(key, 11)
    keys = jax.random.split(base, 15)
    half_side = CANVAS // 2
    content = half_side - half_side // 16
    layered = jax.random.randint(keys[0], (ROIS,), 0, 8)
    level_ids = (layered >= 4).astype(jnp.int32) + (layered >= 6).astype(jnp.int32) + (layered >= 7).astype(jnp.int32)
    lowest = jnp.where(level_ids == 0, content // 30, jnp.where(level_ids == 1, content // 10, jnp.where(level_ids == 2, content // 4, content // 2))).astype(jnp.int32)
    side_x = lowest + jax.random.randint(keys[1], (ROIS,), 0, lowest)
    side_y = lowest + jax.random.randint(keys[2], (ROIS,), 0, lowest)
    left_edge = jax.random.randint(keys[3], (ROIS,), 0, content - side_x + 1)
    top_edge = jax.random.randint(keys[4], (ROIS,), 0, content - side_y + 1)
    boxes = jnp.stack([left_edge, top_edge, left_edge + side_x, top_edge + side_y]).astype(jnp.int32)
    reach_x = side_x // 4
    reach_y = side_y // 4
    move_a = jax.random.randint(keys[5], (ROIS,), -reach_x, reach_x + 1)
    move_b = jax.random.randint(keys[6], (ROIS,), -reach_y, reach_y + 1)
    move_c = jax.random.randint(keys[7], (ROIS,), -reach_x, reach_x + 1)
    move_d = jax.random.randint(keys[8], (ROIS,), -reach_y, reach_y + 1)
    goals = jnp.stack([left_edge + move_a, top_edge + move_b, left_edge + side_x + move_c, top_edge + side_y + move_d]).astype(jnp.int32)
    image_ids = jax.random.randint(keys[9], (ROIS,), 0, 4)
    quadrant = jnp.arange(IMAGES, dtype=jnp.int32) % 4
    offsets = jnp.stack([quadrant % 2 * half_side + jax.random.randint(keys[10], (IMAGES,), 0, half_side // 16 + 1), quadrant // 2 * half_side + jax.random.randint(keys[11], (IMAGES,), 0, half_side // 16 + 1)]).astype(jnp.int32)
    classes = jnp.where(jax.random.randint(keys[12], (ROIS,), 0, 4) == 0, 0, jax.random.randint(keys[13], (ROIS,), 1, CLASSES)).astype(jnp.int32)
    positions = jnp.arange(ROIS, dtype=jnp.int32)
    canvas_ids = positions // R_DEV
    chance = jax.random.randint(keys[14], (ROIS,), 0, 3 * CANVASES)
    flags = ((chance < CANVASES + 2 * canvas_ids) | (positions % R_DEV == 0)).astype(jnp.int32)
    return (boxes, level_ids.astype(jnp.int32), image_ids.astype(jnp.int32), offsets, classes, goals, flags)


def draw_roi_boxes(key, part):
    return region_table(key)[0]


def draw_roi_level(key, part):
    return region_table(key)[1]


def draw_roi_image(key, part):
    return region_table(key)[2]


def draw_canvas_offsets(key, part):
    return region_table(key)[3]


def draw_labels(key, part):
    return region_table(key)[4]


def draw_target_boxes(key, part):
    return region_table(key)[5]


def draw_valid(key, part):
    return region_table(key)[6]


def feature_map(key, cell_count):
    keys = jax.random.split(key, 3)
    growth = 1.0 + 2.0 * jnp.arange(CANVASES, dtype=jnp.float32) / max(CANVASES - 1, 1)
    cells = cell_count * cell_count
    noise = jnp.clip(jax.random.normal(keys[0], (CANVASES, C, cells), jnp.float32), -4.0, 4.0)
    spread = jnp.exp(jax.random.uniform(keys[1], (C,), jnp.float32, 0.0, 1.1))
    centre = jnp.clip(0.5 * jax.random.normal(keys[2], (C,), jnp.float32), -2.0, 2.0)
    values = (centre[None, :, None] + noise) * spread[None, :, None] * growth[:, None, None]
    return values.astype(jnp.bfloat16)


def draw_p2(key, part):
    return feature_map(jax.random.fold_in(key, 2), CANVAS // 4)


def draw_p3(key, part):
    return feature_map(jax.random.fold_in(key, 3), CANVAS // 8)


def draw_p4(key, part):
    return feature_map(jax.random.fold_in(key, 4), CANVAS // 16)


def draw_p5(key, part):
    return feature_map(jax.random.fold_in(key, 5), CANVAS // 32)


def steps_of(own_key, dims, shards, smallest, largest):
    loudness = 1.0
    for axis_at, parts in shards:
        heights = jax.random.uniform(jax.random.fold_in(jax.random.fold_in(own_key, 6), axis_at), (parts,), jnp.float32, smallest / len(shards), largest / len(shards))
        loudness = loudness * jnp.repeat(jnp.exp(heights), dims[axis_at] // parts).reshape((-1,) + (1,) * (len(dims) - 1 - axis_at))
    return loudness


def normal_values(stream_key, dims, scale, reach, cuts=(), kind=jnp.bfloat16):
    drawn = scale * jax.random.normal(stream_key, dims, jnp.float32)
    if cuts:
        drawn = drawn * steps_of(stream_key, dims, cuts, -0.22, 0.18)
    return jnp.clip(drawn, -reach, reach).astype(kind)


def setup_inputs(seed: int = 0) -> dict:
    splits = jax.random.split(jax.random.key(seed), 22)
    p2 = draw_p2(jax.random.fold_in(splits[21], 71), 0)
    p3 = draw_p3(jax.random.fold_in(splits[21], 71), 0)
    p4 = draw_p4(jax.random.fold_in(splits[21], 71), 0)
    p5 = draw_p5(jax.random.fold_in(splits[21], 71), 0)
    norm_gain = jnp.clip(1.0 + 0.1 * jax.random.normal(splits[4], (C,), jnp.float32), 0.5, 1.5)
    norm_bias = normal_values(splits[5], (C,), 0.5, 3.0, ((0, 4),), jnp.float32)
    fc6_weight = normal_values(splits[6], (FLAT, FC), FLAT ** -0.5, 0.0546875, ((0, 8), (1, 4)))
    fc6_bias = normal_values(splits[7], (FC,), 0.5, 3.0, ((0, 4),), jnp.float32)
    fc7_weight = normal_values(splits[8], (FC, FC), FC ** -0.5, 0.1875, ((0, 8), (1, 4)))
    fc7_bias = normal_values(splits[9], (FC,), 0.5, 3.0, ((0, 32),))
    cls_weight = normal_values(splits[10], (FC, CLASSES), 0.1, 0.59765625, ((0, 32),))
    cls_bias = normal_values(splits[11], (CLASSES,), 1.0, 4.0, (), jnp.float32)
    box_weight = normal_values(splits[12], (FC, 4), FC ** -0.5, 0.1875, ((0, 32),))
    box_bias = normal_values(splits[13], (4,), 0.5, 3.0, (), jnp.float32)
    roi_boxes = draw_roi_boxes(jax.random.fold_in(splits[21], 71), 0)
    roi_level = draw_roi_level(jax.random.fold_in(splits[21], 71), 0)
    roi_image = draw_roi_image(jax.random.fold_in(splits[21], 71), 0)
    canvas_offsets = draw_canvas_offsets(jax.random.fold_in(splits[21], 71), 0)
    labels = draw_labels(jax.random.fold_in(splits[21], 71), 0)
    target_boxes = draw_target_boxes(jax.random.fold_in(splits[21], 71), 0)
    valid = draw_valid(jax.random.fold_in(splits[21], 71), 0)
    return dict(p2=p2, p3=p3, p4=p4, p5=p5, norm_gain=norm_gain, norm_bias=norm_bias, fc6_weight=fc6_weight, fc6_bias=fc6_bias, fc7_weight=fc7_weight, fc7_bias=fc7_bias, cls_weight=cls_weight, cls_bias=cls_bias, box_weight=box_weight, box_bias=box_bias, roi_boxes=roi_boxes, roi_level=roi_level, roi_image=roi_image, canvas_offsets=canvas_offsets, labels=labels, target_boxes=target_boxes, valid=valid)


@jax.custom_vjp
def low(v):
    return lax.optimization_barrier(v.astype(jnp.bfloat16)).astype(jnp.float32)

@jax.custom_vjp
def low_back(v):
    return v

def low_keep(v):
    return (low(v), None)

def low_pass(kept, grad):
    return (grad,)

def back_keep(v):
    return (v, None)

def back_low(kept, grad):
    return (low(grad),)
low.defvjp(low_keep, low_pass)
low_back.defvjp(back_keep, back_low)
EPSILON = 1e-05

def axis_weights(begin_at, end_at, step_size, cell_count):
    anchor = begin_at / step_size - 0.5
    extent = (end_at - begin_at) / step_size
    fractions = (jnp.arange(14, dtype=jnp.float32) + 0.5) / 14.0
    samples = anchor[:, None] + extent[:, None] * fractions[None, :]
    grid_points = jnp.arange(cell_count, dtype=jnp.float32)
    tent_value = jnp.maximum(1.0 - jnp.abs(samples[:, :, None] - grid_points[None, None, :]), 0.0)
    return 0.5 * (tent_value[:, 0::2, :] + tent_value[:, 1::2, :])

def reference(p2, p3, p4, p5, norm_gain, norm_bias, fc6_weight, fc6_bias, fc7_weight, fc7_bias, cls_weight, cls_bias, box_weight, box_bias, roi_boxes, roi_level, roi_image, canvas_offsets, labels, target_boxes, valid):
    canvas_ids = jnp.arange(ROIS, dtype=jnp.int32) // R_DEV
    image_ids = (canvas_ids * 4 + roi_image).astype(jnp.int32)
    shift_x = jnp.take(canvas_offsets[0], image_ids)
    shift_y = jnp.take(canvas_offsets[1], image_ids)
    left_edge = (roi_boxes[0] + shift_x).astype(jnp.float32)
    top_edge = (roi_boxes[1] + shift_y).astype(jnp.float32)
    right_edge = (roi_boxes[2] + shift_x).astype(jnp.float32)
    bottom_edge = (roi_boxes[3] + shift_y).astype(jnp.float32)
    block_rows = math.gcd(R_DEV, 64)
    block_count = ROIS // block_rows
    regions = (left_edge.reshape(block_count, block_rows), top_edge.reshape(block_count, block_rows), right_edge.reshape(block_count, block_rows), bottom_edge.reshape(block_count, block_rows), roi_level.reshape(block_count, block_rows), canvas_ids.reshape(block_count, block_rows)[:, 0])
    box_float = roi_boxes.astype(jnp.float32)
    goal_float = target_boxes.astype(jnp.float32)
    prop_width = box_float[2] - box_float[0]
    prop_height = box_float[3] - box_float[1]
    prop_cx = box_float[0] + 0.5 * prop_width
    prop_cy = box_float[1] + 0.5 * prop_height
    goal_width = goal_float[2] - goal_float[0]
    goal_height = goal_float[3] - goal_float[1]
    goal_cx = goal_float[0] + 0.5 * goal_width
    goal_cy = goal_float[1] + 0.5 * goal_height
    targets = jnp.stack([10.0 * (goal_cx - prop_cx) / prop_width, 10.0 * (goal_cy - prop_cy) / prop_height, 5.0 * jnp.log(goal_width / prop_width), 5.0 * jnp.log(goal_height / prop_height)], axis=1)
    valid_rows = valid.astype(jnp.float32)
    foreground = valid_rows * (labels > 0).astype(jnp.float32)
    class_match = labels[:, None] == jnp.arange(CLASSES, dtype=jnp.int32)[None, :]

    def forward(planes, gain, shift, wide, wide_bias, deep, deep_bias, cls_w, cls_b, box_w, box_b):
        pixel_total = CANVASES * sum((plane.shape[2] for plane in planes))
        first_sum = sum((lax.optimization_barrier(jnp.sum(plane, axis=(0, 2))) for plane in planes))
        second_sum = sum((lax.optimization_barrier(jnp.sum(plane * plane, axis=(0, 2))) for plane in planes))
        mean_value = first_sum / pixel_total
        variance = second_sum / pixel_total - mean_value * mean_value
        inv_std = lax.rsqrt(variance + EPSILON)
        normed = [low((plane - mean_value[:, None]) * inv_std[:, None] * gain[:, None] + shift[:, None]) for plane in planes]

        def pool(region):
            left_b, top_b, right_b, bottom_b, level_ids, canvas = region
            summed = jnp.zeros((block_rows, C, 7, 7), jnp.float32)
            for level_idx in range(4):
                step_size = 4.0 * 2 ** level_idx
                cell_count = CANVAS // (4 * 2 ** level_idx)
                chosen = (level_ids == level_idx).astype(jnp.float32)
                rows_w = low(axis_weights(top_b, bottom_b, step_size, cell_count) * chosen[:, None, None])
                cols_w = low(axis_weights(left_b, right_b, step_size, cell_count))
                plane = lax.dynamic_index_in_dim(normed[level_idx], canvas, 0, keepdims=False).reshape(C, cell_count, cell_count)
                inner_rows = low_back(low(jnp.einsum('riy,cyx->rixc', rows_w, plane, precision=lax.Precision.HIGHEST)))
                summed = summed + jnp.einsum('rjx,rixc->rcij', cols_w, inner_rows, precision=lax.Precision.HIGHEST)
            return low_back(low(summed))
        pooled = lax.map(jax.checkpoint(pool), regions).reshape(ROIS, C * 49)
        pre_six = low_back(jnp.dot(pooled, wide, precision=lax.Precision.HIGHEST) + wide_bias)
        hidden_six = low(jax.nn.silu(pre_six))
        pre_seven = low_back(jnp.dot(hidden_six, deep.T, precision=lax.Precision.HIGHEST) + deep_bias)
        hidden_seven = low(jax.nn.silu(pre_seven))
        logits = low_back(jnp.dot(hidden_seven, cls_w, precision=lax.Precision.HIGHEST) + cls_b)
        deltas = low_back(jnp.dot(hidden_seven, box_w, precision=lax.Precision.HIGHEST) + box_b)
        valid_total = jnp.sum(valid_rows)
        top_logit = lax.optimization_barrier(jnp.max(logits, axis=1, keepdims=True))
        log_total = top_logit[:, 0] + jnp.log(lax.optimization_barrier(jnp.sum(jnp.exp(logits - top_logit), axis=1)))
        picked = lax.optimization_barrier(jnp.sum(jnp.where(class_match, logits, 0.0), axis=1))
        class_loss = jnp.sum(valid_rows * (log_total - picked)) / valid_total
        misfit = deltas - targets
        huber_terms = jnp.where(jnp.abs(misfit) < 1.0, 0.5 * misfit * misfit, jnp.abs(misfit) - 0.5)
        regress_loss = jnp.sum(foreground * lax.optimization_barrier(jnp.sum(huber_terms, axis=1))) / valid_total
        centre_x = prop_cx + deltas[:, 0] / 10.0 * prop_width
        centre_y = prop_cy + deltas[:, 1] / 10.0 * prop_height
        new_width = prop_width * jnp.exp(deltas[:, 2] / 5.0)
        new_height = prop_height * jnp.exp(deltas[:, 3] / 5.0)
        decoded = jnp.stack([centre_x - 0.5 * new_width, centre_y - 0.5 * new_height, centre_x + 0.5 * new_width, centre_y + 0.5 * new_height]) / (CANVAS // 2)
        return ((class_loss + regress_loss) * ROIS, (class_loss, regress_loss, decoded))
    inputs = ([plane.astype(jnp.float32) for plane in (p2, p3, p4, p5)], norm_gain, norm_bias, fc6_weight.astype(jnp.float32), fc6_bias, fc7_weight.astype(jnp.float32), fc7_bias.astype(jnp.float32), cls_weight.astype(jnp.float32), cls_bias, box_weight.astype(jnp.float32), box_bias)
    scaled, pull_back, extras = jax.vjp(forward, *inputs, has_aux=True)
    grads = pull_back(jnp.ones((), jnp.float32))
    map_grads = grads[0]
    return (extras[0], extras[1], extras[2], map_grads[0], map_grads[1], map_grads[2], map_grads[3], grads[1], grads[2], grads[3], grads[4], grads[5], grads[6], grads[7], grads[8], grads[9], grads[10])
```

```python
import functools
import math

import jax
import jax.numpy as jnp
from jax import lax
from jax.experimental import pallas as pl
from jax.experimental.pallas import tpu as pltpu
from jax.sharding import PartitionSpec as P

CANVAS = 1024
EPSILON = 1e-05
LANES = 128
SPAN = 10
PAIR = 2
SIDES = tuple(CANVAS // (4 * 2**level) for level in range(4))
TILES = tuple(side * side // LANES for side in SIDES)
FIRST = tuple(sum(TILES[:level]) for level in range(4))
ALL_TILES = sum(TILES)
PADDED = ALL_TILES + max(SPAN - min(TILES), 0)
SLOTS = 32
USED = tuple(slot for slot in range(SLOTS) if slot % 8 < 7)
WIDE = len(USED) * LANES
F32_FIELDS = 7
I32_FIELDS = 6


def silu_slope(values):
    sigma = jax.nn.sigmoid(values)
    return sigma * (1.0 + values * (1.0 - sigma))


def contract_first(left_m, right_m):
    return lax.dot_general(
        left_m, right_m, (((0,), (0,)), ((), ())), preferred_element_type=jnp.float32
    )


def contract_last(left_m, right_m):
    return lax.dot_general(
        left_m, right_m, (((1,), (1,)), ((), ())), preferred_element_type=jnp.float32
    )


def region_tables(left, top, right, bottom, level):
    def by_level(values):
        chosen = jnp.full(level.shape, values[0])
        for at in range(1, 4):
            chosen = jnp.where(level == at, values[at], chosen)
        return chosen

    step = by_level([4.0 * 2**at for at in range(4)])
    side = by_level(list(SIDES))
    rows_log = by_level([(max(LANES // n, 1)).bit_length() - 1 for n in SIDES])
    across = by_level([max(n // LANES, 1) for n in SIDES])
    x_anchor, x_extent = left / step - 0.5, (right - left) / step
    y_anchor, y_extent = top / step - 0.5, (bottom - top) / step

    def window(anchor, extent):
        low = jnp.floor(anchor + extent * (0.5 / 14.0)).astype(jnp.int32)
        high = jnp.floor(anchor + extent * (13.5 / 14.0)).astype(jnp.int32) + 1
        return jnp.clip(low, 0, side - 1), jnp.clip(high, 0, side - 1)

    y_low, y_high = window(y_anchor, y_extent)
    x_low, x_high = window(x_anchor, x_extent)
    group_low, group_high = y_low >> rows_log, y_high >> rows_log
    chunks = (group_high - group_low + SPAN) // SPAN
    group = jnp.maximum(jnp.minimum(group_low, (side >> rows_log) - chunks * SPAN), 0)
    tile_x = x_low // LANES
    tiles_x = x_high // LANES - tile_x + 1
    first_tile = by_level(list(FIRST)) + group * across + tile_x
    mask = jnp.minimum(side, LANES) - 1
    shift = 7 - rows_log
    rows_per = (1 << rows_log).astype(jnp.float32)
    floats = jnp.stack(
        [
            x_anchor,
            x_extent,
            y_anchor,
            y_extent,
            (tile_x * LANES).astype(jnp.float32),
            group.astype(jnp.float32) * rows_per,
            rows_per,
        ]
    ).astype(jnp.float32)
    ints = jnp.stack([first_tile, across, mask, shift, chunks, tiles_x]).astype(jnp.int32)
    return floats.reshape(-1), ints.reshape(-1)


def window_weights(floats, ints, rois, region, chunk, tile_x):
    x_anchor, x_extent, y_anchor, y_extent, x_origin, y_origin, rows_per = (
        floats[at * rois + region] for at in range(F32_FIELDS)
    )
    first_tile, across, mask, shift = (ints[at * rois + region] for at in range(4))
    if chunk is not None:
        first_tile = first_tile + chunk * (SPAN * across) + tile_x
        x_origin = x_origin + (tile_x * LANES).astype(jnp.float32)
        y_origin = y_origin + (chunk * SPAN).astype(jnp.float32) * rows_per
    lane = lax.broadcasted_iota(jnp.int32, (8, LANES), 1)
    bin_at = lax.broadcasted_iota(jnp.int32, (8, LANES), 0)
    x_cell = (lane & mask).astype(jnp.float32) + x_origin
    y_cell = lax.shift_right_logical(lane, jnp.broadcast_to(shift, lane.shape)).astype(
        jnp.float32
    ) + y_origin
    part = jnp.where(bin_at < 7, (2.0 * bin_at.astype(jnp.float32) + 0.5) / 14.0, -1e6)
    near = y_anchor + y_extent * part - y_cell
    far = y_anchor + y_extent * (part + 1.0 / 14.0) - y_cell

    def tent(distance):
        return jnp.maximum(1.0 - jnp.abs(distance), 0.0)

    across_w = []
    for j in range(7):
        one = x_anchor + x_extent * ((2 * j + 0.5) / 14.0)
        two = x_anchor + x_extent * ((2 * j + 1.5) / 14.0)
        across_w.append(0.25 * (tent(one - x_cell) + tent(two - x_cell)))
    across_w.append(jnp.zeros((8, LANES), jnp.float32))
    packed = [
        jnp.concatenate([across_w[2 * at], across_w[2 * at + 1]], axis=0).astype(jnp.bfloat16)
        for at in range(4)
    ]
    blocks = []
    for at in range(SPAN):
        offset = rows_per * float(at)
        down = tent(near - offset) + tent(far - offset)
        both = jnp.concatenate([down, down], axis=0).astype(jnp.bfloat16)
        blocks.append(jnp.concatenate([both * item for item in packed], axis=0))
    return jnp.concatenate(blocks, axis=1), first_tile, across


def tile_lanes(first_tile, across, at):
    return pl.ds(pl.multiple_of((first_tile + at * across) * LANES, LANES), LANES)


def pool_kernel(
    rois, floats, ints, mean, scale, shift, p2, p3, p4, p5,
    pooled_out, centred_out, weight_out, maps, values, totals, sems,
):
    channels = mean.shape[1] // 2
    copies = []
    for level, plane in enumerate((p2, p3, p4, p5)):
        cells = TILES[level] * LANES
        copies.append(
            pltpu.make_async_copy(
                plane.at[0],
                maps.at[pl.ds(0, channels), pl.ds(FIRST[level] * LANES, cells)],
                sems.at[level],
            )
        )
        copies[-1].start()
    ones = jnp.ones((16, LANES), jnp.bfloat16)

    def fill(at, carry):
        maps[pl.ds(channels, 16), pl.ds(pl.multiple_of(at * LANES, LANES), LANES)] = ones
        return carry

    lax.fori_loop(0, ALL_TILES, fill, 0)
    extra = PADDED - ALL_TILES
    if extra:
        maps[:, pl.ds(ALL_TILES * LANES, extra * LANES)] = jnp.zeros(
            (channels + 16, extra * LANES), jnp.bfloat16
        )
    for copy in copies:
        copy.wait()
    low_lane = lax.broadcasted_iota(jnp.int32, (SLOTS, 2 * channels), 1) < channels

    def item(region, chunk, tile_x):
        kernel_w, first_tile, across = window_weights(floats, ints, rois, region, chunk, tile_x)
        cells = jnp.concatenate(
            [maps[:, tile_lanes(first_tile, across, at)] for at in range(SPAN)], axis=1
        )
        result = contract_last(kernel_w, cells)
        pair = jnp.concatenate(
            [result[:SLOTS, :channels], result[SLOTS:, :channels]], axis=1
        )
        total = jnp.where(
            low_lane,
            jnp.broadcast_to(result[:SLOTS, channels : channels + 1], low_lane.shape),
            jnp.broadcast_to(result[SLOTS:, channels : channels + 1], low_lane.shape),
        )
        return pair, total

    def step(at, carry):
        for lane_at in range(PAIR):
            region = at * PAIR + lane_at
            pair, total = item(region, None, None)
            values[pl.ds(region, SLOTS, stride=rois), :] = pair
            totals[pl.ds(region, SLOTS, stride=rois), :] = total
        for lane_at in range(PAIR):
            region = at * PAIR + lane_at
            tiles_x = ints[5 * rois + region]

            def more(index, inner):
                chunk = index // tiles_x
                pair, total = item(region, chunk, index - chunk * tiles_x)
                place = pl.ds(region, SLOTS, stride=rois)
                values[place, :] = values[place, :] + pair
                totals[place, :] = totals[place, :] + total
                return inner

            lax.fori_loop(1, ints[4 * rois + region] * tiles_x, more, 0)
        return carry

    lax.fori_loop(0, rois // PAIR, step, 0)
    for at, slot in enumerate(USED):
        rows = pl.ds(slot * rois, rois)
        lanes = pl.ds(at * LANES, LANES)
        total = totals[rows, :]
        centred = values[rows, :] - mean[...] * total
        centred_out[:, lanes] = centred.astype(jnp.bfloat16)
        weight_out[:, lanes] = total.astype(jnp.bfloat16)
        pooled_out[:, lanes] = (centred * scale[...] + shift[...] * total).astype(jnp.bfloat16)


def unpool_kernel(
    rois, floats, ints, base, slope, grads, p2, p3, p4, p5,
    o2, o3, o4, o5, maps, sums, slots, sems, out_sems,
):
    channels = base.shape[0]
    copies = []
    for level, plane in enumerate((p2, p3, p4, p5)):
        cells = TILES[level] * LANES
        copies.append(
            pltpu.make_async_copy(
                plane.at[0], maps.at[:, pl.ds(FIRST[level] * LANES, cells)], sems.at[level]
            )
        )
        copies[-1].start()
    for slot in range(SLOTS):
        rows = pl.ds(slot * rois, rois)
        if slot in USED:
            lanes = pl.ds(USED.index(slot) * LANES, LANES)
            slots[rows, :] = grads[:, lanes].astype(jnp.float32)
        else:
            slots[rows, :] = jnp.zeros((rois, LANES), jnp.float32)
    for copy in copies:
        copy.wait()
    base_v, slope_v = base[...], slope[...]

    def begin(at, carry):
        lanes = pl.ds(pl.multiple_of(at * LANES, LANES), LANES)
        sums[:, lanes] = base_v + slope_v * maps[:, lanes].astype(jnp.float32)
        return carry

    lax.fori_loop(0, ALL_TILES, begin, 0)
    extra = PADDED - ALL_TILES
    if extra:
        sums[:, pl.ds(ALL_TILES * LANES, extra * LANES)] = jnp.zeros(
            (channels, extra * LANES), jnp.float32
        )

    def item(region, chunk, tile_x):
        kernel_w, first_tile, across = window_weights(floats, ints, rois, region, chunk, tile_x)
        mine = slots[pl.ds(region, SLOTS, stride=rois), :]
        stacked = jnp.concatenate([mine[:, :channels], mine[:, channels:]], axis=0)
        turned = stacked.T.astype(jnp.bfloat16)
        result = jnp.dot(turned, kernel_w, preferred_element_type=jnp.float32)
        return result, first_tile, across

    def add(result, first_tile, across):
        for at in range(SPAN):
            lanes = tile_lanes(first_tile, across, at)
            sums[:, lanes] = sums[:, lanes] + result[:, at * LANES : (at + 1) * LANES]

    def step(at, carry):
        results = [item(at * PAIR + lane_at, None, None) for lane_at in range(PAIR)]
        for result in results:
            add(*result)
        for lane_at in range(PAIR):
            region = at * PAIR + lane_at
            tiles_x = ints[5 * rois + region]

            def more(index, inner):
                chunk = index // tiles_x
                add(*item(region, chunk, index - chunk * tiles_x))
                return inner

            lax.fori_loop(1, ints[4 * rois + region] * tiles_x, more, 0)
        return carry

    lax.fori_loop(0, rois // PAIR, step, 0)
    copies = []
    for level, plane in enumerate((o2, o3, o4, o5)):
        cells = TILES[level] * LANES
        copies.append(
            pltpu.make_async_copy(
                sums.at[:, pl.ds(FIRST[level] * LANES, cells)], plane.at[0], out_sems.at[level]
            )
        )
        copies[-1].start()
    for copy in copies:
        copy.wait()


ANY = pl.BlockSpec(memory_space=pl.ANY)
SMEM = pl.BlockSpec(memory_space=pltpu.SMEM)
VMEM = pl.BlockSpec(memory_space=pltpu.VMEM)
LIMIT = 60 * 1024 * 1024


def pool_maps(floats, ints, mean, scale, shift, planes, rois):
    channels = planes[0].shape[1]
    flat = jax.ShapeDtypeStruct((rois, WIDE), jnp.bfloat16)
    return pl.pallas_call(
        functools.partial(pool_kernel, rois),
        out_shape=(flat, flat, flat),
        in_specs=[SMEM, SMEM, VMEM, VMEM, VMEM, ANY, ANY, ANY, ANY],
        out_specs=(VMEM, VMEM, VMEM),
        scratch_shapes=[
            pltpu.VMEM((channels + 16, PADDED * LANES), jnp.bfloat16),
            pltpu.VMEM((SLOTS * rois, LANES), jnp.float32),
            pltpu.VMEM((SLOTS * rois, LANES), jnp.float32),
            pltpu.SemaphoreType.DMA((4,)),
        ],
        compiler_params=pltpu.CompilerParams(vmem_limit_bytes=LIMIT),
        name="pool",
    )(floats, ints, mean, scale, shift, *planes)


def unpool_maps(floats, ints, base, slope, grads, planes, rois):
    channels = planes[0].shape[1]
    return pl.pallas_call(
        functools.partial(unpool_kernel, rois),
        out_shape=tuple(jax.ShapeDtypeStruct(plane.shape, jnp.float32) for plane in planes),
        in_specs=[SMEM, SMEM, VMEM, VMEM, VMEM, ANY, ANY, ANY, ANY],
        out_specs=(ANY, ANY, ANY, ANY),
        scratch_shapes=[
            pltpu.VMEM((channels, ALL_TILES * LANES), jnp.bfloat16),
            pltpu.VMEM((channels, PADDED * LANES), jnp.float32),
            pltpu.VMEM((SLOTS * rois, LANES), jnp.float32),
            pltpu.SemaphoreType.DMA((4,)),
            pltpu.SemaphoreType.DMA((4,)),
        ],
        compiler_params=pltpu.CompilerParams(vmem_limit_bytes=LIMIT),
        name="unpool",
    )(floats, ints, base, slope, grads, *planes)


def local(
    p2, p3, p4, p5, norm_gain, norm_bias, fc6_weight, fc6_bias, fc7_weight, fc7_bias,
    cls_weight, cls_bias, box_weight, box_bias, roi_boxes, roi_level, roi_image,
    canvas_offsets, labels, target_boxes, valid,
):
    channels = p2.shape[1]
    rois = roi_level.shape[0]
    cols = lax.axis_size("col")
    rows = lax.axis_size("roi")
    hidden = fc6_bias.shape[0] * cols
    piece = fc6_bias.shape[0]
    high = rows // cols
    few = channels // high
    planes = (p2, p3, p4, p5)

    block = fc6_weight.reshape(few, 7, 7, piece)
    block = jnp.pad(block, ((0, 0), (0, 0), (0, 1), (0, 0))).reshape(few, 7, 2, 4, piece)
    block = block.transpose(3, 1, 2, 0, 4).reshape(len(USED) * 2, few, piece)
    pairs = [
        ((kappa * high + rho // cols) * cols + rho % cols, rho * cols + kappa)
        for rho in range(rows)
        for kappa in range(cols)
    ]
    block = lax.ppermute(block, ("roi", "col"), pairs)
    wide = lax.all_gather(block, "roi", axis=0)
    wide = wide.reshape(high, cols, len(USED) * 2, few, piece)
    wide = wide.transpose(2, 0, 3, 1, 4).reshape(WIDE, hidden)

    per = fc7_bias.shape[0]
    classes, boxes = cls_weight.shape[1], box_weight.shape[1]
    head = jnp.concatenate([cls_weight, box_weight, fc7_bias[:, None]], axis=1)
    head = jnp.pad(head, ((0, 0), (0, piece - head.shape[1])))
    bias_high = fc6_bias.astype(jnp.bfloat16)
    rest = fc6_bias - bias_high.astype(jnp.float32)
    bias_mid = rest.astype(jnp.bfloat16)
    bias_low = (rest - bias_mid.astype(jnp.float32)).astype(jnp.bfloat16)
    small = jnp.concatenate(
        [fc7_weight, head, jnp.stack([bias_high, bias_mid, bias_low])], axis=0
    )
    deep_rows = fc7_weight.shape[0]
    small = jnp.pad(small, ((0, -small.shape[0] % 16), (0, 0)))
    small = lax.all_gather(small, ("roi", "col"), axis=0)
    deep = small[:, :deep_rows].reshape(rows, cols, deep_rows, piece)
    deep = deep.transpose(0, 2, 1, 3).reshape(hidden, hidden)
    head = small[:, deep_rows : deep_rows + per].reshape(hidden, piece)[:, :LANES]
    bias_seven = head[:, classes + boxes].astype(jnp.float32)
    bias_six = small[:cols, deep_rows + per : deep_rows + per + 3].astype(jnp.float32)
    bias_six = jnp.sum(bias_six, axis=1).reshape(hidden)

    values = [plane[0].astype(jnp.float32) for plane in planes]
    pixel_total = rows * sum(plane.shape[1] for plane in values)
    first_sum = sum(jnp.sum(plane, axis=1) for plane in values)
    second_sum = sum(jnp.sum(plane * plane, axis=1) for plane in values)
    local_valid = jnp.sum(valid.astype(jnp.float32))
    first_sum, second_sum, valid_total = lax.psum((first_sum, second_sum, local_valid), "roi")
    mean = first_sum / pixel_total
    variance = second_sum / pixel_total - mean * mean
    inv_std = lax.rsqrt(variance + EPSILON)
    scale = norm_gain * inv_std

    picks = roi_image[None, :] == jnp.arange(4, dtype=jnp.int32)[:, None]
    shift_x = jnp.sum(jnp.where(picks, canvas_offsets[0][:, None], 0), axis=0)
    shift_y = jnp.sum(jnp.where(picks, canvas_offsets[1][:, None], 0), axis=0)
    floats, ints = region_tables(
        (roi_boxes[0] + shift_x).astype(jnp.float32),
        (roi_boxes[1] + shift_y).astype(jnp.float32),
        (roi_boxes[2] + shift_x).astype(jnp.float32),
        (roi_boxes[3] + shift_y).astype(jnp.float32),
        roi_level,
    )

    def twice(vector):
        return jnp.concatenate([vector, vector])[None]

    pooled, centred, weight = pool_maps(
        floats, ints, twice(mean), twice(scale), twice(norm_bias), planes, rois
    )

    partial_six = jnp.dot(pooled, wide, preferred_element_type=jnp.float32).astype(jnp.bfloat16)
    pre_six = lax.psum_scatter(partial_six, "col", scatter_dimension=0, tiled=True)
    pre_six = pre_six.astype(jnp.float32) + bias_six
    hidden_six = jax.nn.silu(pre_six).astype(jnp.bfloat16)
    pre_seven = contract_last(hidden_six, deep) + bias_seven
    hidden_seven = jax.nn.silu(pre_seven).astype(jnp.bfloat16)
    scores = jnp.dot(hidden_seven, head, preferred_element_type=jnp.float32)
    logits = scores[:, :classes] + cls_bias
    deltas = scores[:, classes : classes + boxes] + box_bias

    quarter = rois // cols
    first_row = lax.axis_index("col") * quarter
    mine_labels = lax.dynamic_slice_in_dim(labels, first_row, quarter)
    mine_valid = lax.dynamic_slice_in_dim(valid, first_row, quarter).astype(jnp.float32)
    mine_boxes = lax.dynamic_slice_in_dim(roi_boxes, first_row, quarter, axis=1).astype(jnp.float32)
    mine_goals = lax.dynamic_slice_in_dim(target_boxes, first_row, quarter, axis=1).astype(
        jnp.float32
    )
    prop_width = mine_boxes[2] - mine_boxes[0]
    prop_height = mine_boxes[3] - mine_boxes[1]
    prop_cx = mine_boxes[0] + 0.5 * prop_width
    prop_cy = mine_boxes[1] + 0.5 * prop_height
    goal_width = mine_goals[2] - mine_goals[0]
    goal_height = mine_goals[3] - mine_goals[1]
    goal_cx = mine_goals[0] + 0.5 * goal_width
    goal_cy = mine_goals[1] + 0.5 * goal_height
    targets = jnp.stack(
        [
            10.0 * (goal_cx - prop_cx) / prop_width,
            10.0 * (goal_cy - prop_cy) / prop_height,
            5.0 * jnp.log(goal_width / prop_width),
            5.0 * jnp.log(goal_height / prop_height),
        ],
        axis=1,
    )
    foreground = mine_valid * (mine_labels > 0).astype(jnp.float32)
    top_logit = jnp.max(logits, axis=1, keepdims=True)
    log_total = top_logit[:, 0] + jnp.log(jnp.sum(jnp.exp(logits - top_logit), axis=1))
    onehot = (mine_labels[:, None] == jnp.arange(classes, dtype=jnp.int32)[None, :]).astype(
        jnp.float32
    )
    picked = jnp.sum(onehot * logits, axis=1)
    misfit = deltas - targets
    huber_terms = jnp.where(jnp.abs(misfit) < 1.0, 0.5 * misfit * misfit, jnp.abs(misfit) - 0.5)
    class_part = jnp.sum(mine_valid * (log_total - picked))
    box_part = jnp.sum(foreground * jnp.sum(huber_terms, axis=1))
    centre_x = prop_cx + deltas[:, 0] / 10.0 * prop_width
    centre_y = prop_cy + deltas[:, 1] / 10.0 * prop_height
    new_width = prop_width * jnp.exp(deltas[:, 2] / 5.0)
    new_height = prop_height * jnp.exp(deltas[:, 3] / 5.0)
    decoded = jnp.stack(
        [
            centre_x - 0.5 * new_width,
            centre_y - 0.5 * new_height,
            centre_x + 0.5 * new_width,
            centre_y + 0.5 * new_height,
        ]
    ) / (CANVAS // 2)
    loss_scale = rois * rows / valid_total
    softmax = jnp.exp(logits - log_total[:, None])
    logit_grads = loss_scale * mine_valid[:, None] * (softmax - onehot)
    delta_grads = loss_scale * foreground[:, None] * jnp.clip(misfit, -1.0, 1.0)
    score_grads = jnp.concatenate([logit_grads, delta_grads], axis=1)
    score_grads = jnp.pad(score_grads, ((0, 0), (0, LANES - score_grads.shape[1])))
    score_grads = score_grads.astype(jnp.bfloat16)

    head_term = contract_first(hidden_seven, score_grads)
    hidden_grads = contract_last(score_grads, head)
    pre_seven_grads = (hidden_grads * silu_slope(pre_seven)).astype(jnp.bfloat16)
    deep_term = contract_first(pre_seven_grads, hidden_six)
    six_hidden_grads = jnp.dot(pre_seven_grads, deep, preferred_element_type=jnp.float32)
    pre_six_grads = (six_hidden_grads * silu_slope(pre_six)).astype(jnp.bfloat16)
    six_grads_all = lax.all_gather(pre_six_grads, "col", axis=0, tiled=True)

    wide_term = contract_first(pooled, six_grads_all).astype(jnp.bfloat16)
    wide_term = wide_term.reshape(len(USED) * 2, high, few, cols, piece)
    wide_term = wide_term.transpose(1, 3, 0, 2, 4).reshape(rows * len(USED) * 2, few, piece)
    wide_grad = lax.psum_scatter(wide_term, "roi", scatter_dimension=0, tiled=True)
    wide_grad = lax.ppermute(wide_grad, ("roi", "col"), [(there, here) for here, there in pairs])
    wide_grad = wide_grad.reshape(4, 7, 2, few, piece).transpose(3, 1, 2, 0, 4)
    wide_grad = wide_grad.reshape(few, 7, 8, piece)[:, :, :7].reshape(few * 49, piece)
    fc6_weight_grad = wide_grad.astype(jnp.float32)

    sums = jnp.concatenate(
        [
            jnp.sum(score_grads.astype(jnp.float32), axis=0),
            jnp.stack([class_part, box_part]),
        ]
    )
    everyone = rows * cols
    deep_term = deep_term.reshape(rows, deep_rows, cols, piece).transpose(0, 2, 1, 3)
    deep_term = deep_term.reshape(everyone, deep_rows, piece)
    seven_bias_term = jnp.sum(pre_seven_grads.astype(jnp.float32), axis=0)
    head_term = jnp.concatenate(
        [head_term[:, : classes + boxes], seven_bias_term[:, None]], axis=1
    )
    head_term = jnp.pad(head_term, ((0, 0), (0, piece - head_term.shape[1])))
    head_term = head_term.reshape(everyone, per, piece)
    six_bias_term = jnp.sum(pre_six_grads.astype(jnp.float32), axis=0).reshape(cols, 1, piece)
    six_bias_term = jnp.broadcast_to(six_bias_term[None], (rows, cols, 1, piece))
    six_bias_term = six_bias_term.reshape(everyone, 1, piece)
    sums = jnp.pad(sums, (0, piece - sums.shape[0]))
    sums = jnp.broadcast_to(sums[None, None], (everyone, 1, piece))
    small_term = jnp.concatenate([deep_term, head_term, six_bias_term, sums], axis=1)
    small_term = jnp.pad(small_term, ((0, 0), (0, -small_term.shape[1] % 8), (0, 0)))
    small_grad = lax.psum_scatter(small_term, ("roi", "col"), scatter_dimension=0, tiled=True)[0]
    fc7_weight_grad = small_grad[:deep_rows]
    head_grad = small_grad[deep_rows : deep_rows + per]
    cls_weight_grad = head_grad[:, :classes]
    box_weight_grad = head_grad[:, classes : classes + boxes]
    fc7_bias_grad = head_grad[:, classes + boxes]
    fc6_bias_grad = small_grad[deep_rows + per]
    sums = small_grad[deep_rows + per + 1]
    class_bias_grad = sums[:classes]
    box_bias_grad = sums[classes : classes + boxes]
    cls_loss = sums[LANES] / valid_total
    box_loss = sums[LANES + 1] / valid_total

    pool_grads = contract_last(six_grads_all, wide)
    gain_part = jnp.sum(pool_grads * centred.astype(jnp.float32), axis=0)
    shift_part = jnp.sum(pool_grads * weight.astype(jnp.float32), axis=0)
    gain_part = jnp.sum(gain_part.reshape(-1, channels), axis=0) * inv_std
    shift_part = jnp.sum(shift_part.reshape(-1, channels), axis=0)
    norm_gain_grad, norm_bias_grad = lax.psum((gain_part, shift_part), "roi")

    scaled = (pool_grads * jnp.tile(scale, WIDE // channels)).astype(jnp.bfloat16)
    slope = -scale * inv_std * norm_gain_grad / pixel_total
    base = -scale * norm_bias_grad / pixel_total - slope * mean

    def spread(vector):
        return jnp.broadcast_to(vector[:, None], (channels, LANES))

    input_grads = unpool_maps(floats, ints, spread(base), spread(slope), scaled, planes, rois)
    return (
        cls_loss,
        box_loss,
        decoded,
        input_grads[0],
        input_grads[1],
        input_grads[2],
        input_grads[3],
        norm_gain_grad,
        norm_bias_grad,
        fc6_weight_grad,
        fc6_bias_grad,
        fc7_weight_grad,
        fc7_bias_grad,
        cls_weight_grad,
        class_bias_grad,
        box_weight_grad,
        box_bias_grad,
    )


def solution(mesh):
    return jax.shard_map(
        local,
        mesh=mesh,
        in_specs=(
            P("roi", "col", None),
            P("roi", "col", None),
            P("roi", "col", None),
            P("roi", "col", None),
            P("col"),
            P("col"),
            P("roi", "col"),
            P("col"),
            P("roi", "col"),
            P(("roi", "col")),
            P(("roi", "col"), None),
            P(),
            P(("roi", "col"), None),
            P(),
            P(None, "roi"),
            P("roi"),
            P("roi"),
            P(None, "roi"),
            P("roi"),
            P(None, "roi"),
            P("roi"),
        ),
        out_specs=(
            P(),
            P(),
            P(None, ("roi", "col")),
            P("roi", "col", None),
            P("roi", "col", None),
            P("roi", "col", None),
            P("roi", "col", None),
            P("col"),
            P("col"),
            P("roi", "col"),
            P("col"),
            P("roi", "col"),
            P(("roi", "col")),
            P(("roi", "col"), None),
            P(),
            P(("roi", "col"), None),
            P(),
        ),
        check_vma=False,
    )
```

```python
import functools
import math

import jax
import jax.numpy as jnp
from jax import lax
from jax.experimental import pallas as pl
from jax.experimental.pallas import tpu as pltpu
from jax.sharding import PartitionSpec as P

CANVAS = 1024
EPSILON = 1e-05
LANES = 128
SPAN = 10
GROUP = 16
MORE = 8
SPARE = 8
SIDES = tuple(CANVAS // (4 * 2**level) for level in range(4))
TILES = tuple(side * side // LANES for side in SIDES)
FIRST = tuple(sum(TILES[:level]) for level in range(4))
ALL_TILES = sum(TILES)
PADDED = ALL_TILES + max(SPAN - min(TILES), 0)
SLOTS = 32
USED = tuple(slot for slot in range(SLOTS) if slot % 8 < 7)
WIDE = len(USED) * LANES
F32_FIELDS = 7
I32_FIELDS = 6


def silu_slope(values):
    sigma = jax.nn.sigmoid(values)
    return sigma * (1.0 + values * (1.0 - sigma))


def contract_first(left_m, right_m):
    return lax.dot_general(
        left_m, right_m, (((0,), (0,)), ((), ())), preferred_element_type=jnp.float32
    )


def contract_last(left_m, right_m):
    return lax.dot_general(
        left_m, right_m, (((1,), (1,)), ((), ())), preferred_element_type=jnp.float32
    )


def region_tables(left, top, right, bottom, level):
    def by_level(values):
        chosen = jnp.full(level.shape, values[0])
        for at in range(1, 4):
            chosen = jnp.where(level == at, values[at], chosen)
        return chosen

    step = by_level([4.0 * 2**at for at in range(4)])
    side = by_level(list(SIDES))
    rows_log = by_level([(max(LANES // n, 1)).bit_length() - 1 for n in SIDES])
    across = by_level([max(n // LANES, 1) for n in SIDES])
    x_anchor, x_extent = left / step - 0.5, (right - left) / step
    y_anchor, y_extent = top / step - 0.5, (bottom - top) / step

    def window(anchor, extent):
        low = jnp.floor(anchor + extent * (0.5 / 14.0)).astype(jnp.int32)
        high = jnp.floor(anchor + extent * (13.5 / 14.0)).astype(jnp.int32) + 1
        return jnp.clip(low, 0, side - 1), jnp.clip(high, 0, side - 1)

    y_low, y_high = window(y_anchor, y_extent)
    x_low, x_high = window(x_anchor, x_extent)
    group_low, group_high = y_low >> rows_log, y_high >> rows_log
    chunks = (group_high - group_low + SPAN) // SPAN
    group = jnp.maximum(jnp.minimum(group_low, (side >> rows_log) - chunks * SPAN), 0)
    tile_x = x_low // LANES
    tiles_x = x_high // LANES - tile_x + 1
    first_tile = by_level(list(FIRST)) + group * across + tile_x
    mask = jnp.minimum(side, LANES) - 1
    shift = 7 - rows_log
    rows_per = (1 << rows_log).astype(jnp.float32)
    nothing = jnp.zeros((SPARE,), jnp.int32)
    parts = chunks * tiles_x
    key = 2 * (level > 0).astype(jnp.int32) + (parts > 1).astype(jnp.int32)
    rois = level.shape[0]
    at = jnp.arange(rois, dtype=jnp.int32)
    before = (key[None, :] < key[:, None]) | (
        (key[None, :] == key[:, None]) & (at[None, :] < at[:, None])
    )
    rank = jnp.sum(before.astype(jnp.int32), axis=1)
    order = jnp.sum(jnp.where(rank[None, :] == at[:, None], at[None, :], 0), axis=1)
    order = jnp.concatenate([order, jnp.full((GROUP,), rois, jnp.int32)])
    ends = jnp.stack([jnp.sum((key <= last).astype(jnp.int32)) for last in range(4)])
    floats = jnp.stack(
        [
            x_anchor,
            x_extent,
            y_anchor,
            y_extent,
            (tile_x * LANES).astype(jnp.float32),
            group.astype(jnp.float32) * rows_per,
            rows_per,
        ]
    ).astype(jnp.float32)
    ints = jnp.stack([first_tile, across, mask, shift, parts, tiles_x]).astype(jnp.int32)
    away = jnp.full((F32_FIELDS, SPARE), -1e6, jnp.float32)
    floats = jnp.concatenate([floats, away], axis=1)
    ints = jnp.concatenate([ints, jnp.broadcast_to(nothing, (I32_FIELDS, SPARE))], axis=1)
    return floats.reshape(-1), ints.reshape(-1), jnp.concatenate([order, ends])


def window_weights(floats, ints, rois, region, chunk, tile_x):
    rois = rois + SPARE
    x_anchor, x_extent, y_anchor, y_extent, x_origin, y_origin, rows_per = (
        floats[at * rois + region] for at in range(F32_FIELDS)
    )
    first_tile, across, mask, shift = (ints[at * rois + region] for at in range(4))
    if chunk is not None:
        first_tile = first_tile + chunk * (SPAN * across) + tile_x
        x_origin = x_origin + (tile_x * LANES).astype(jnp.float32)
        y_origin = y_origin + (chunk * SPAN).astype(jnp.float32) * rows_per
    lane = lax.broadcasted_iota(jnp.int32, (8, LANES), 1)
    bin_at = lax.broadcasted_iota(jnp.int32, (8, LANES), 0)
    x_cell = (lane & mask).astype(jnp.float32) + x_origin
    y_cell = lax.shift_right_logical(lane, jnp.broadcast_to(shift, lane.shape)).astype(
        jnp.float32
    ) + y_origin
    part = jnp.where(bin_at < 7, (2.0 * bin_at.astype(jnp.float32) + 0.5) / 14.0, -1e6)
    near = y_anchor + y_extent * part - y_cell
    far = y_anchor + y_extent * (part + 1.0 / 14.0) - y_cell

    def tent(distance):
        return jnp.maximum(1.0 - jnp.abs(distance), 0.0)

    across_w = []
    for j in range(7):
        one = x_anchor + x_extent * ((2 * j + 0.5) / 14.0)
        two = x_anchor + x_extent * ((2 * j + 1.5) / 14.0)
        across_w.append(0.25 * (tent(one - x_cell) + tent(two - x_cell)))
    across_w.append(jnp.zeros((8, LANES), jnp.float32))
    packed = [
        jnp.concatenate([across_w[2 * at], across_w[2 * at + 1]], axis=0).astype(jnp.bfloat16)
        for at in range(4)
    ]
    blocks = []
    for at in range(SPAN):
        offset = rows_per * float(at)
        down = tent(near - offset) + tent(far - offset)
        both = jnp.concatenate([down, down], axis=0).astype(jnp.bfloat16)
        blocks.append(jnp.concatenate([both * item for item in packed], axis=0))
    return jnp.concatenate(blocks, axis=1), first_tile, across


def tile_lanes(first_tile, across, at):
    return pl.ds(pl.multiple_of((first_tile + at * across) * LANES, LANES), LANES)


def for_groups(order, start, stop, size, body):
    def step(at, carry):
        first = start + at * size
        inside = [first + index < stop for index in range(size)]
        spare = order.shape[0] - 5
        places = [
            jnp.where(good, first + index, spare) for index, good in enumerate(inside)
        ]
        body([order[place] for place in places])
        return carry

    lax.fori_loop(0, (stop - start + size - 1) // size, step, 0)


def for_parts(ints, order, rois, start, stop, size, body):
    stride = rois + SPARE

    def second(regions):
        for region in regions:
            tiles_x = ints[5 * stride + region]
            wide = (tiles_x > 1).astype(jnp.int32)
            body(region, 1 - wide, wide)

    for_groups(order, start, stop, size, second)

    def later(at, carry):
        region = order[at]
        tiles_x = ints[5 * stride + region]

        def part(index, inner):
            chunk = index // tiles_x
            body(region, chunk, index - chunk * tiles_x)
            return inner

        return lax.fori_loop(2, ints[4 * stride + region], part, carry)

    lax.fori_loop(start, stop, later, 0)


def ends_of(order):
    size = order.shape[0]
    return [order[size - 4 + at] for at in range(4)]


def pool_kernel(
    rois, floats, ints, order, mean, scale, shift, p2, p3, p4, p5,
    pooled_out, centred_out, weight_out, maps, values, sems,
):
    channels = mean.shape[1] // 2
    stride = rois + SPARE
    copies = []
    for level, plane in enumerate((p2, p3, p4, p5)):
        cells = TILES[level] * LANES
        copies.append(
            pltpu.make_async_copy(
                plane.at[0],
                maps.at[pl.ds(0, channels), pl.ds(FIRST[level] * LANES, cells)],
                sems.at[level],
            )
        )
        copies[-1].start()
    ones = jnp.ones((16, 8 * LANES), jnp.bfloat16)

    def fill(at, carry):
        lanes = pl.ds(pl.multiple_of(at * 8 * LANES, 8 * LANES), 8 * LANES)
        maps[pl.ds(channels, 16), lanes] = ones
        return carry

    lax.fori_loop(0, ALL_TILES // 8, fill, 0)
    extra = PADDED - ALL_TILES
    if extra:
        maps[:, pl.ds(ALL_TILES * LANES, extra * LANES)] = jnp.zeros(
            (channels + 16, extra * LANES), jnp.bfloat16
        )
    for copy in copies:
        copy.wait()

    def item(region, chunk, tile_x):
        kernel_w, first_tile, across = window_weights(floats, ints, rois, region, chunk, tile_x)
        cells = jnp.concatenate(
            [maps[:, tile_lanes(first_tile, across, at)] for at in range(SPAN)], axis=1
        )
        return contract_last(kernel_w, cells)

    def place(region):
        return pl.ds(region, 2 * SLOTS, stride=stride)

    def first(regions):
        for region in regions:
            values[place(region), : channels + 16] = item(region, None, None)

    def further(region, chunk, tile_x):
        values[place(region), : channels + 16] = values[place(region), : channels + 16] + item(region, chunk, tile_x)

    low_end, low_multi, rest_end, all_end = ends_of(order)
    for_groups(order, 0, all_end, GROUP, first)
    for_parts(ints, order, rois, low_end, low_multi, MORE, further)
    for_parts(ints, order, rois, rest_end, all_end, MORE, further)
    low_lane = lax.broadcasted_iota(jnp.int32, (rois, LANES), 1) < channels
    for at, slot in enumerate(USED):
        lanes = pl.ds(at * LANES, LANES)
        one = values[pl.ds(slot * stride, rois), :]
        two = values[pl.ds((slot + SLOTS) * stride, rois), :]
        value = jnp.where(low_lane, one, pltpu.roll(two, channels, 1))
        total = jnp.where(low_lane, one[:, channels : channels + 1], two[:, channels : channels + 1])
        centred = value - mean[...] * total
        centred_out[:, lanes] = centred.astype(jnp.bfloat16)
        weight_out[:, lanes] = total.astype(jnp.bfloat16)
        pooled_out[:, lanes] = (centred * scale[...] + shift[...] * total).astype(jnp.bfloat16)


def unpool_kernel(
    rois, floats, ints, order, base, slope, grads, p2, p3, p4, p5,
    o2, o3, o4, o5, maps, sums, slots, sems, out_sems,
):
    channels = base.shape[0]
    stride = rois + SPARE
    planes, outs = (p2, p3, p4, p5), (o2, o3, o4, o5)
    pieces = [(level, at) for level in range(4) for at in range(4 if level == 0 else 1)]

    def fetch(index):
        level, at = pieces[index]
        cells = TILES[level] * LANES // (4 if level == 0 else 1)
        return pltpu.make_async_copy(
            planes[level].at[0, :, pl.ds(at * cells, cells)],
            maps.at[:, pl.ds(FIRST[level] * LANES + at * cells, cells)],
            sems.at[index],
        )

    for index in range(len(pieces)):
        fetch(index).start()
    for slot in range(SLOTS):
        rows = pl.ds(slot * stride, rois)
        slots[pl.ds(slot * stride + rois, SPARE), :] = jnp.zeros((SPARE, LANES), jnp.float32)
        if slot in USED:
            lanes = pl.ds(USED.index(slot) * LANES, LANES)
            slots[rows, :] = grads[:, lanes].astype(jnp.float32)
        else:
            slots[rows, :] = jnp.zeros((rois, LANES), jnp.float32)
    base_v, slope_v = base[...], slope[...]

    def begin(at, carry):
        for part in range(4):
            lanes = pl.ds(pl.multiple_of((at * 4 + part) * LANES, LANES), LANES)
            sums[:, lanes] = base_v + slope_v * maps[:, lanes].astype(jnp.float32)
        return carry

    for index, (level, at) in enumerate(pieces):
        tiles = TILES[level] // (4 if level == 0 else 1)
        start = FIRST[level] + at * tiles
        fetch(index).wait()
        lax.fori_loop(start // 4, (start + tiles) // 4, begin, 0)
    extra = PADDED - ALL_TILES
    if extra:
        sums[:, pl.ds(ALL_TILES * LANES, extra * LANES)] = jnp.zeros(
            (channels, extra * LANES), jnp.float32
        )

    def item(region, chunk, tile_x):
        kernel_w, first_tile, across = window_weights(floats, ints, rois, region, chunk, tile_x)
        mine = slots[pl.ds(region, SLOTS, stride=stride), :]
        stacked = jnp.concatenate([mine[:, :channels], mine[:, channels:]], axis=0)
        turned = stacked.T.astype(jnp.bfloat16)
        result = jnp.dot(turned, kernel_w, preferred_element_type=jnp.float32)
        for at in range(SPAN):
            lanes = tile_lanes(first_tile, across, at)
            sums[:, lanes] = sums[:, lanes] + result[:, at * LANES : (at + 1) * LANES]

    def first(regions):
        for region in regions:
            item(region, None, None)

    def send(level):
        cells = TILES[level] * LANES
        return pltpu.make_async_copy(
            sums.at[:, pl.ds(FIRST[level] * LANES, cells)], outs[level].at[0], out_sems.at[level]
        )

    low_end, low_multi, rest_end, all_end = ends_of(order)
    for_groups(order, 0, low_multi, GROUP, first)
    for_parts(ints, order, rois, low_end, low_multi, MORE, item)
    send(0).start()
    for_groups(order, low_multi, all_end, GROUP, first)
    for_parts(ints, order, rois, rest_end, all_end, MORE, item)
    for level in range(1, 4):
        send(level).start()
    for level in range(4):
        send(level).wait()


ANY = pl.BlockSpec(memory_space=pl.ANY)
SMEM = pl.BlockSpec(memory_space=pltpu.SMEM)
VMEM = pl.BlockSpec(memory_space=pltpu.VMEM)
LIMIT = 60 * 1024 * 1024


def pool_maps(floats, ints, order, mean, scale, shift, planes, rois):
    channels = planes[0].shape[1]
    flat = jax.ShapeDtypeStruct((rois, WIDE), jnp.bfloat16)
    return pl.pallas_call(
        functools.partial(pool_kernel, rois),
        out_shape=(flat, flat, flat),
        in_specs=[SMEM, SMEM, SMEM, VMEM, VMEM, VMEM, ANY, ANY, ANY, ANY],
        out_specs=(VMEM, VMEM, VMEM),
        scratch_shapes=[
            pltpu.VMEM((channels + 16, PADDED * LANES), jnp.bfloat16),
            pltpu.VMEM((2 * SLOTS * (rois + SPARE), LANES), jnp.float32),
            pltpu.SemaphoreType.DMA((4,)),
        ],
        compiler_params=pltpu.CompilerParams(vmem_limit_bytes=LIMIT),
        name="pool",
    )(floats, ints, order, mean, scale, shift, *planes)


def unpool_maps(floats, ints, order, base, slope, grads, planes, rois):
    channels = planes[0].shape[1]
    return pl.pallas_call(
        functools.partial(unpool_kernel, rois),
        out_shape=tuple(jax.ShapeDtypeStruct(plane.shape, jnp.float32) for plane in planes),
        in_specs=[SMEM, SMEM, SMEM, VMEM, VMEM, VMEM, ANY, ANY, ANY, ANY],
        out_specs=(ANY, ANY, ANY, ANY),
        scratch_shapes=[
            pltpu.VMEM((channels, ALL_TILES * LANES), jnp.bfloat16),
            pltpu.VMEM((channels, PADDED * LANES), jnp.float32),
            pltpu.VMEM((SLOTS * (rois + SPARE), LANES), jnp.float32),
            pltpu.SemaphoreType.DMA((7,)),
            pltpu.SemaphoreType.DMA((4,)),
        ],
        compiler_params=pltpu.CompilerParams(vmem_limit_bytes=LIMIT),
        name="unpool",
    )(floats, ints, order, base, slope, grads, *planes)


def local(
    p2, p3, p4, p5, norm_gain, norm_bias, fc6_weight, fc6_bias, fc7_weight, fc7_bias,
    cls_weight, cls_bias, box_weight, box_bias, roi_boxes, roi_level, roi_image,
    canvas_offsets, labels, target_boxes, valid,
):
    channels = p2.shape[1]
    rois = roi_level.shape[0]
    cols = lax.axis_size("col")
    rows = lax.axis_size("roi")
    hidden = fc6_bias.shape[0] * cols
    piece = fc6_bias.shape[0]
    high = rows // cols
    few = channels // high
    planes = (p2, p3, p4, p5)

    block = fc6_weight.reshape(few, 7, 7, piece)
    block = jnp.pad(block, ((0, 0), (0, 0), (0, 1), (0, 0))).reshape(few, 7, 2, 4, piece)
    block = block.transpose(3, 1, 2, 0, 4).reshape(len(USED) * 2, few, piece)
    pairs = [
        ((kappa * high + rho // cols) * cols + rho % cols, rho * cols + kappa)
        for rho in range(rows)
        for kappa in range(cols)
    ]
    block = lax.ppermute(block, ("roi", "col"), pairs)
    wide = lax.all_gather(block, "roi", axis=0)
    wide = wide.reshape(high, cols, len(USED) * 2, few, piece)
    wide = wide.transpose(2, 0, 3, 1, 4).reshape(WIDE, hidden)

    per = fc7_bias.shape[0]
    classes, boxes = cls_weight.shape[1], box_weight.shape[1]
    head = jnp.concatenate([cls_weight, box_weight, fc7_bias[:, None]], axis=1)
    head = jnp.pad(head, ((0, 0), (0, piece - head.shape[1])))
    bias_high = fc6_bias.astype(jnp.bfloat16)
    rest = fc6_bias - bias_high.astype(jnp.float32)
    bias_mid = rest.astype(jnp.bfloat16)
    bias_low = (rest - bias_mid.astype(jnp.float32)).astype(jnp.bfloat16)
    small = jnp.concatenate(
        [fc7_weight, head, jnp.stack([bias_high, bias_mid, bias_low])], axis=0
    )
    deep_rows = fc7_weight.shape[0]
    small = jnp.pad(small, ((0, -small.shape[0] % 16), (0, 0)))
    small = lax.all_gather(small, ("roi", "col"), axis=0)
    deep = small[:, :deep_rows].reshape(rows, cols, deep_rows, piece)
    deep = deep.transpose(0, 2, 1, 3).reshape(hidden, hidden)
    head = small[:, deep_rows : deep_rows + per].reshape(hidden, piece)[:, :LANES]
    bias_seven = head[:, classes + boxes].astype(jnp.float32)
    bias_six = small[:cols, deep_rows + per : deep_rows + per + 3].astype(jnp.float32)
    bias_six = jnp.sum(bias_six, axis=1).reshape(hidden)

    values = [plane[0].astype(jnp.float32) for plane in planes]
    pixel_total = rows * sum(plane.shape[1] for plane in values)
    first_sum = sum(jnp.sum(plane, axis=1) for plane in values)
    second_sum = sum(jnp.sum(plane * plane, axis=1) for plane in values)
    local_valid = jnp.sum(valid.astype(jnp.float32))
    first_sum, second_sum, valid_total = lax.psum((first_sum, second_sum, local_valid), "roi")
    mean = first_sum / pixel_total
    variance = second_sum / pixel_total - mean * mean
    inv_std = lax.rsqrt(variance + EPSILON)
    scale = norm_gain * inv_std

    picks = roi_image[None, :] == jnp.arange(4, dtype=jnp.int32)[:, None]
    shift_x = jnp.sum(jnp.where(picks, canvas_offsets[0][:, None], 0), axis=0)
    shift_y = jnp.sum(jnp.where(picks, canvas_offsets[1][:, None], 0), axis=0)
    floats, ints, order = region_tables(
        (roi_boxes[0] + shift_x).astype(jnp.float32),
        (roi_boxes[1] + shift_y).astype(jnp.float32),
        (roi_boxes[2] + shift_x).astype(jnp.float32),
        (roi_boxes[3] + shift_y).astype(jnp.float32),
        roi_level,
    )

    def twice(vector):
        return jnp.concatenate([vector, vector])[None]

    pooled, centred, weight = pool_maps(
        floats, ints, order, twice(mean), twice(scale), twice(norm_bias), planes, rois
    )

    partial_six = jnp.dot(pooled, wide, preferred_element_type=jnp.float32).astype(jnp.bfloat16)
    pre_six = lax.psum_scatter(partial_six, "col", scatter_dimension=0, tiled=True)
    pre_six = pre_six.astype(jnp.float32) + bias_six
    hidden_six = jax.nn.silu(pre_six).astype(jnp.bfloat16)
    pre_seven = contract_last(hidden_six, deep) + bias_seven
    hidden_seven = jax.nn.silu(pre_seven).astype(jnp.bfloat16)
    scores = jnp.dot(hidden_seven, head, preferred_element_type=jnp.float32)
    logits = scores[:, :classes] + cls_bias
    deltas = scores[:, classes : classes + boxes] + box_bias

    quarter = rois // cols
    first_row = lax.axis_index("col") * quarter
    mine_labels = lax.dynamic_slice_in_dim(labels, first_row, quarter)
    mine_valid = lax.dynamic_slice_in_dim(valid, first_row, quarter).astype(jnp.float32)
    mine_boxes = lax.dynamic_slice_in_dim(roi_boxes, first_row, quarter, axis=1).astype(jnp.float32)
    mine_goals = lax.dynamic_slice_in_dim(target_boxes, first_row, quarter, axis=1).astype(
        jnp.float32
    )
    prop_width = mine_boxes[2] - mine_boxes[0]
    prop_height = mine_boxes[3] - mine_boxes[1]
    prop_cx = mine_boxes[0] + 0.5 * prop_width
    prop_cy = mine_boxes[1] + 0.5 * prop_height
    goal_width = mine_goals[2] - mine_goals[0]
    goal_height = mine_goals[3] - mine_goals[1]
    goal_cx = mine_goals[0] + 0.5 * goal_width
    goal_cy = mine_goals[1] + 0.5 * goal_height
    targets = jnp.stack(
        [
            10.0 * (goal_cx - prop_cx) / prop_width,
            10.0 * (goal_cy - prop_cy) / prop_height,
            5.0 * jnp.log(goal_width / prop_width),
            5.0 * jnp.log(goal_height / prop_height),
        ],
        axis=1,
    )
    foreground = mine_valid * (mine_labels > 0).astype(jnp.float32)
    top_logit = jnp.max(logits, axis=1, keepdims=True)
    log_total = top_logit[:, 0] + jnp.log(jnp.sum(jnp.exp(logits - top_logit), axis=1))
    onehot = (mine_labels[:, None] == jnp.arange(classes, dtype=jnp.int32)[None, :]).astype(
        jnp.float32
    )
    picked = jnp.sum(onehot * logits, axis=1)
    misfit = deltas - targets
    huber_terms = jnp.where(jnp.abs(misfit) < 1.0, 0.5 * misfit * misfit, jnp.abs(misfit) - 0.5)
    class_part = jnp.sum(mine_valid * (log_total - picked))
    box_part = jnp.sum(foreground * jnp.sum(huber_terms, axis=1))
    centre_x = prop_cx + deltas[:, 0] / 10.0 * prop_width
    centre_y = prop_cy + deltas[:, 1] / 10.0 * prop_height
    new_width = prop_width * jnp.exp(deltas[:, 2] / 5.0)
    new_height = prop_height * jnp.exp(deltas[:, 3] / 5.0)
    decoded = jnp.stack(
        [
            centre_x - 0.5 * new_width,
            centre_y - 0.5 * new_height,
            centre_x + 0.5 * new_width,
            centre_y + 0.5 * new_height,
        ]
    ) / (CANVAS // 2)
    loss_scale = rois * rows / valid_total
    softmax = jnp.exp(logits - log_total[:, None])
    logit_grads = loss_scale * mine_valid[:, None] * (softmax - onehot)
    delta_grads = loss_scale * foreground[:, None] * jnp.clip(misfit, -1.0, 1.0)
    score_grads = jnp.concatenate([logit_grads, delta_grads], axis=1)
    score_grads = jnp.pad(score_grads, ((0, 0), (0, LANES - score_grads.shape[1])))
    score_grads = score_grads.astype(jnp.bfloat16)

    head_term = contract_first(hidden_seven, score_grads)
    hidden_grads = contract_last(score_grads, head)
    pre_seven_grads = (hidden_grads * silu_slope(pre_seven)).astype(jnp.bfloat16)
    deep_term = contract_first(pre_seven_grads, hidden_six)
    six_hidden_grads = jnp.dot(pre_seven_grads, deep, preferred_element_type=jnp.float32)
    pre_six_grads = (six_hidden_grads * silu_slope(pre_six)).astype(jnp.bfloat16)
    six_grads_all = lax.all_gather(pre_six_grads, "col", axis=0, tiled=True)

    wide_term = contract_first(pooled, six_grads_all).astype(jnp.bfloat16)
    wide_term = wide_term.reshape(len(USED) * 2, high, few, cols, piece)
    wide_term = wide_term.transpose(1, 3, 0, 2, 4).reshape(rows * len(USED) * 2, few, piece)
    wide_grad = lax.psum_scatter(wide_term, "roi", scatter_dimension=0, tiled=True)
    wide_grad = lax.ppermute(wide_grad, ("roi", "col"), [(there, here) for here, there in pairs])
    wide_grad = wide_grad.reshape(4, 7, 2, few, piece).transpose(3, 1, 2, 0, 4)
    wide_grad = wide_grad.reshape(few, 7, 8, piece)[:, :, :7].reshape(few * 49, piece)
    fc6_weight_grad = wide_grad.astype(jnp.float32)

    sums = jnp.concatenate(
        [
            jnp.sum(score_grads.astype(jnp.float32), axis=0),
            jnp.stack([class_part, box_part]),
        ]
    )
    everyone = rows * cols
    deep_term = deep_term.reshape(rows, deep_rows, cols, piece).transpose(0, 2, 1, 3)
    deep_term = deep_term.reshape(everyone, deep_rows, piece)
    seven_bias_term = jnp.sum(pre_seven_grads.astype(jnp.float32), axis=0)
    head_term = jnp.concatenate(
        [head_term[:, : classes + boxes], seven_bias_term[:, None]], axis=1
    )
    head_term = jnp.pad(head_term, ((0, 0), (0, piece - head_term.shape[1])))
    head_term = head_term.reshape(everyone, per, piece)
    six_bias_term = jnp.sum(pre_six_grads.astype(jnp.float32), axis=0).reshape(cols, 1, piece)
    six_bias_term = jnp.broadcast_to(six_bias_term[None], (rows, cols, 1, piece))
    six_bias_term = six_bias_term.reshape(everyone, 1, piece)
    sums = jnp.pad(sums, (0, piece - sums.shape[0]))
    sums = jnp.broadcast_to(sums[None, None], (everyone, 1, piece))
    small_term = jnp.concatenate([deep_term, head_term, six_bias_term, sums], axis=1)
    small_term = jnp.pad(small_term, ((0, 0), (0, -small_term.shape[1] % 8), (0, 0)))
    small_grad = lax.psum_scatter(small_term, ("roi", "col"), scatter_dimension=0, tiled=True)[0]
    fc7_weight_grad = small_grad[:deep_rows]
    head_grad = small_grad[deep_rows : deep_rows + per]
    cls_weight_grad = head_grad[:, :classes]
    box_weight_grad = head_grad[:, classes : classes + boxes]
    fc7_bias_grad = head_grad[:, classes + boxes]
    fc6_bias_grad = small_grad[deep_rows + per]
    sums = small_grad[deep_rows + per + 1]
    class_bias_grad = sums[:classes]
    box_bias_grad = sums[classes : classes + boxes]
    cls_loss = sums[LANES] / valid_total
    box_loss = sums[LANES + 1] / valid_total

    pool_grads = contract_last(six_grads_all, wide)
    gain_part = jnp.sum(pool_grads * centred.astype(jnp.float32), axis=0)
    shift_part = jnp.sum(pool_grads * weight.astype(jnp.float32), axis=0)
    gain_part = jnp.sum(gain_part.reshape(-1, channels), axis=0) * inv_std
    shift_part = jnp.sum(shift_part.reshape(-1, channels), axis=0)
    norm_gain_grad, norm_bias_grad = lax.psum((gain_part, shift_part), "roi")

    scaled = (pool_grads * jnp.tile(scale, WIDE // channels)).astype(jnp.bfloat16)
    slope = -scale * inv_std * norm_gain_grad / pixel_total
    base = -scale * norm_bias_grad / pixel_total - slope * mean

    def spread(vector):
        return jnp.broadcast_to(vector[:, None], (channels, LANES))

    input_grads = unpool_maps(floats, ints, order, spread(base), spread(slope), scaled, planes, rois)
    return (
        cls_loss,
        box_loss,
        decoded,
        input_grads[0],
        input_grads[1],
        input_grads[2],
        input_grads[3],
        norm_gain_grad,
        norm_bias_grad,
        fc6_weight_grad,
        fc6_bias_grad,
        fc7_weight_grad,
        fc7_bias_grad,
        cls_weight_grad,
        class_bias_grad,
        box_weight_grad,
        box_bias_grad,
    )


MESH = pl.DeviceIdType.MESH
KEPT = tuple(at for at in range(2 * len(USED)) if at % 2 == 0 or at // 2 < 21)
LEADING = 42
SPARES = tuple(at for at in range(2 * len(USED)) if at not in KEPT)
SMALL = 6


def ring_of(rows):
    return list(range(0, rows, 2)) + list(range(rows - 1, 0, -2))


def greet(axis, count):
    barrier = pltpu.get_barrier_semaphore()
    me = lax.axis_index(axis)
    for step in range(1, count):
        pl.semaphore_signal(
            barrier,
            inc=1,
            device_id={axis: lax.rem(me + step, count)},
            device_id_type=MESH,
        )


def met(count):
    pl.semaphore_wait(pltpu.get_barrier_semaphore(), count)


def remote(src, dst, sends, recvs, at, axis, peer):
    return pltpu.make_async_remote_copy(
        src_ref=src,
        dst_ref=dst,
        send_sem=sends.at[at],
        recv_sem=recvs.at[at],
        device_id={axis: peer},
        device_id_type=MESH,
    )


def share(slots, axis, count, sends, recvs, first=0):
    me = lax.axis_index(axis)
    copies = [
        remote(slots.at[me], slots.at[me], sends, recvs, first + step - 1, axis,
               lax.rem(me + step, count))
        for step in range(1, count)
    ]
    for copy in copies:
        copy.start()
    return copies


def neighbours(me):
    core, chip = lax.rem(me, 2), lax.div(me, 2)
    return me + 1 - 2 * core, me + 2 - 4 * chip


class Relay:
    def __init__(self, view, sends, recvs, first):
        me = lax.axis_index("col")
        core, chip = neighbours(me)
        self.near = remote(view(me), view(me), sends, recvs, first, "col", core)
        self.far = remote(view(me), view(me), sends, recvs, first + 1, "col", chip)
        self.passed = remote(view(chip), view(chip), sends, recvs, first + 2, "col", core)

    def start(self):
        self.far.start()
        self.near.start()

    def forward(self):
        self.far.wait_recv()
        self.passed.start()

    def wait(self):
        self.near.wait()
        self.far.wait_send()
        self.passed.wait()


def stats_kernel(
    rows, pixels, facts, p2, p3, p4, p5, out, maps, slots, sems, sends, recvs
):
    channels = maps.shape[0]
    planes = (p2, p3, p4, p5)
    pieces = [(level, at) for level in range(4) for at in range(4 if level == 0 else 1)]
    greet("roi", rows)

    def fetch(index):
        level, at = pieces[index]
        cells = TILES[level] * LANES // (4 if level == 0 else 1)
        return pltpu.make_async_copy(
            planes[level].at[0, :, pl.ds(at * cells, cells)],
            maps.at[:, pl.ds(FIRST[level] * LANES + at * cells, cells)],
            sems.at[index],
        )

    for index in range(len(pieces)):
        fetch(index).start()

    def add(at, carry):
        one, two = carry
        for part in range(4):
            lanes = pl.ds(pl.multiple_of((at * 4 + part) * LANES, LANES), LANES)
            value = maps[:, lanes].astype(jnp.float32)
            one, two = one + value, two + value * value
        return one, two

    carry = (jnp.zeros((channels, LANES), jnp.float32),) * 2
    for index, (level, at) in enumerate(pieces):
        tiles = TILES[level] // (4 if level == 0 else 1)
        start = FIRST[level] + at * tiles
        fetch(index).wait()
        carry = lax.fori_loop(start // 4, (start + tiles) // 4, add, carry)
    sums = [jnp.sum(item.T, axis=0, keepdims=True) for item in carry]
    me = lax.axis_index("roi")
    slots[me] = jnp.concatenate(
        [jnp.concatenate(sums, axis=1), facts[1:2], jnp.zeros((6, LANES), jnp.float32)], axis=0
    )
    met(rows - 1)
    for copy in share(slots, "roi", rows, sends, recvs):
        copy.wait()
    total = slots[0]
    for at in range(1, rows):
        total = total + slots[at]
    turned = pltpu.roll(total, channels, 1)
    low = lax.broadcasted_iota(jnp.int32, total.shape, 1) < channels
    mean = jnp.where(low, total, turned) / pixels
    inv_std = lax.rsqrt(jnp.where(low, turned, total) / pixels - mean * mean + EPSILON)
    scale = facts[...] * inv_std
    out[...] = jnp.concatenate(
        [mean[:1], scale[:1], inv_std[:1], total[1:2], jnp.zeros((4, LANES), jnp.float32)], axis=0
    )


def gather_small_kernel(rows, cols, mine, out, sends, recvs, col_sends, col_recvs, sem):
    row, col = lax.axis_index("roi"), lax.axis_index("col")
    greet("roi", rows)
    greet("col", cols)
    own = pltpu.make_async_copy(mine, out.at[col, row], sem)
    own.start()
    own.wait()
    met(rows + cols - 2)
    copies = [
        remote(mine, out.at[col, row], sends, recvs, step - 1, "roi", lax.rem(row + step, rows))
        for step in range(1, rows)
    ]
    for copy in copies:
        copy.start()
    for copy in copies:
        copy.wait()
    relay = Relay(lambda at: out.at[at], col_sends, col_recvs, 0)
    relay.start()
    relay.forward()
    relay.wait()


def place_wide(pieces, wide, sems, rows, high):
    few, piece = pieces.shape[2], pieces.shape[3]
    copies = []
    for position, owner in enumerate(ring_of(rows)):
        span = pl.ds((owner % high) * few, few)
        lanes = pl.ds((owner // high) * piece, piece)
        copies.append(
            pltpu.make_async_copy(
                pieces.at[position, pl.ds(0, LEADING)],
                wide.at[pl.ds(0, LEADING), span, lanes],
                sems.at[position, 0],
            )
        )
        for at in range(LEADING, len(KEPT)):
            copies.append(
                pltpu.make_async_copy(
                    pieces.at[position, at],
                    wide.at[KEPT[at], span, lanes],
                    sems.at[position, at - LEADING + 1],
                )
            )
    for copy in copies:
        copy.start()
    for at in SPARES:
        wide[at] = jnp.zeros(wide.shape[1:], wide.dtype)
    return copies


def head_kernel(
    rows, cols, classes, boxes, pooled, facts, score_bias, small, pieces,
    g6_all, g7_out, hid6_out, hid7_out, gs_out, scores_out, losses_out,
    wide, mine, taken, sems, sends, recvs, relay_sends, relay_recvs,
):
    me = lax.axis_index("col")
    rois, hidden = g6_all.shape
    quarter, piece = rois // cols, hidden // cols
    greet("col", cols)
    copies = place_wide(pieces, wide, sems, rows, rows // cols)
    met(cols - 1)
    for copy in copies:
        copy.wait()

    def sending(part, step):
        lanes = pl.ds(pl.multiple_of(part * piece, piece), piece)
        peer = lax.rem(me + step, cols)
        return pltpu.make_async_remote_copy(
            src_ref=mine.at[peer, :, lanes],
            dst_ref=taken.at[step - 1, :, lanes],
            send_sem=sends.at[step - 1, part],
            recv_sem=recvs.at[step - 1, part],
            device_id={"col": peer},
            device_id_type=MESH,
        )

    def first_layer(part, carry):
        lanes = pl.ds(pl.multiple_of(part * piece, piece), piece)
        weights = wide[:, :, lanes].reshape(WIDE, piece)
        result = jnp.dot(pooled[...], weights, preferred_element_type=jnp.float32)
        result = result.astype(jnp.bfloat16)
        for at in range(cols):
            mine[at, :, lanes] = result[at * quarter : (at + 1) * quarter]
        for step in range(1, cols):
            sending(part, step).start()
        return carry

    lax.fori_loop(0, cols, first_layer, 0)
    for part in range(cols):
        for step in range(1, cols):
            sending(part, step).wait()
    pre_six = mine[me].astype(jnp.float32)
    for step in range(1, cols):
        pre_six = pre_six + taken[step - 1].astype(jnp.float32)
    bias = jnp.concatenate(
        [jnp.sum(small[at, 0, 5, :3].astype(jnp.float32), axis=0, keepdims=True) for at in range(cols)],
        axis=1,
    )
    pre_six = pre_six + bias
    sigma_six = jax.nn.sigmoid(pre_six)
    hidden_six = (pre_six * sigma_six).astype(jnp.bfloat16)
    hid6_out[...] = hidden_six
    deep = [small[at, :, :4].reshape(hidden, piece) for at in range(cols)]
    head = jnp.concatenate(
        [small[at, row, 4, :, :LANES] for row in range(rows) for at in range(cols)], axis=0
    )
    lane = lax.broadcasted_iota(jnp.int32, (quarter, LANES), 1)
    pick = (lane == classes + boxes).astype(jnp.bfloat16)
    pre_seven = contract_last(pick, head)
    for at in range(cols):
        pre_seven = pre_seven + contract_last(
            hidden_six[:, at * piece : (at + 1) * piece], deep[at]
        )
    sigma_seven = jax.nn.sigmoid(pre_seven)
    hidden_seven = (pre_seven * sigma_seven).astype(jnp.bfloat16)
    hid7_out[...] = hidden_seven
    scores = jnp.dot(hidden_seven, head, preferred_element_type=jnp.float32) + score_bias[...]
    scores_out[...] = scores
    targets, onehot, weights = facts[0], facts[1], facts[2]
    is_class = lane < classes
    top = jnp.max(jnp.where(is_class, scores, -jnp.inf), axis=1, keepdims=True)
    powers = jnp.where(is_class, jnp.exp(jnp.where(is_class, scores - top, 0.0)), 0.0)
    log_total = top + jnp.log(jnp.sum(powers, axis=1, keepdims=True))
    picked = jnp.sum(onehot * scores, axis=1, keepdims=True)
    softmax = jnp.where(is_class, jnp.exp(jnp.where(is_class, scores - log_total, 0.0)), 0.0)
    misfit = jnp.where(is_class, 0.0, scores - targets)
    size = jnp.abs(misfit)
    huber = jnp.where(size < 1.0, 0.5 * misfit * misfit, size - 0.5)
    class_part = jnp.sum(weights[:, :1] * (log_total - picked), axis=0, keepdims=True)
    box_part = jnp.sum(jnp.where(is_class, 0.0, weights * huber), axis=0, keepdims=True)
    losses_out[...] = jnp.concatenate(
        [
            jnp.broadcast_to(class_part, (1, LANES)),
            box_part,
            jnp.zeros((6, LANES), jnp.float32),
        ],
        axis=0,
    )
    grads = jnp.where(is_class, softmax - onehot, jnp.clip(misfit, -1.0, 1.0))
    score_grads = (weights * grads).astype(jnp.bfloat16)
    gs_out[...] = score_grads
    slope_seven = sigma_seven * (1.0 + pre_seven * (1.0 - sigma_seven))
    g7 = (contract_last(score_grads, head) * slope_seven).astype(jnp.bfloat16)
    g7_out[...] = g7
    place = pl.ds(pl.multiple_of(me * quarter, quarter), quarter)
    for at in range(cols):
        lanes = slice(at * piece, (at + 1) * piece)
        back = jnp.dot(g7, deep[at], preferred_element_type=jnp.float32)
        sigma, value = sigma_six[:, lanes], pre_six[:, lanes]
        back = back * (sigma * (1.0 + value * (1.0 - sigma)))
        g6_all[place, lanes] = back.astype(jnp.bfloat16)
    relay = Relay(
        lambda at: g6_all.at[pl.ds(pl.multiple_of(at * quarter, quarter), quarter)],
        relay_sends, relay_recvs, 0,
    )
    relay.start()
    relay.forward()
    relay.wait()


def wide_grad_kernel(
    rows, cols, pooled, g6_all, g7, hid6, hid7, gs, losses,
    terms, g7_all, gs_all, losses_all,
    hid6_own, hid7_all, buffers, extras, head_term, out_sems, sends, recvs,
):
    me = lax.axis_index("col")
    rois, hidden = g6_all.shape
    quarter, piece = rois // cols, hidden // cols
    high = rows // cols
    few = buffers.shape[2] // 4
    ring = ring_of(rows)
    greet("col", cols)

    def block(at):
        return pl.ds(pl.multiple_of(at * quarter, quarter), quarter)

    g7_all[block(me), :] = g7[...]
    hid7_all[block(me), :] = hid7[...]
    gs_all[block(me), :] = gs[...]
    losses_all[me] = losses[...]
    own = pl.ds(pl.multiple_of(me * piece, piece), piece)
    hid6_own[block(me), :] = hid6[:, own]
    met(cols - 1)
    relays = [
        Relay(lambda at: g7_all.at[block(at)], sends, recvs, 0),
        Relay(lambda at: hid7_all.at[block(at)], sends, recvs, 3),
    ]
    for relay in relays:
        relay.start()
    copies = []
    for step in range(1, cols):
        peer = lax.rem(me + step, cols)
        theirs = pl.ds(pl.multiple_of(peer * piece, piece), piece)
        copies.append(
            remote(hid6.at[:, theirs], hid6_own.at[block(me)], sends, recvs, 5 + step, "col", peer)
        )
        copies.append(
            remote(gs, gs_all.at[block(me)], sends, recvs, 8 + step, "col", peer)
        )
        copies.append(
            remote(losses, losses_all.at[me], sends, recvs, 11 + step, "col", peer)
        )
    for copy in copies:
        copy.start()

    def leaving(slot, at):
        size = 4 * few
        span = pl.ds(pl.multiple_of(at * size, size), size)
        return pltpu.make_async_copy(buffers.at[slot], terms.at[:, span], out_sems.at[slot])

    def step(pair, carry):
        for slot in range(2):
            at = pair * 2 + slot

            @pl.when(pair > 0)
            def _():
                leaving(slot, at - 2).wait()

            lanes = pl.ds(pl.multiple_of(at * 2 * LANES, 2 * LANES), 2 * LANES)
            result = contract_first(pooled[:, lanes], g6_all[...]).astype(jnp.bfloat16)
            for position, owner in enumerate(ring):
                columns = slice((owner // high) * piece, (owner // high + 1) * piece)
                for part in range(4):
                    first = (part * high + owner % high) * few
                    buffers[slot, position, part * few : (part + 1) * few, :] = result[
                        first : first + few, columns
                    ]
            leaving(slot, at).start()
        return carry

    pairs = len(USED) // 4
    lax.fori_loop(0, pairs, step, 0)
    for relay in relays:
        relay.forward()
    for relay in relays:
        relay.wait()
    for copy in copies:
        copy.wait()
    deep_term = contract_first(g7_all[...], hid6_own[...]).astype(jnp.bfloat16)
    head_term[...] = contract_first(hid7_all[...], gs_all[...])
    owned, per = hidden // rows, hidden // (rows * cols)
    for position, owner in enumerate(ring):
        extras[position, :owned, :] = deep_term[owner * owned : (owner + 1) * owned]
        mine = pl.ds(pl.multiple_of(owner * owned + me * per, per), per)
        extras[position, owned : owned + per, :] = jnp.concatenate(
            [head_term[mine, :], jnp.zeros((per, piece - LANES), jnp.float32)], axis=1
        ).astype(jnp.bfloat16)
    for slot in range(2):
        leaving(slot, 2 * pairs - 2 + slot).wait()
    copies = [
        pltpu.make_async_copy(
            extras.at[:, pl.ds(at * few, few)],
            terms.at[:, pl.ds(SPARES[at] * few, few)],
            out_sems.at[2 + at],
        )
        for at in range((owned + per) // few)
    ]
    for copy in copies:
        copy.start()
    for copy in copies:
        copy.wait()


def pool_grad_kernel(
    rows, cols, pixels, g6_all, g7_all, gs_all, losses_all, centred, weight, stats, pieces,
    grads, totals, base, slope, wide, slots, sems, sends, recvs,
):
    row, col = lax.axis_index("roi"), lax.axis_index("col")
    rois, hidden = g6_all.shape
    channels = base.shape[0]
    piece = hidden // cols
    greet("roi", rows)
    copies = place_wide(pieces, wide, sems, rows, rows // cols)
    own = pl.ds(pl.multiple_of(col * piece, piece), piece)

    def columns(values):
        return jnp.sum(values.astype(jnp.float32), axis=0, keepdims=True)

    def as_rows(vector):
        return [
            vector[:, at * LANES : (at + 1) * LANES] for at in range(vector.shape[1] // LANES)
        ]

    bias_rows = as_rows(columns(g6_all[:, own])) + as_rows(columns(g7_all[...]))
    bias_rows += [columns(gs_all[...])]
    losses = losses_all[0]
    for at in range(1, cols):
        losses = losses + losses_all[at]
    for copy in copies:
        copy.wait()
    scale = stats[1:2]

    def step(at, carry):
        gain, shift = carry
        lanes = pl.ds(pl.multiple_of(at * 2 * LANES, 2 * LANES), 2 * LANES)
        weights = wide[pl.ds(at * 4, 4)].reshape(2 * LANES, hidden)
        result = contract_last(g6_all[...], weights)
        with_centred = result * centred[:, lanes].astype(jnp.float32)
        with_weight = result * weight[:, lanes].astype(jnp.float32)
        both = jnp.concatenate([scale, scale], axis=1)
        grads[:, lanes] = (result * both).astype(jnp.bfloat16)
        for half in range(2):
            part = slice(half * LANES, (half + 1) * LANES)
            gain = gain + jnp.sum(with_centred[:, part].reshape(rois // 8, 8, LANES), axis=0)
            shift = shift + jnp.sum(with_weight[:, part].reshape(rois // 8, 8, LANES), axis=0)
        return gain, shift

    nothing = jnp.zeros((8, LANES), jnp.float32)
    gain, shift = lax.fori_loop(0, len(USED) // 2, step, (nothing, nothing))
    low = lax.broadcasted_iota(jnp.int32, (8, LANES), 1) < channels
    both = jnp.where(
        low, gain + pltpu.roll(gain, channels, 1), shift + pltpu.roll(shift, channels, 1)
    )
    both = jnp.sum(both, axis=0, keepdims=True)
    lines = [both] + bias_rows + [losses[:2]]
    count = 1 + len(bias_rows) + 2
    lines.append(jnp.zeros((16 - count, LANES), jnp.float32))
    slots[row] = jnp.concatenate(lines, axis=0)
    met(rows - 1)
    for copy in share(slots, "roi", rows, sends, recvs):
        copy.wait()
    total = slots[0]
    for at in range(1, rows):
        total = total + slots[at]
    gain_grad = total[:1] * stats[2:3]
    totals[...] = jnp.concatenate([total[:15], gain_grad], axis=0)
    slope_row = -stats[1:2] * stats[2:3] * gain_grad / pixels
    shift_grad = pltpu.roll(jnp.broadcast_to(total[:1], (8, LANES)), channels, 1)[:1]
    base_row = -stats[1:2] * shift_grad / pixels - slope_row * stats[:1]
    slope[...] = jnp.broadcast_to(slope_row[:, :channels], (LANES, channels)).T
    base[...] = jnp.broadcast_to(base_row[:, :channels], (LANES, channels)).T


def restore_kernel(few, term, out, half):
    for part in range(out.shape[1] // LANES):
        lanes = slice(part * LANES, (part + 1) * LANES)
        for slot in range(len(KEPT)):
            at = KEPT[slot]
            place = pl.ds(at // 2 % 7 * 7 + at // 14 + 4 * (at % 2), few, stride=49)
            half[part, place, :] = term[at * few : (at + 1) * few, lanes].astype(jnp.float32)
        out[:, lanes] = half[part]


def comm_params(number):
    return pltpu.CompilerParams(
        vmem_limit_bytes=LIMIT, collective_id=number, has_side_effects=True
    )


def shaped(shape, dtype):
    return jax.ShapeDtypeStruct(shape, dtype)


def statistics(facts, planes, rows, pixels):
    channels = planes[0].shape[1]
    return pl.pallas_call(
        functools.partial(stats_kernel, rows, pixels),
        out_shape=shaped((8, LANES), jnp.float32),
        in_specs=[VMEM, ANY, ANY, ANY, ANY],
        out_specs=VMEM,
        scratch_shapes=[
            pltpu.VMEM((channels, ALL_TILES * LANES), jnp.bfloat16),
            pltpu.VMEM((rows, 8, LANES), jnp.float32),
            pltpu.SemaphoreType.DMA((7,)),
            pltpu.SemaphoreType.DMA((rows - 1,)),
            pltpu.SemaphoreType.DMA((rows - 1,)),
        ],
        compiler_params=comm_params(0),
        name="statistics",
    )(facts, *planes)


def gather_small(mine, rows, cols):
    return pl.pallas_call(
        functools.partial(gather_small_kernel, rows, cols),
        out_shape=shaped((cols, rows) + mine.shape, mine.dtype),
        in_specs=[VMEM],
        out_specs=VMEM,
        scratch_shapes=[
            pltpu.SemaphoreType.DMA((rows - 1,)),
            pltpu.SemaphoreType.DMA((rows - 1,)),
            pltpu.SemaphoreType.DMA((3,)),
            pltpu.SemaphoreType.DMA((3,)),
            pltpu.SemaphoreType.DMA,
        ],
        compiler_params=comm_params(1),
        name="gather_small",
    )(mine)


def run_head(pooled, facts, score_bias, small, pieces, rows, cols, classes, boxes):
    rois, channels = pooled.shape[0], LANES // 2
    quarter, hidden = rois // cols, pieces.shape[3] * cols
    bf16, f32 = jnp.bfloat16, jnp.float32
    return pl.pallas_call(
        functools.partial(head_kernel, rows, cols, classes, boxes),
        out_shape=(
            shaped((rois, hidden), bf16),
            shaped((quarter, hidden), bf16),
            shaped((quarter, hidden), bf16),
            shaped((quarter, hidden), bf16),
            shaped((quarter, LANES), bf16),
            shaped((quarter, LANES), f32),
            shaped((8, LANES), f32),
        ),
        in_specs=[VMEM, VMEM, VMEM, VMEM, ANY],
        out_specs=(VMEM,) * 7,
        scratch_shapes=[
            pltpu.VMEM((2 * len(USED), channels, hidden), bf16),
            pltpu.VMEM((cols, quarter, hidden), bf16),
            pltpu.VMEM((cols - 1, quarter, hidden), bf16),
            pltpu.SemaphoreType.DMA((rows, 8)),
            pltpu.SemaphoreType.DMA((cols - 1, cols)),
            pltpu.SemaphoreType.DMA((cols - 1, cols)),
            pltpu.SemaphoreType.DMA((3,)),
            pltpu.SemaphoreType.DMA((3,)),
        ],
        compiler_params=comm_params(2),
        name="head",
    )(pooled, facts, score_bias, small, pieces)


def wide_grads(pooled, g6_all, g7, hid6, hid7, gs, losses, rows, cols):
    rois, hidden = g6_all.shape
    piece, few = hidden // cols, LANES // 2 // (rows // cols)
    owned, per = hidden // rows, hidden // (rows * cols)
    bf16, f32 = jnp.bfloat16, jnp.float32
    return pl.pallas_call(
        functools.partial(wide_grad_kernel, rows, cols),
        out_shape=(
            shaped((rows, 2 * len(USED) * few, piece), bf16),
            shaped((rois, hidden), bf16),
            shaped((rois, LANES), bf16),
            shaped((cols, 8, LANES), f32),
        ),
        in_specs=[VMEM] * 7,
        out_specs=(ANY, VMEM, VMEM, VMEM),
        scratch_shapes=[
            pltpu.VMEM((rois, piece), bf16),
            pltpu.VMEM((rois, hidden), bf16),
            pltpu.VMEM((2, rows, 4 * few, piece), bf16),
            pltpu.VMEM((rows, owned + per, piece), bf16),
            pltpu.VMEM((hidden, LANES), f32),
            pltpu.SemaphoreType.DMA((2 + len(SPARES),)),
            pltpu.SemaphoreType.DMA((15,)),
            pltpu.SemaphoreType.DMA((15,)),
        ],
        compiler_params=comm_params(3),
        name="wide_grads",
    )(pooled, g6_all, g7, hid6, hid7, gs, losses)


def pool_grads(g6_all, g7_all, gs_all, losses_all, centred, weight, stats, pieces, rows, cols, pixels):
    rois, hidden = g6_all.shape
    channels = LANES // 2
    bf16, f32 = jnp.bfloat16, jnp.float32
    return pl.pallas_call(
        functools.partial(pool_grad_kernel, rows, cols, pixels),
        out_shape=(
            shaped((rois, WIDE), bf16),
            shaped((16, LANES), f32),
            shaped((channels, LANES), f32),
            shaped((channels, LANES), f32),
        ),
        in_specs=[VMEM] * 7 + [ANY],
        out_specs=(VMEM,) * 4,
        scratch_shapes=[
            pltpu.VMEM((2 * len(USED), channels, hidden), bf16),
            pltpu.VMEM((rows, 16, LANES), f32),
            pltpu.SemaphoreType.DMA((rows, 8)),
            pltpu.SemaphoreType.DMA((rows - 1,)),
            pltpu.SemaphoreType.DMA((rows - 1,)),
        ],
        compiler_params=comm_params(4),
        name="pool_grads",
    )(g6_all, g7_all, gs_all, losses_all, centred, weight, stats, pieces)


def restore(term, few):
    return pl.pallas_call(
        functools.partial(restore_kernel, few),
        out_shape=shaped((49 * few, term.shape[1]), jnp.float32),
        in_specs=[VMEM],
        out_specs=VMEM,
        scratch_shapes=[pltpu.VMEM((term.shape[1] // LANES, 49 * few, LANES), jnp.float32)],
        compiler_params=pltpu.CompilerParams(vmem_limit_bytes=LIMIT),
        name="restore",
    )(term)


def targets_of(mine_boxes, mine_goals):
    prop_width = mine_boxes[2] - mine_boxes[0]
    prop_height = mine_boxes[3] - mine_boxes[1]
    prop_cx = mine_boxes[0] + 0.5 * prop_width
    prop_cy = mine_boxes[1] + 0.5 * prop_height
    goal_width = mine_goals[2] - mine_goals[0]
    goal_height = mine_goals[3] - mine_goals[1]
    goal_cx = mine_goals[0] + 0.5 * goal_width
    goal_cy = mine_goals[1] + 0.5 * goal_height
    return jnp.stack(
        [
            10.0 * (goal_cx - prop_cx) / prop_width,
            10.0 * (goal_cy - prop_cy) / prop_height,
            5.0 * jnp.log(goal_width / prop_width),
            5.0 * jnp.log(goal_height / prop_height),
        ],
        axis=1,
    )


def decode(mine_boxes, deltas):
    prop_width = mine_boxes[2] - mine_boxes[0]
    prop_height = mine_boxes[3] - mine_boxes[1]
    prop_cx = mine_boxes[0] + 0.5 * prop_width
    prop_cy = mine_boxes[1] + 0.5 * prop_height
    centre_x = prop_cx + deltas[:, 0] / 10.0 * prop_width
    centre_y = prop_cy + deltas[:, 1] / 10.0 * prop_height
    new_width = prop_width * jnp.exp(deltas[:, 2] / 5.0)
    new_height = prop_height * jnp.exp(deltas[:, 3] / 5.0)
    return jnp.stack(
        [
            centre_x - 0.5 * new_width,
            centre_y - 0.5 * new_height,
            centre_x + 0.5 * new_width,
            centre_y + 0.5 * new_height,
        ]
    ) / (CANVAS // 2)


def local_near(
    p2, p3, p4, p5, norm_gain, norm_bias, fc6_weight, fc6_bias, fc7_weight, fc7_bias,
    cls_weight, cls_bias, box_weight, box_bias, roi_boxes, roi_level, roi_image,
    canvas_offsets, labels, target_boxes, valid,
):
    channels = p2.shape[1]
    rois = roi_level.shape[0]
    cols = lax.axis_size("col")
    rows = lax.axis_size("roi")
    piece = fc6_bias.shape[0]
    high = rows // cols
    few = channels // high
    planes = (p2, p3, p4, p5)
    pixels = rows * sum(plane.shape[2] for plane in planes)
    ring = ring_of(rows)
    per = fc7_bias.shape[0]
    classes, boxes = cls_weight.shape[1], box_weight.shape[1]
    bf16, f32 = jnp.bfloat16, jnp.float32

    block = fc6_weight.reshape(few, 7, 7, piece)
    block = jnp.pad(block, ((0, 0), (0, 0), (0, 1), (0, 0))).reshape(few, 7, 2, 4, piece)
    block = block.transpose(3, 1, 2, 0, 4).reshape(2 * len(USED), few, piece)
    block = jnp.concatenate([block[:LEADING], block[LEADING::2]])
    pairs = [
        ((kappa * high + rho % high) * cols + rho // high, rho * cols + kappa)
        for rho in range(rows)
        for kappa in range(cols)
    ]
    block = lax.ppermute(block, ("roi", "col"), pairs)
    pieces = lax.all_gather(block, "roi", axis=0, axis_index_groups=[ring])

    head = jnp.concatenate([cls_weight, box_weight, fc7_bias[:, None]], axis=1)
    head = jnp.pad(head, ((0, 0), (0, piece - head.shape[1])))
    bias_high = fc6_bias.astype(bf16)
    rest = fc6_bias - bias_high.astype(f32)
    bias_mid = rest.astype(bf16)
    bias_low = (rest - bias_mid.astype(f32)).astype(bf16)
    bias = jnp.pad(jnp.stack([bias_high, bias_mid, bias_low]), ((0, few - 3), (0, 0)))
    small = jnp.concatenate([fc7_weight, head, bias], axis=0).reshape(SMALL, few, piece)

    def twice(vector):
        return jnp.concatenate([vector, vector])[None]

    count = jnp.sum(valid.astype(f32))
    norm_facts = jnp.concatenate(
        [twice(norm_gain), jnp.full((1, LANES), count), jnp.zeros((6, LANES), f32)]
    )
    stats = statistics(norm_facts, planes, rows, float(pixels))
    valid_total = stats[3, 0]

    picks = roi_image[None, :] == jnp.arange(4, dtype=jnp.int32)[:, None]
    shift_x = jnp.sum(jnp.where(picks, canvas_offsets[0][:, None], 0), axis=0)
    shift_y = jnp.sum(jnp.where(picks, canvas_offsets[1][:, None], 0), axis=0)
    floats, ints, order = region_tables(
        (roi_boxes[0] + shift_x).astype(f32),
        (roi_boxes[1] + shift_y).astype(f32),
        (roi_boxes[2] + shift_x).astype(f32),
        (roi_boxes[3] + shift_y).astype(f32),
        roi_level,
    )
    pooled, centred, weight = pool_maps(
        floats, ints, order, stats[:1], stats[1:2], twice(norm_bias), planes, rois
    )
    small = gather_small(small, rows, cols)

    quarter = rois // cols
    first_row = lax.axis_index("col") * quarter
    mine_labels = lax.dynamic_slice_in_dim(labels, first_row, quarter)
    mine_valid = lax.dynamic_slice_in_dim(valid, first_row, quarter).astype(f32)
    mine_boxes = lax.dynamic_slice_in_dim(roi_boxes, first_row, quarter, axis=1).astype(f32)
    mine_goals = lax.dynamic_slice_in_dim(target_boxes, first_row, quarter, axis=1).astype(f32)
    foreground = mine_valid * (mine_labels > 0).astype(f32)
    loss_scale = rois * rows / valid_total
    lane = jnp.arange(LANES, dtype=jnp.int32)[None, :]
    after = LANES - classes - boxes
    facts = jnp.stack(
        [
            jnp.pad(targets_of(mine_boxes, mine_goals), ((0, 0), (classes, after))),
            (mine_labels[:, None] == lane).astype(f32),
            loss_scale
            * jnp.where(
                lane < classes,
                mine_valid[:, None],
                jnp.where(lane < classes + boxes, foreground[:, None], 0.0),
            ),
        ]
    )
    score_bias = jnp.pad(jnp.concatenate([cls_bias, box_bias]), (0, after))[None]
    g6_all, g7, hid6, hid7, gs, scores, losses = run_head(
        pooled, facts, score_bias, small, pieces, rows, cols, classes, boxes
    )
    decoded = decode(mine_boxes, scores[:, classes : classes + boxes])

    terms, g7_all, gs_all, losses_all = wide_grads(
        pooled, g6_all, g7, hid6, hid7, gs, losses, rows, cols
    )
    wide_rows = terms.shape[1]
    term = lax.psum_scatter(
        terms.reshape(rows * wide_rows, piece), "roi", scatter_dimension=0, tiled=True,
        axis_index_groups=[ring],
    )
    back = lax.ppermute(term, ("roi", "col"), [(there, here) for here, there in pairs])
    fc6_weight_grad = restore(back, few)
    extra = [
        term[SPARES[at] * few : (SPARES[at] + 1) * few].astype(f32)
        for at in range((fc7_weight.shape[0] + per) // few)
    ]
    fc7_weight_grad = jnp.concatenate(extra[:-1], axis=0)
    cls_weight_grad = extra[-1][:, :classes]
    box_weight_grad = extra[-1][:, classes : classes + boxes]

    grads, totals, base, slope = pool_grads(
        g6_all, g7_all, gs_all, losses_all, centred, weight, stats, pieces, rows, cols,
        float(pixels),
    )
    input_grads = unpool_maps(floats, ints, order, base, slope, grads, planes, rois)
    fc6_bias_grad = totals[1 : 1 + piece // LANES].reshape(-1)
    seven = totals[1 + piece // LANES :][: cols * piece // LANES].reshape(-1)
    place = (lax.axis_index("roi") * cols + lax.axis_index("col")) * per
    fc7_bias_grad = lax.dynamic_slice_in_dim(seven, place, per)
    line = 1 + (cols + 1) * piece // LANES
    return (
        totals[line + 1, 0] / (rois * rows),
        jnp.sum(totals[line + 2]) / (rois * rows),
        decoded,
        *input_grads,
        totals[15, :channels],
        totals[0, channels:],
        fc6_weight_grad,
        fc6_bias_grad,
        fc7_weight_grad,
        fc7_bias_grad,
        cls_weight_grad,
        totals[line, :classes],
        box_weight_grad,
        totals[line, classes : classes + boxes],
    )


def solution(mesh):
    near = mesh.shape["roi"] == 2 * mesh.shape["col"] and mesh.shape["col"] == 4
    return jax.shard_map(
        local_near if near else local,
        mesh=mesh,
        in_specs=(
            P("roi", "col", None),
            P("roi", "col", None),
            P("roi", "col", None),
            P("roi", "col", None),
            P("col"),
            P("col"),
            P("roi", "col"),
            P("col"),
            P("roi", "col"),
            P(("roi", "col")),
            P(("roi", "col"), None),
            P(),
            P(("roi", "col"), None),
            P(),
            P(None, "roi"),
            P("roi"),
            P("roi"),
            P(None, "roi"),
            P("roi"),
            P(None, "roi"),
            P("roi"),
        ),
        out_specs=(
            P(),
            P(),
            P(None, ("roi", "col")),
            P("roi", "col", None),
            P("roi", "col", None),
            P("roi", "col", None),
            P("roi", "col", None),
            P("col"),
            P("col"),
            P("roi", "col"),
            P("col"),
            P("roi", "col"),
            P(("roi", "col")),
            P(("roi", "col"), None),
            P(),
            P(("roi", "col"), None),
            P(),
        ),
        check_vma=False,
    )
```

```python
import functools
import math

import jax
import jax.numpy as jnp
from jax import lax
from jax.experimental import pallas as pl
from jax.experimental.pallas import tpu as pltpu
from jax.sharding import PartitionSpec as P

CANVAS = 1024
EPSILON = 1e-05
LANES = 128
SPAN = 10
GROUP = 16
MORE = 8
SPARE = 8
SIDES = tuple(CANVAS // (4 * 2**level) for level in range(4))
TILES = tuple(side * side // LANES for side in SIDES)
FIRST = tuple(sum(TILES[:level]) for level in range(4))
ALL_TILES = sum(TILES)
PADDED = ALL_TILES + max(SPAN - min(TILES), 0)
SLOTS = 32
USED = tuple(slot for slot in range(SLOTS) if slot % 8 < 7)
WIDE = len(USED) * LANES
F32_FIELDS = 7
I32_FIELDS = 6


def silu_slope(values):
    sigma = jax.nn.sigmoid(values)
    return sigma * (1.0 + values * (1.0 - sigma))


def contract_first(left_m, right_m):
    return lax.dot_general(
        left_m, right_m, (((0,), (0,)), ((), ())), preferred_element_type=jnp.float32
    )


def contract_last(left_m, right_m):
    return lax.dot_general(
        left_m, right_m, (((1,), (1,)), ((), ())), preferred_element_type=jnp.float32
    )


def region_tables(left, top, right, bottom, level):
    def by_level(values):
        chosen = jnp.full(level.shape, values[0])
        for at in range(1, 4):
            chosen = jnp.where(level == at, values[at], chosen)
        return chosen

    step = by_level([4.0 * 2**at for at in range(4)])
    side = by_level(list(SIDES))
    rows_log = by_level([(max(LANES // n, 1)).bit_length() - 1 for n in SIDES])
    across = by_level([max(n // LANES, 1) for n in SIDES])
    x_anchor, x_extent = left / step - 0.5, (right - left) / step
    y_anchor, y_extent = top / step - 0.5, (bottom - top) / step

    def window(anchor, extent):
        low = jnp.floor(anchor + extent * (0.5 / 14.0)).astype(jnp.int32)
        high = jnp.floor(anchor + extent * (13.5 / 14.0)).astype(jnp.int32) + 1
        return jnp.clip(low, 0, side - 1), jnp.clip(high, 0, side - 1)

    y_low, y_high = window(y_anchor, y_extent)
    x_low, x_high = window(x_anchor, x_extent)
    group_low, group_high = y_low >> rows_log, y_high >> rows_log
    chunks = (group_high - group_low + SPAN) // SPAN
    group = jnp.maximum(jnp.minimum(group_low, (side >> rows_log) - chunks * SPAN), 0)
    tile_x = x_low // LANES
    tiles_x = x_high // LANES - tile_x + 1
    first_tile = by_level(list(FIRST)) + group * across + tile_x
    mask = jnp.minimum(side, LANES) - 1
    shift = 7 - rows_log
    rows_per = (1 << rows_log).astype(jnp.float32)
    nothing = jnp.zeros((SPARE,), jnp.int32)
    parts = chunks * tiles_x
    key = 2 * (level > 0).astype(jnp.int32) + (parts > 1).astype(jnp.int32)
    rois = level.shape[0]
    at = jnp.arange(rois, dtype=jnp.int32)
    before = (key[None, :] < key[:, None]) | (
        (key[None, :] == key[:, None]) & (at[None, :] < at[:, None])
    )
    rank = jnp.sum(before.astype(jnp.int32), axis=1)
    order = jnp.sum(jnp.where(rank[None, :] == at[:, None], at[None, :], 0), axis=1)
    order = jnp.concatenate([order, jnp.full((GROUP,), rois, jnp.int32)])
    ends = jnp.stack([jnp.sum((key <= last).astype(jnp.int32)) for last in range(4)])
    floats = jnp.stack(
        [
            x_anchor,
            x_extent,
            y_anchor,
            y_extent,
            (tile_x * LANES).astype(jnp.float32),
            group.astype(jnp.float32) * rows_per,
            rows_per,
        ]
    ).astype(jnp.float32)
    ints = jnp.stack([first_tile, across, mask, shift, parts, tiles_x]).astype(jnp.int32)
    away = jnp.full((F32_FIELDS, SPARE), -1e6, jnp.float32)
    floats = jnp.concatenate([floats, away], axis=1)
    ints = jnp.concatenate([ints, jnp.broadcast_to(nothing, (I32_FIELDS, SPARE))], axis=1)
    return floats.reshape(-1), ints.reshape(-1), jnp.concatenate([order, ends])


def window_weights(floats, ints, rois, region, chunk, tile_x):
    rois = rois + SPARE
    x_anchor, x_extent, y_anchor, y_extent, x_origin, y_origin, rows_per = (
        floats[at * rois + region] for at in range(F32_FIELDS)
    )
    first_tile, across, mask, shift = (ints[at * rois + region] for at in range(4))
    if chunk is not None:
        first_tile = first_tile + chunk * (SPAN * across) + tile_x
        x_origin = x_origin + (tile_x * LANES).astype(jnp.float32)
        y_origin = y_origin + (chunk * SPAN).astype(jnp.float32) * rows_per
    lane = lax.broadcasted_iota(jnp.int32, (8, LANES), 1)
    bin_at = lax.broadcasted_iota(jnp.int32, (8, LANES), 0)
    x_cell = (lane & mask).astype(jnp.float32) + x_origin
    y_cell = lax.shift_right_logical(lane, jnp.broadcast_to(shift, lane.shape)).astype(
        jnp.float32
    ) + y_origin
    part = jnp.where(bin_at < 7, (2.0 * bin_at.astype(jnp.float32) + 0.5) / 14.0, -1e6)
    near = y_anchor + y_extent * part - y_cell
    far = y_anchor + y_extent * (part + 1.0 / 14.0) - y_cell

    def tent(distance):
        return jnp.maximum(1.0 - jnp.abs(distance), 0.0)

    across_w = []
    for j in range(7):
        one = x_anchor + x_extent * ((2 * j + 0.5) / 14.0)
        two = x_anchor + x_extent * ((2 * j + 1.5) / 14.0)
        across_w.append(0.25 * (tent(one - x_cell) + tent(two - x_cell)))
    across_w.append(jnp.zeros((8, LANES), jnp.float32))
    packed = [
        jnp.concatenate([across_w[2 * at], across_w[2 * at + 1]], axis=0).astype(jnp.bfloat16)
        for at in range(4)
    ]
    blocks = []
    for at in range(SPAN):
        offset = rows_per * float(at)
        down = tent(near - offset) + tent(far - offset)
        both = jnp.concatenate([down, down], axis=0).astype(jnp.bfloat16)
        blocks.append(jnp.concatenate([both * item for item in packed], axis=0))
    return jnp.concatenate(blocks, axis=1), first_tile, across


def tile_lanes(first_tile, across, at):
    return pl.ds(pl.multiple_of((first_tile + at * across) * LANES, LANES), LANES)


def for_groups(order, start, stop, size, body):
    def step(at, carry):
        first = start + at * size
        inside = [first + index < stop for index in range(size)]
        spare = order.shape[0] - 5
        places = [
            jnp.where(good, first + index, spare) for index, good in enumerate(inside)
        ]
        body([order[place] for place in places])
        return carry

    lax.fori_loop(0, (stop - start + size - 1) // size, step, 0)


def for_parts(ints, order, rois, start, stop, size, body):
    stride = rois + SPARE

    def second(regions):
        for region in regions:
            tiles_x = ints[5 * stride + region]
            wide = (tiles_x > 1).astype(jnp.int32)
            body(region, 1 - wide, wide)

    for_groups(order, start, stop, size, second)

    def later(at, carry):
        region = order[at]
        tiles_x = ints[5 * stride + region]

        def part(index, inner):
            chunk = index // tiles_x
            body(region, chunk, index - chunk * tiles_x)
            return inner

        return lax.fori_loop(2, ints[4 * stride + region], part, carry)

    lax.fori_loop(start, stop, later, 0)


def ends_of(order):
    size = order.shape[0]
    return [order[size - 4 + at] for at in range(4)]


def pool_kernel(
    rois, floats, ints, order, mean, scale, shift, p2, p3, p4, p5,
    pooled_out, centred_out, weight_out, maps, values, sems,
):
    channels = mean.shape[1] // 2
    stride = rois + SPARE
    copies = []
    for level, plane in enumerate((p2, p3, p4, p5)):
        cells = TILES[level] * LANES
        copies.append(
            pltpu.make_async_copy(
                plane.at[0],
                maps.at[pl.ds(0, channels), pl.ds(FIRST[level] * LANES, cells)],
                sems.at[level],
            )
        )
        copies[-1].start()
    ones = jnp.ones((16, 8 * LANES), jnp.bfloat16)

    def fill(at, carry):
        lanes = pl.ds(pl.multiple_of(at * 8 * LANES, 8 * LANES), 8 * LANES)
        maps[pl.ds(channels, 16), lanes] = ones
        return carry

    lax.fori_loop(0, ALL_TILES // 8, fill, 0)
    extra = PADDED - ALL_TILES
    if extra:
        maps[:, pl.ds(ALL_TILES * LANES, extra * LANES)] = jnp.zeros(
            (channels + 16, extra * LANES), jnp.bfloat16
        )
    for copy in copies:
        copy.wait()

    def item(region, chunk, tile_x):
        kernel_w, first_tile, across = window_weights(floats, ints, rois, region, chunk, tile_x)
        cells = jnp.concatenate(
            [maps[:, tile_lanes(first_tile, across, at)] for at in range(SPAN)], axis=1
        )
        return contract_last(kernel_w, cells)

    def place(region):
        return pl.ds(region, 2 * SLOTS, stride=stride)

    def first(regions):
        for region in regions:
            values[place(region), : channels + 16] = item(region, None, None)

    def further(region, chunk, tile_x):
        values[place(region), : channels + 16] = values[place(region), : channels + 16] + item(region, chunk, tile_x)

    low_end, low_multi, rest_end, all_end = ends_of(order)
    for_groups(order, 0, all_end, GROUP, first)
    for_parts(ints, order, rois, low_end, low_multi, MORE, further)
    for_parts(ints, order, rois, rest_end, all_end, MORE, further)
    low_lane = lax.broadcasted_iota(jnp.int32, (rois, LANES), 1) < channels
    for at, slot in enumerate(USED):
        lanes = pl.ds(at * LANES, LANES)
        one = values[pl.ds(slot * stride, rois), :]
        two = values[pl.ds((slot + SLOTS) * stride, rois), :]
        value = jnp.where(low_lane, one, pltpu.roll(two, channels, 1))
        total = jnp.where(low_lane, one[:, channels : channels + 1], two[:, channels : channels + 1])
        centred = value - mean[...] * total
        centred_out[:, lanes] = centred.astype(jnp.bfloat16)
        weight_out[:, lanes] = total.astype(jnp.bfloat16)
        pooled_out[:, lanes] = (centred * scale[...] + shift[...] * total).astype(jnp.bfloat16)


def unpool_kernel(
    rois, floats, ints, order, base, slope, grads, p2, p3, p4, p5,
    o2, o3, o4, o5, maps, sums, slots, sems, out_sems,
):
    channels = base.shape[0]
    stride = rois + SPARE
    planes, outs = (p2, p3, p4, p5), (o2, o3, o4, o5)
    pieces = [(level, at) for level in range(4) for at in range(4 if level == 0 else 1)]

    def fetch(index):
        level, at = pieces[index]
        cells = TILES[level] * LANES // (4 if level == 0 else 1)
        return pltpu.make_async_copy(
            planes[level].at[0, :, pl.ds(at * cells, cells)],
            maps.at[:, pl.ds(FIRST[level] * LANES + at * cells, cells)],
            sems.at[index],
        )

    for index in range(len(pieces)):
        fetch(index).start()
    for slot in range(SLOTS):
        rows = pl.ds(slot * stride, rois)
        slots[pl.ds(slot * stride + rois, SPARE), :] = jnp.zeros((SPARE, LANES), jnp.float32)
        if slot in USED:
            lanes = pl.ds(USED.index(slot) * LANES, LANES)
            slots[rows, :] = grads[:, lanes].astype(jnp.float32)
        else:
            slots[rows, :] = jnp.zeros((rois, LANES), jnp.float32)
    base_v, slope_v = base[...], slope[...]

    def begin(at, carry):
        for part in range(4):
            lanes = pl.ds(pl.multiple_of((at * 4 + part) * LANES, LANES), LANES)
            sums[:, lanes] = base_v + slope_v * maps[:, lanes].astype(jnp.float32)
        return carry

    for index, (level, at) in enumerate(pieces):
        tiles = TILES[level] // (4 if level == 0 else 1)
        start = FIRST[level] + at * tiles
        fetch(index).wait()
        lax.fori_loop(start // 4, (start + tiles) // 4, begin, 0)
    extra = PADDED - ALL_TILES
    if extra:
        sums[:, pl.ds(ALL_TILES * LANES, extra * LANES)] = jnp.zeros(
            (channels, extra * LANES), jnp.float32
        )

    def item(region, chunk, tile_x):
        kernel_w, first_tile, across = window_weights(floats, ints, rois, region, chunk, tile_x)
        mine = slots[pl.ds(region, SLOTS, stride=stride), :]
        stacked = jnp.concatenate([mine[:, :channels], mine[:, channels:]], axis=0)
        turned = stacked.T.astype(jnp.bfloat16)
        result = jnp.dot(turned, kernel_w, preferred_element_type=jnp.float32)
        for at in range(SPAN):
            lanes = tile_lanes(first_tile, across, at)
            sums[:, lanes] = sums[:, lanes] + result[:, at * LANES : (at + 1) * LANES]

    def first(regions):
        for region in regions:
            item(region, None, None)

    def send(level):
        cells = TILES[level] * LANES
        return pltpu.make_async_copy(
            sums.at[:, pl.ds(FIRST[level] * LANES, cells)], outs[level].at[0], out_sems.at[level]
        )

    low_end, low_multi, rest_end, all_end = ends_of(order)
    for_groups(order, 0, low_multi, GROUP, first)
    for_parts(ints, order, rois, low_end, low_multi, MORE, item)
    send(0).start()
    for_groups(order, low_multi, all_end, GROUP, first)
    for_parts(ints, order, rois, rest_end, all_end, MORE, item)
    for level in range(1, 4):
        send(level).start()
    for level in range(4):
        send(level).wait()


ANY = pl.BlockSpec(memory_space=pl.ANY)
SMEM = pl.BlockSpec(memory_space=pltpu.SMEM)
VMEM = pl.BlockSpec(memory_space=pltpu.VMEM)
LIMIT = 60 * 1024 * 1024


def pool_maps(floats, ints, order, mean, scale, shift, planes, rois):
    channels = planes[0].shape[1]
    flat = jax.ShapeDtypeStruct((rois, WIDE), jnp.bfloat16)
    return pl.pallas_call(
        functools.partial(pool_kernel, rois),
        out_shape=(flat, flat, flat),
        in_specs=[SMEM, SMEM, SMEM, VMEM, VMEM, VMEM, ANY, ANY, ANY, ANY],
        out_specs=(VMEM, VMEM, VMEM),
        scratch_shapes=[
            pltpu.VMEM((channels + 16, PADDED * LANES), jnp.bfloat16),
            pltpu.VMEM((2 * SLOTS * (rois + SPARE), LANES), jnp.float32),
            pltpu.SemaphoreType.DMA((4,)),
        ],
        compiler_params=pltpu.CompilerParams(vmem_limit_bytes=LIMIT),
        name="pool",
    )(floats, ints, order, mean, scale, shift, *planes)


def unpool_maps(floats, ints, order, base, slope, grads, planes, rois):
    channels = planes[0].shape[1]
    return pl.pallas_call(
        functools.partial(unpool_kernel, rois),
        out_shape=tuple(jax.ShapeDtypeStruct(plane.shape, jnp.float32) for plane in planes),
        in_specs=[SMEM, SMEM, SMEM, VMEM, VMEM, VMEM, ANY, ANY, ANY, ANY],
        out_specs=(ANY, ANY, ANY, ANY),
        scratch_shapes=[
            pltpu.VMEM((channels, ALL_TILES * LANES), jnp.bfloat16),
            pltpu.VMEM((channels, PADDED * LANES), jnp.float32),
            pltpu.VMEM((SLOTS * (rois + SPARE), LANES), jnp.float32),
            pltpu.SemaphoreType.DMA((7,)),
            pltpu.SemaphoreType.DMA((4,)),
        ],
        compiler_params=pltpu.CompilerParams(vmem_limit_bytes=LIMIT),
        name="unpool",
    )(floats, ints, order, base, slope, grads, *planes)


def local(
    p2, p3, p4, p5, norm_gain, norm_bias, fc6_weight, fc6_bias, fc7_weight, fc7_bias,
    cls_weight, cls_bias, box_weight, box_bias, roi_boxes, roi_level, roi_image,
    canvas_offsets, labels, target_boxes, valid,
):
    channels = p2.shape[1]
    rois = roi_level.shape[0]
    cols = lax.axis_size("col")
    rows = lax.axis_size("roi")
    hidden = fc6_bias.shape[0] * cols
    piece = fc6_bias.shape[0]
    high = rows // cols
    few = channels // high
    planes = (p2, p3, p4, p5)

    block = fc6_weight.reshape(few, 7, 7, piece)
    block = jnp.pad(block, ((0, 0), (0, 0), (0, 1), (0, 0))).reshape(few, 7, 2, 4, piece)
    block = block.transpose(3, 1, 2, 0, 4).reshape(len(USED) * 2, few, piece)
    pairs = [
        ((kappa * high + rho // cols) * cols + rho % cols, rho * cols + kappa)
        for rho in range(rows)
        for kappa in range(cols)
    ]
    block = lax.ppermute(block, ("roi", "col"), pairs)
    wide = lax.all_gather(block, "roi", axis=0)
    wide = wide.reshape(high, cols, len(USED) * 2, few, piece)
    wide = wide.transpose(2, 0, 3, 1, 4).reshape(WIDE, hidden)

    per = fc7_bias.shape[0]
    classes, boxes = cls_weight.shape[1], box_weight.shape[1]
    head = jnp.concatenate([cls_weight, box_weight, fc7_bias[:, None]], axis=1)
    head = jnp.pad(head, ((0, 0), (0, piece - head.shape[1])))
    bias_high = fc6_bias.astype(jnp.bfloat16)
    rest = fc6_bias - bias_high.astype(jnp.float32)
    bias_mid = rest.astype(jnp.bfloat16)
    bias_low = (rest - bias_mid.astype(jnp.float32)).astype(jnp.bfloat16)
    small = jnp.concatenate(
        [fc7_weight, head, jnp.stack([bias_high, bias_mid, bias_low])], axis=0
    )
    deep_rows = fc7_weight.shape[0]
    small = jnp.pad(small, ((0, -small.shape[0] % 16), (0, 0)))
    small = lax.all_gather(small, ("roi", "col"), axis=0)
    deep = small[:, :deep_rows].reshape(rows, cols, deep_rows, piece)
    deep = deep.transpose(0, 2, 1, 3).reshape(hidden, hidden)
    head = small[:, deep_rows : deep_rows + per].reshape(hidden, piece)[:, :LANES]
    bias_seven = head[:, classes + boxes].astype(jnp.float32)
    bias_six = small[:cols, deep_rows + per : deep_rows + per + 3].astype(jnp.float32)
    bias_six = jnp.sum(bias_six, axis=1).reshape(hidden)

    values = [plane[0].astype(jnp.float32) for plane in planes]
    pixel_total = rows * sum(plane.shape[1] for plane in values)
    first_sum = sum(jnp.sum(plane, axis=1) for plane in values)
    second_sum = sum(jnp.sum(plane * plane, axis=1) for plane in values)
    local_valid = jnp.sum(valid.astype(jnp.float32))
    first_sum, second_sum, valid_total = lax.psum((first_sum, second_sum, local_valid), "roi")
    mean = first_sum / pixel_total
    variance = second_sum / pixel_total - mean * mean
    inv_std = lax.rsqrt(variance + EPSILON)
    scale = norm_gain * inv_std

    picks = roi_image[None, :] == jnp.arange(4, dtype=jnp.int32)[:, None]
    shift_x = jnp.sum(jnp.where(picks, canvas_offsets[0][:, None], 0), axis=0)
    shift_y = jnp.sum(jnp.where(picks, canvas_offsets[1][:, None], 0), axis=0)
    floats, ints, order = region_tables(
        (roi_boxes[0] + shift_x).astype(jnp.float32),
        (roi_boxes[1] + shift_y).astype(jnp.float32),
        (roi_boxes[2] + shift_x).astype(jnp.float32),
        (roi_boxes[3] + shift_y).astype(jnp.float32),
        roi_level,
    )

    def twice(vector):
        return jnp.concatenate([vector, vector])[None]

    pooled, centred, weight = pool_maps(
        floats, ints, order, twice(mean), twice(scale), twice(norm_bias), planes, rois
    )

    partial_six = jnp.dot(pooled, wide, preferred_element_type=jnp.float32).astype(jnp.bfloat16)
    pre_six = lax.psum_scatter(partial_six, "col", scatter_dimension=0, tiled=True)
    pre_six = pre_six.astype(jnp.float32) + bias_six
    hidden_six = jax.nn.silu(pre_six).astype(jnp.bfloat16)
    pre_seven = contract_last(hidden_six, deep) + bias_seven
    hidden_seven = jax.nn.silu(pre_seven).astype(jnp.bfloat16)
    scores = jnp.dot(hidden_seven, head, preferred_element_type=jnp.float32)
    logits = scores[:, :classes] + cls_bias
    deltas = scores[:, classes : classes + boxes] + box_bias

    quarter = rois // cols
    first_row = lax.axis_index("col") * quarter
    mine_labels = lax.dynamic_slice_in_dim(labels, first_row, quarter)
    mine_valid = lax.dynamic_slice_in_dim(valid, first_row, quarter).astype(jnp.float32)
    mine_boxes = lax.dynamic_slice_in_dim(roi_boxes, first_row, quarter, axis=1).astype(jnp.float32)
    mine_goals = lax.dynamic_slice_in_dim(target_boxes, first_row, quarter, axis=1).astype(
        jnp.float32
    )
    prop_width = mine_boxes[2] - mine_boxes[0]
    prop_height = mine_boxes[3] - mine_boxes[1]
    prop_cx = mine_boxes[0] + 0.5 * prop_width
    prop_cy = mine_boxes[1] + 0.5 * prop_height
    goal_width = mine_goals[2] - mine_goals[0]
    goal_height = mine_goals[3] - mine_goals[1]
    goal_cx = mine_goals[0] + 0.5 * goal_width
    goal_cy = mine_goals[1] + 0.5 * goal_height
    targets = jnp.stack(
        [
            10.0 * (goal_cx - prop_cx) / prop_width,
            10.0 * (goal_cy - prop_cy) / prop_height,
            5.0 * jnp.log(goal_width / prop_width),
            5.0 * jnp.log(goal_height / prop_height),
        ],
        axis=1,
    )
    foreground = mine_valid * (mine_labels > 0).astype(jnp.float32)
    top_logit = jnp.max(logits, axis=1, keepdims=True)
    log_total = top_logit[:, 0] + jnp.log(jnp.sum(jnp.exp(logits - top_logit), axis=1))
    onehot = (mine_labels[:, None] == jnp.arange(classes, dtype=jnp.int32)[None, :]).astype(
        jnp.float32
    )
    picked = jnp.sum(onehot * logits, axis=1)
    misfit = deltas - targets
    huber_terms = jnp.where(jnp.abs(misfit) < 1.0, 0.5 * misfit * misfit, jnp.abs(misfit) - 0.5)
    class_part = jnp.sum(mine_valid * (log_total - picked))
    box_part = jnp.sum(foreground * jnp.sum(huber_terms, axis=1))
    centre_x = prop_cx + deltas[:, 0] / 10.0 * prop_width
    centre_y = prop_cy + deltas[:, 1] / 10.0 * prop_height
    new_width = prop_width * jnp.exp(deltas[:, 2] / 5.0)
    new_height = prop_height * jnp.exp(deltas[:, 3] / 5.0)
    decoded = jnp.stack(
        [
            centre_x - 0.5 * new_width,
            centre_y - 0.5 * new_height,
            centre_x + 0.5 * new_width,
            centre_y + 0.5 * new_height,
        ]
    ) / (CANVAS // 2)
    loss_scale = rois * rows / valid_total
    softmax = jnp.exp(logits - log_total[:, None])
    logit_grads = loss_scale * mine_valid[:, None] * (softmax - onehot)
    delta_grads = loss_scale * foreground[:, None] * jnp.clip(misfit, -1.0, 1.0)
    score_grads = jnp.concatenate([logit_grads, delta_grads], axis=1)
    score_grads = jnp.pad(score_grads, ((0, 0), (0, LANES - score_grads.shape[1])))
    score_grads = score_grads.astype(jnp.bfloat16)

    head_term = contract_first(hidden_seven, score_grads)
    hidden_grads = contract_last(score_grads, head)
    pre_seven_grads = (hidden_grads * silu_slope(pre_seven)).astype(jnp.bfloat16)
    deep_term = contract_first(pre_seven_grads, hidden_six)
    six_hidden_grads = jnp.dot(pre_seven_grads, deep, preferred_element_type=jnp.float32)
    pre_six_grads = (six_hidden_grads * silu_slope(pre_six)).astype(jnp.bfloat16)
    six_grads_all = lax.all_gather(pre_six_grads, "col", axis=0, tiled=True)

    wide_term = contract_first(pooled, six_grads_all).astype(jnp.bfloat16)
    wide_term = wide_term.reshape(len(USED) * 2, high, few, cols, piece)
    wide_term = wide_term.transpose(1, 3, 0, 2, 4).reshape(rows * len(USED) * 2, few, piece)
    wide_grad = lax.psum_scatter(wide_term, "roi", scatter_dimension=0, tiled=True)
    wide_grad = lax.ppermute(wide_grad, ("roi", "col"), [(there, here) for here, there in pairs])
    wide_grad = wide_grad.reshape(4, 7, 2, few, piece).transpose(3, 1, 2, 0, 4)
    wide_grad = wide_grad.reshape(few, 7, 8, piece)[:, :, :7].reshape(few * 49, piece)
    fc6_weight_grad = wide_grad.astype(jnp.float32)

    sums = jnp.concatenate(
        [
            jnp.sum(score_grads.astype(jnp.float32), axis=0),
            jnp.stack([class_part, box_part]),
        ]
    )
    everyone = rows * cols
    deep_term = deep_term.reshape(rows, deep_rows, cols, piece).transpose(0, 2, 1, 3)
    deep_term = deep_term.reshape(everyone, deep_rows, piece)
    seven_bias_term = jnp.sum(pre_seven_grads.astype(jnp.float32), axis=0)
    head_term = jnp.concatenate(
        [head_term[:, : classes + boxes], seven_bias_term[:, None]], axis=1
    )
    head_term = jnp.pad(head_term, ((0, 0), (0, piece - head_term.shape[1])))
    head_term = head_term.reshape(everyone, per, piece)
    six_bias_term = jnp.sum(pre_six_grads.astype(jnp.float32), axis=0).reshape(cols, 1, piece)
    six_bias_term = jnp.broadcast_to(six_bias_term[None], (rows, cols, 1, piece))
    six_bias_term = six_bias_term.reshape(everyone, 1, piece)
    sums = jnp.pad(sums, (0, piece - sums.shape[0]))
    sums = jnp.broadcast_to(sums[None, None], (everyone, 1, piece))
    small_term = jnp.concatenate([deep_term, head_term, six_bias_term, sums], axis=1)
    small_term = jnp.pad(small_term, ((0, 0), (0, -small_term.shape[1] % 8), (0, 0)))
    small_grad = lax.psum_scatter(small_term, ("roi", "col"), scatter_dimension=0, tiled=True)[0]
    fc7_weight_grad = small_grad[:deep_rows]
    head_grad = small_grad[deep_rows : deep_rows + per]
    cls_weight_grad = head_grad[:, :classes]
    box_weight_grad = head_grad[:, classes : classes + boxes]
    fc7_bias_grad = head_grad[:, classes + boxes]
    fc6_bias_grad = small_grad[deep_rows + per]
    sums = small_grad[deep_rows + per + 1]
    class_bias_grad = sums[:classes]
    box_bias_grad = sums[classes : classes + boxes]
    cls_loss = sums[LANES] / valid_total
    box_loss = sums[LANES + 1] / valid_total

    pool_grads = contract_last(six_grads_all, wide)
    gain_part = jnp.sum(pool_grads * centred.astype(jnp.float32), axis=0)
    shift_part = jnp.sum(pool_grads * weight.astype(jnp.float32), axis=0)
    gain_part = jnp.sum(gain_part.reshape(-1, channels), axis=0) * inv_std
    shift_part = jnp.sum(shift_part.reshape(-1, channels), axis=0)
    norm_gain_grad, norm_bias_grad = lax.psum((gain_part, shift_part), "roi")

    scaled = (pool_grads * jnp.tile(scale, WIDE // channels)).astype(jnp.bfloat16)
    slope = -scale * inv_std * norm_gain_grad / pixel_total
    base = -scale * norm_bias_grad / pixel_total - slope * mean

    def spread(vector):
        return jnp.broadcast_to(vector[:, None], (channels, LANES))

    input_grads = unpool_maps(floats, ints, order, spread(base), spread(slope), scaled, planes, rois)
    return (
        cls_loss,
        box_loss,
        decoded,
        input_grads[0],
        input_grads[1],
        input_grads[2],
        input_grads[3],
        norm_gain_grad,
        norm_bias_grad,
        fc6_weight_grad,
        fc6_bias_grad,
        fc7_weight_grad,
        fc7_bias_grad,
        cls_weight_grad,
        class_bias_grad,
        box_weight_grad,
        box_bias_grad,
    )


MESH = pl.DeviceIdType.MESH
KEPT = tuple(at for at in range(2 * len(USED)) if at % 2 == 0 or at // 2 < 21)
LEADING = 42
SPARES = tuple(at for at in range(2 * len(USED)) if at not in KEPT)
SMALL = 5


def ring_of(rows):
    return list(range(0, rows, 2)) + list(range(rows - 1, 0, -2))


def origin(kappa, rows, cols, position):
    far = position >= rows // 2
    plane = rows - 1 - position if far else position
    code = lax.rem(plane + cols - kappa, cols)
    return 2 * lax.rem(code, 2) + lax.div(code, 2), int(far)


def position_of(kappa, rows, cols, block, half):
    plane = lax.rem(2 * (block % 2) + block // 2 + kappa, cols)
    return rows - 1 - plane if half else plane


def greet(axis, count):
    barrier = pltpu.get_barrier_semaphore()
    me = lax.axis_index(axis)
    for step in range(1, count):
        pl.semaphore_signal(
            barrier,
            inc=1,
            device_id={axis: lax.rem(me + step, count)},
            device_id_type=MESH,
        )


def met(count):
    pl.semaphore_wait(pltpu.get_barrier_semaphore(), count)


def remote(src, dst, sends, recvs, at, axis, peer):
    return pltpu.make_async_remote_copy(
        src_ref=src,
        dst_ref=dst,
        send_sem=sends.at[at],
        recv_sem=recvs.at[at],
        device_id={axis: peer},
        device_id_type=MESH,
    )


def share(slots, axis, count, sends, recvs, first=0):
    me = lax.axis_index(axis)
    copies = [
        remote(slots.at[me], slots.at[me], sends, recvs, first + step - 1, axis,
               lax.rem(me + step, count))
        for step in range(1, count)
    ]
    for copy in copies:
        copy.start()
    return copies


def neighbours(me):
    core, chip = lax.rem(me, 2), lax.div(me, 2)
    return me + 1 - 2 * core, me + 2 - 4 * chip


class Relay:
    def __init__(self, view, sends, recvs, first):
        me = lax.axis_index("col")
        core, chip = neighbours(me)
        self.near = remote(view(me), view(me), sends, recvs, first, "col", core)
        self.far = remote(view(me), view(me), sends, recvs, first + 1, "col", chip)
        self.passed = remote(view(chip), view(chip), sends, recvs, first + 2, "col", core)

    def start(self):
        self.far.start()
        self.near.start()

    def forward(self):
        self.far.wait_recv()
        self.passed.start()

    def wait(self):
        self.near.wait()
        self.far.wait_send()
        self.passed.wait()


def stats_kernel(
    rows, pixels, facts, p2, p3, p4, p5, out, maps, slots, sems, sends, recvs
):
    channels = maps.shape[0]
    planes = (p2, p3, p4, p5)
    pieces = [(level, at) for level in range(4) for at in range(4 if level == 0 else 1)]
    greet("roi", rows)

    def fetch(index):
        level, at = pieces[index]
        cells = TILES[level] * LANES // (4 if level == 0 else 1)
        return pltpu.make_async_copy(
            planes[level].at[0, :, pl.ds(at * cells, cells)],
            maps.at[:, pl.ds(FIRST[level] * LANES + at * cells, cells)],
            sems.at[index],
        )

    for index in range(len(pieces)):
        fetch(index).start()

    def add(at, carry):
        one, two = carry
        for part in range(4):
            lanes = pl.ds(pl.multiple_of((at * 4 + part) * LANES, LANES), LANES)
            value = maps[:, lanes].astype(jnp.float32)
            one, two = one + value, two + value * value
        return one, two

    carry = (jnp.zeros((channels, LANES), jnp.float32),) * 2
    for index, (level, at) in enumerate(pieces):
        tiles = TILES[level] // (4 if level == 0 else 1)
        start = FIRST[level] + at * tiles
        fetch(index).wait()
        carry = lax.fori_loop(start // 4, (start + tiles) // 4, add, carry)
    sums = [jnp.sum(item.T, axis=0, keepdims=True) for item in carry]
    me = lax.axis_index("roi")
    slots[me] = jnp.concatenate(
        [jnp.concatenate(sums, axis=1), facts[1:2], jnp.zeros((6, LANES), jnp.float32)], axis=0
    )
    met(rows - 1)
    for copy in share(slots, "roi", rows, sends, recvs):
        copy.wait()
    total = slots[0]
    for at in range(1, rows):
        total = total + slots[at]
    turned = pltpu.roll(total, channels, 1)
    low = lax.broadcasted_iota(jnp.int32, total.shape, 1) < channels
    mean = jnp.where(low, total, turned) / pixels
    inv_std = lax.rsqrt(jnp.where(low, turned, total) / pixels - mean * mean + EPSILON)
    scale = facts[...] * inv_std
    out[...] = jnp.concatenate(
        [mean[:1], scale[:1], inv_std[:1], total[1:2], jnp.zeros((4, LANES), jnp.float32)], axis=0
    )


def gather_small_kernel(rows, cols, mine, out, sends, recvs, col_sends, col_recvs, sem):
    row, col = lax.axis_index("roi"), lax.axis_index("col")
    depth = rows // 2
    plane, side = lax.div(row, 2), lax.rem(row, 2)
    partner = row + 1 - 2 * side
    greet("roi", rows)
    greet("col", cols)
    own = pltpu.make_async_copy(mine, out.at[col, row], sem)
    own.start()
    own.wait()
    met(rows + cols - 2)
    along = [
        remote(mine, out.at[col, row], sends, recvs, step - 1, "roi",
               lax.rem(plane + step, depth) * 2 + side)
        for step in range(1, depth)
    ]
    across = []
    for step in range(depth):
        source = lax.rem(plane + depth - step, depth) * 2 + side
        block = out.at[col, source]
        across.append(remote(block, block, sends, recvs, depth - 1 + step, "roi", partner))
    for copy in along:
        copy.start()
    across[0].start()
    for step in range(1, depth):
        along[step - 1].wait_recv()
        across[step].start()
    for copy in along:
        copy.wait_send()
    for copy in across:
        copy.wait()
    relay = Relay(lambda at: out.at[at], col_sends, col_recvs, 0)
    relay.start()
    relay.forward()
    relay.wait()


def place_wide(pieces, wide, sems, rows, cols):
    few, piece = pieces.shape[2], pieces.shape[3]
    kappa = lax.axis_index("col")
    copies = []
    for position in range(rows):
        block, half = origin(kappa, rows, cols, position)
        span = pl.ds(half * few, few)
        lanes = pl.ds(pl.multiple_of(block * piece, piece), piece)
        copies.append(
            pltpu.make_async_copy(
                pieces.at[position, pl.ds(0, LEADING)],
                wide.at[pl.ds(0, LEADING), span, lanes],
                sems.at[position, 0],
            )
        )
        for at in range(LEADING, len(KEPT)):
            copies.append(
                pltpu.make_async_copy(
                    pieces.at[position, at],
                    wide.at[KEPT[at], span, lanes],
                    sems.at[position, at - LEADING + 1],
                )
            )
    for copy in copies:
        copy.start()
    for at in SPARES:
        wide[at] = jnp.zeros(wide.shape[1:], wide.dtype)
    return copies


def head_kernel(
    rows, cols, classes, boxes, pooled, facts, score_bias, small, pieces,
    g6_all, g7_out, hid6_out, hid7_out, gs_out, scores_out, losses_out,
    wide, mine, taken, sems, sends, recvs, relay_sends, relay_recvs,
):
    me = lax.axis_index("col")
    rois, hidden = g6_all.shape
    quarter, piece = rois // cols, hidden // cols
    greet("col", cols)
    copies = place_wide(pieces, wide, sems, rows, cols)
    met(cols - 1)
    for copy in copies:
        copy.wait()

    def sending(part, step):
        lanes = pl.ds(pl.multiple_of(part * piece, piece), piece)
        peer = lax.rem(me + step, cols)
        return pltpu.make_async_remote_copy(
            src_ref=mine.at[peer, :, lanes],
            dst_ref=taken.at[step - 1, :, lanes],
            send_sem=sends.at[step - 1, part],
            recv_sem=recvs.at[step - 1, part],
            device_id={"col": peer},
            device_id_type=MESH,
        )

    def first_layer(part, carry):
        lanes = pl.ds(pl.multiple_of(part * piece, piece), piece)
        weights = wide[:, :, lanes].reshape(WIDE, piece)
        result = jnp.dot(pooled[...], weights, preferred_element_type=jnp.float32)
        result = result.astype(jnp.bfloat16)
        for at in range(cols):
            mine[at, :, lanes] = result[at * quarter : (at + 1) * quarter]
        for step in range(1, cols):
            sending(part, step).start()
        return carry

    lax.fori_loop(0, cols, first_layer, 0)
    for part in range(cols):
        for step in range(1, cols):
            sending(part, step).wait()
    pre_six = mine[me].astype(jnp.float32)
    for step in range(1, cols):
        pre_six = pre_six + taken[step - 1].astype(jnp.float32)
    lines = [small[at, 0, 4, :16, LANES:].astype(jnp.float32) for at in range(cols)]
    bias = jnp.concatenate(
        [
            (line[part : part + 1] + line[part + 2 : part + 3]) + line[part + 4 : part + 5]
            for line in lines
            for part in range(2)
        ],
        axis=1,
    )
    pre_six = pre_six + bias
    sigma_six = jax.nn.sigmoid(pre_six)
    hidden_six = (pre_six * sigma_six).astype(jnp.bfloat16)
    hid6_out[...] = hidden_six
    deep = [small[at, :, :4].reshape(hidden, piece) for at in range(cols)]
    head = jnp.concatenate(
        [small[at, row, 4, :, :LANES] for row in range(rows) for at in range(cols)], axis=0
    )
    lane = lax.broadcasted_iota(jnp.int32, (quarter, LANES), 1)
    pick = (lane == classes + boxes).astype(jnp.bfloat16)
    pre_seven = contract_last(pick, head)
    for at in range(cols):
        pre_seven = pre_seven + contract_last(
            hidden_six[:, at * piece : (at + 1) * piece], deep[at]
        )
    sigma_seven = jax.nn.sigmoid(pre_seven)
    hidden_seven = (pre_seven * sigma_seven).astype(jnp.bfloat16)
    hid7_out[...] = hidden_seven
    scores = jnp.dot(hidden_seven, head, preferred_element_type=jnp.float32) + score_bias[...]
    scores_out[...] = scores
    targets, onehot, weights = facts[0], facts[1], facts[2]
    is_class = lane < classes
    top = jnp.max(jnp.where(is_class, scores, -jnp.inf), axis=1, keepdims=True)
    powers = jnp.where(is_class, jnp.exp(jnp.where(is_class, scores - top, 0.0)), 0.0)
    log_total = top + jnp.log(jnp.sum(powers, axis=1, keepdims=True))
    picked = jnp.sum(onehot * scores, axis=1, keepdims=True)
    softmax = jnp.where(is_class, jnp.exp(jnp.where(is_class, scores - log_total, 0.0)), 0.0)
    misfit = jnp.where(is_class, 0.0, scores - targets)
    size = jnp.abs(misfit)
    huber = jnp.where(size < 1.0, 0.5 * misfit * misfit, size - 0.5)
    class_part = jnp.sum(weights[:, :1] * (log_total - picked), axis=0, keepdims=True)
    box_part = jnp.sum(jnp.where(is_class, 0.0, weights * huber), axis=0, keepdims=True)
    grads = jnp.where(is_class, softmax - onehot, jnp.clip(misfit, -1.0, 1.0))
    score_grads = (weights * grads).astype(jnp.bfloat16)
    gs_out[...] = score_grads
    losses_out[...] = jnp.concatenate(
        [
            jnp.broadcast_to(class_part, (1, LANES)),
            box_part,
            jnp.sum(score_grads.astype(jnp.float32), axis=0, keepdims=True),
            jnp.zeros((5, LANES), jnp.float32),
        ],
        axis=0,
    )
    slope_seven = sigma_seven * (1.0 + pre_seven * (1.0 - sigma_seven))
    g7 = (contract_last(score_grads, head) * slope_seven).astype(jnp.bfloat16)
    g7_out[...] = g7
    place = pl.ds(pl.multiple_of(me * quarter, quarter), quarter)
    for at in range(cols):
        lanes = slice(at * piece, (at + 1) * piece)
        back = jnp.dot(g7, deep[at], preferred_element_type=jnp.float32)
        sigma, value = sigma_six[:, lanes], pre_six[:, lanes]
        back = back * (sigma * (1.0 + value * (1.0 - sigma)))
        g6_all[place, lanes] = back.astype(jnp.bfloat16)
    relay = Relay(
        lambda at: g6_all.at[pl.ds(pl.multiple_of(at * quarter, quarter), quarter)],
        relay_sends, relay_recvs, 0,
    )
    relay.start()
    relay.forward()
    relay.wait()


def wide_grad_kernel(
    rows, cols, pooled, g6_all, g7, hid6, hid7, gs, losses,
    terms, g7_all, losses_all,
    hid6_own, buffers, extras, head_mine, head_taken, out_sems, sends, recvs,
):
    me = lax.axis_index("col")
    rois, hidden = g6_all.shape
    quarter, piece = rois // cols, hidden // cols
    owned, per = hidden // rows, hidden // (rows * cols)
    few = buffers.shape[2] // 4
    ring = ring_of(rows)
    greet("col", cols)

    def block(at):
        return pl.ds(pl.multiple_of(at * quarter, quarter), quarter)

    g7_all[block(me), :] = g7[...]
    losses_all[me] = losses[...]
    own = pl.ds(pl.multiple_of(me * piece, piece), piece)
    hid6_own[block(me), :] = hid6[:, own]
    head_term = contract_first(hid7[...], gs[...]).astype(jnp.bfloat16)
    for row in range(rows):
        for at in range(cols):
            first = row * owned + at * per
            head_mine[at, row] = head_term[first : first + per]
    met(cols - 1)
    relay = Relay(lambda at: g7_all.at[block(at)], sends, recvs, 0)
    relay.start()
    copies = []
    for step in range(1, cols):
        peer = lax.rem(me + step, cols)
        theirs = pl.ds(pl.multiple_of(peer * piece, piece), piece)
        copies.append(
            remote(hid6.at[:, theirs], hid6_own.at[block(me)], sends, recvs, 2 + step, "col", peer)
        )
        copies.append(
            remote(head_mine.at[peer], head_taken.at[step - 1], sends, recvs, 5 + step, "col", peer)
        )
        copies.append(
            remote(losses, losses_all.at[me], sends, recvs, 8 + step, "col", peer)
        )
    for copy in copies:
        copy.start()

    def leaving(slot, at):
        size = 4 * few
        span = pl.ds(pl.multiple_of(at * size, size), size)
        return pltpu.make_async_copy(buffers.at[slot], terms.at[:, span], out_sems.at[slot])

    def step(pair, carry):
        for slot in range(2):
            at = pair * 2 + slot

            @pl.when(pair > 0)
            def _():
                leaving(slot, at - 2).wait()

            lanes = pl.ds(pl.multiple_of(at * 2 * LANES, 2 * LANES), 2 * LANES)
            result = contract_first(pooled[:, lanes], g6_all[...]).astype(jnp.bfloat16)
            for column in range(cols):
                columns = slice(column * piece, (column + 1) * piece)
                for half in range(2):
                    position = position_of(me, rows, cols, column, half)
                    for part in range(4):
                        first = (part * 2 + half) * few
                        buffers[slot, position, part * few : (part + 1) * few, :] = result[
                            first : first + few, columns
                        ]
            leaving(slot, at).start()
        return carry

    pairs = len(USED) // 4
    lax.fori_loop(0, pairs - 3, step, 0)
    relay.forward()
    lax.fori_loop(pairs - 3, pairs, step, 0)
    relay.wait()
    for copy in copies:
        copy.wait()
    deep_term = contract_first(g7_all[...], hid6_own[...]).astype(jnp.bfloat16)
    nothing = jnp.zeros((per, piece - LANES), jnp.bfloat16)
    for position, owner in enumerate(ring):
        extras[position, :owned, :] = deep_term[owner * owned : (owner + 1) * owned]
        total = head_mine[me, owner].astype(jnp.float32)
        for at in range(cols - 1):
            total = total + head_taken[at, owner].astype(jnp.float32)
        extras[position, owned : owned + per, :] = jnp.concatenate(
            [total.astype(jnp.bfloat16), nothing], axis=1
        )
    for slot in range(2):
        leaving(slot, 2 * pairs - 2 + slot).wait()
    copies = [
        pltpu.make_async_copy(
            extras.at[:, pl.ds(at * few, few)],
            terms.at[:, pl.ds(SPARES[at] * few, few)],
            out_sems.at[2 + at],
        )
        for at in range((owned + per) // few)
    ]
    for copy in copies:
        copy.start()
    for copy in copies:
        copy.wait()


def pool_grad_kernel(
    rows, cols, pixels, g6_all, g7_all, losses_all, centred, weight, stats, pieces,
    grads, totals, base, slope, wide, slots, sems, sends, recvs,
):
    row, col = lax.axis_index("roi"), lax.axis_index("col")
    rois, hidden = g6_all.shape
    channels = base.shape[0]
    piece = hidden // cols
    greet("roi", rows)
    copies = place_wide(pieces, wide, sems, rows, cols)
    own = pl.ds(pl.multiple_of(col * piece, piece), piece)

    def columns(values):
        return jnp.sum(values.astype(jnp.float32), axis=0, keepdims=True)

    def as_rows(vector):
        return [
            vector[:, at * LANES : (at + 1) * LANES] for at in range(vector.shape[1] // LANES)
        ]

    bias_rows = as_rows(columns(g6_all[:, own])) + as_rows(columns(g7_all[...]))
    losses = losses_all[0]
    for at in range(1, cols):
        losses = losses + losses_all[at]
    for copy in copies:
        copy.wait()
    scale = stats[1:2]

    def step(at, carry):
        gain, shift = carry
        lanes = pl.ds(pl.multiple_of(at * 2 * LANES, 2 * LANES), 2 * LANES)
        weights = wide[pl.ds(at * 4, 4)].reshape(2 * LANES, hidden)
        result = contract_last(g6_all[...], weights)
        with_centred = result * centred[:, lanes].astype(jnp.float32)
        with_weight = result * weight[:, lanes].astype(jnp.float32)
        both = jnp.concatenate([scale, scale], axis=1)
        grads[:, lanes] = (result * both).astype(jnp.bfloat16)
        for half in range(2):
            part = slice(half * LANES, (half + 1) * LANES)
            gain = gain + jnp.sum(with_centred[:, part].reshape(rois // 8, 8, LANES), axis=0)
            shift = shift + jnp.sum(with_weight[:, part].reshape(rois // 8, 8, LANES), axis=0)
        return gain, shift

    nothing = jnp.zeros((8, LANES), jnp.float32)
    gain, shift = lax.fori_loop(0, len(USED) // 2, step, (nothing, nothing))
    low = lax.broadcasted_iota(jnp.int32, (8, LANES), 1) < channels
    both = jnp.where(
        low, gain + pltpu.roll(gain, channels, 1), shift + pltpu.roll(shift, channels, 1)
    )
    both = jnp.sum(both, axis=0, keepdims=True)
    lines = [both] + bias_rows + [losses[2:3], losses[:2]]
    count = 1 + len(bias_rows) + 3
    lines.append(jnp.zeros((16 - count, LANES), jnp.float32))
    slots[row] = jnp.concatenate(lines, axis=0)
    met(rows - 1)
    for copy in share(slots, "roi", rows, sends, recvs):
        copy.wait()
    total = slots[0]
    for at in range(1, rows):
        total = total + slots[at]
    gain_grad = total[:1] * stats[2:3]
    totals[...] = jnp.concatenate([total[:15], gain_grad], axis=0)
    slope_row = -stats[1:2] * stats[2:3] * gain_grad / pixels
    shift_grad = pltpu.roll(jnp.broadcast_to(total[:1], (8, LANES)), channels, 1)[:1]
    base_row = -stats[1:2] * shift_grad / pixels - slope_row * stats[:1]
    slope[...] = jnp.broadcast_to(slope_row[:, :channels], (LANES, channels)).T
    base[...] = jnp.broadcast_to(base_row[:, :channels], (LANES, channels)).T


def restore_kernel(few, term, out, half):
    for part in range(out.shape[1] // LANES):
        lanes = slice(part * LANES, (part + 1) * LANES)
        for slot in range(len(KEPT)):
            at = KEPT[slot]
            place = pl.ds(at // 2 % 7 * 7 + at // 14 + 4 * (at % 2), few, stride=49)
            half[part, place, :] = term[at * few : (at + 1) * few, lanes].astype(jnp.float32)
        out[:, lanes] = half[part]


def comm_params(number):
    return pltpu.CompilerParams(
        vmem_limit_bytes=LIMIT, collective_id=number, has_side_effects=True
    )


def shaped(shape, dtype):
    return jax.ShapeDtypeStruct(shape, dtype)


def statistics(facts, planes, rows, pixels):
    channels = planes[0].shape[1]
    return pl.pallas_call(
        functools.partial(stats_kernel, rows, pixels),
        out_shape=shaped((8, LANES), jnp.float32),
        in_specs=[VMEM, ANY, ANY, ANY, ANY],
        out_specs=VMEM,
        scratch_shapes=[
            pltpu.VMEM((channels, ALL_TILES * LANES), jnp.bfloat16),
            pltpu.VMEM((rows, 8, LANES), jnp.float32),
            pltpu.SemaphoreType.DMA((7,)),
            pltpu.SemaphoreType.DMA((rows - 1,)),
            pltpu.SemaphoreType.DMA((rows - 1,)),
        ],
        compiler_params=comm_params(0),
        name="statistics",
    )(facts, *planes)


def gather_small(mine, rows, cols):
    return pl.pallas_call(
        functools.partial(gather_small_kernel, rows, cols),
        out_shape=shaped((cols, rows) + mine.shape, mine.dtype),
        in_specs=[VMEM],
        out_specs=VMEM,
        scratch_shapes=[
            pltpu.SemaphoreType.DMA((rows - 1,)),
            pltpu.SemaphoreType.DMA((rows - 1,)),
            pltpu.SemaphoreType.DMA((3,)),
            pltpu.SemaphoreType.DMA((3,)),
            pltpu.SemaphoreType.DMA,
        ],
        compiler_params=comm_params(1),
        name="gather_small",
    )(mine)


def run_head(pooled, facts, score_bias, small, pieces, rows, cols, classes, boxes):
    rois, channels = pooled.shape[0], LANES // 2
    quarter, hidden = rois // cols, pieces.shape[3] * cols
    bf16, f32 = jnp.bfloat16, jnp.float32
    return pl.pallas_call(
        functools.partial(head_kernel, rows, cols, classes, boxes),
        out_shape=(
            shaped((rois, hidden), bf16),
            shaped((quarter, hidden), bf16),
            shaped((quarter, hidden), bf16),
            shaped((quarter, hidden), bf16),
            shaped((quarter, LANES), bf16),
            shaped((quarter, LANES), f32),
            shaped((8, LANES), f32),
        ),
        in_specs=[VMEM, VMEM, VMEM, VMEM, ANY],
        out_specs=(VMEM,) * 7,
        scratch_shapes=[
            pltpu.VMEM((2 * len(USED), channels, hidden), bf16),
            pltpu.VMEM((cols, quarter, hidden), bf16),
            pltpu.VMEM((cols - 1, quarter, hidden), bf16),
            pltpu.SemaphoreType.DMA((rows, 8)),
            pltpu.SemaphoreType.DMA((cols - 1, cols)),
            pltpu.SemaphoreType.DMA((cols - 1, cols)),
            pltpu.SemaphoreType.DMA((3,)),
            pltpu.SemaphoreType.DMA((3,)),
        ],
        compiler_params=comm_params(2),
        name="head",
    )(pooled, facts, score_bias, small, pieces)


def wide_grads(pooled, g6_all, g7, hid6, hid7, gs, losses, rows, cols):
    rois, hidden = g6_all.shape
    piece, few = hidden // cols, LANES // 2 // (rows // cols)
    owned, per = hidden // rows, hidden // (rows * cols)
    bf16, f32 = jnp.bfloat16, jnp.float32
    return pl.pallas_call(
        functools.partial(wide_grad_kernel, rows, cols),
        out_shape=(
            shaped((rows, 2 * len(USED) * few, piece), bf16),
            shaped((rois, hidden), bf16),
            shaped((cols, 8, LANES), f32),
        ),
        in_specs=[VMEM] * 7,
        out_specs=(ANY, VMEM, VMEM),
        scratch_shapes=[
            pltpu.VMEM((rois, piece), bf16),
            pltpu.VMEM((2, rows, 4 * few, piece), bf16),
            pltpu.VMEM((rows, owned + per, piece), bf16),
            pltpu.VMEM((cols, rows, per, LANES), bf16),
            pltpu.VMEM((cols - 1, rows, per, LANES), bf16),
            pltpu.SemaphoreType.DMA((2 + len(SPARES),)),
            pltpu.SemaphoreType.DMA((12,)),
            pltpu.SemaphoreType.DMA((12,)),
        ],
        compiler_params=comm_params(3),
        name="wide_grads",
    )(pooled, g6_all, g7, hid6, hid7, gs, losses)


def pool_grads(g6_all, g7_all, losses_all, centred, weight, stats, pieces, rows, cols, pixels):
    rois, hidden = g6_all.shape
    channels = LANES // 2
    bf16, f32 = jnp.bfloat16, jnp.float32
    return pl.pallas_call(
        functools.partial(pool_grad_kernel, rows, cols, pixels),
        out_shape=(
            shaped((rois, WIDE), bf16),
            shaped((16, LANES), f32),
            shaped((channels, LANES), f32),
            shaped((channels, LANES), f32),
        ),
        in_specs=[VMEM] * 6 + [ANY],
        out_specs=(VMEM,) * 4,
        scratch_shapes=[
            pltpu.VMEM((2 * len(USED), channels, hidden), bf16),
            pltpu.VMEM((rows, 16, LANES), f32),
            pltpu.SemaphoreType.DMA((rows, 8)),
            pltpu.SemaphoreType.DMA((rows - 1,)),
            pltpu.SemaphoreType.DMA((rows - 1,)),
        ],
        compiler_params=comm_params(4),
        name="pool_grads",
    )(g6_all, g7_all, losses_all, centred, weight, stats, pieces)


def restore(term, few):
    return pl.pallas_call(
        functools.partial(restore_kernel, few),
        out_shape=shaped((49 * few, term.shape[1]), jnp.float32),
        in_specs=[VMEM],
        out_specs=VMEM,
        scratch_shapes=[pltpu.VMEM((term.shape[1] // LANES, 49 * few, LANES), jnp.float32)],
        compiler_params=pltpu.CompilerParams(vmem_limit_bytes=LIMIT),
        name="restore",
    )(term)


def targets_of(mine_boxes, mine_goals):
    prop_width = mine_boxes[2] - mine_boxes[0]
    prop_height = mine_boxes[3] - mine_boxes[1]
    prop_cx = mine_boxes[0] + 0.5 * prop_width
    prop_cy = mine_boxes[1] + 0.5 * prop_height
    goal_width = mine_goals[2] - mine_goals[0]
    goal_height = mine_goals[3] - mine_goals[1]
    goal_cx = mine_goals[0] + 0.5 * goal_width
    goal_cy = mine_goals[1] + 0.5 * goal_height
    return jnp.stack(
        [
            10.0 * (goal_cx - prop_cx) / prop_width,
            10.0 * (goal_cy - prop_cy) / prop_height,
            5.0 * jnp.log(goal_width / prop_width),
            5.0 * jnp.log(goal_height / prop_height),
        ],
        axis=1,
    )


def decode(mine_boxes, deltas):
    prop_width = mine_boxes[2] - mine_boxes[0]
    prop_height = mine_boxes[3] - mine_boxes[1]
    prop_cx = mine_boxes[0] + 0.5 * prop_width
    prop_cy = mine_boxes[1] + 0.5 * prop_height
    centre_x = prop_cx + deltas[:, 0] / 10.0 * prop_width
    centre_y = prop_cy + deltas[:, 1] / 10.0 * prop_height
    new_width = prop_width * jnp.exp(deltas[:, 2] / 5.0)
    new_height = prop_height * jnp.exp(deltas[:, 3] / 5.0)
    return jnp.stack(
        [
            centre_x - 0.5 * new_width,
            centre_y - 0.5 * new_height,
            centre_x + 0.5 * new_width,
            centre_y + 0.5 * new_height,
        ]
    ) / (CANVAS // 2)


def local_near(
    p2, p3, p4, p5, norm_gain, norm_bias, fc6_weight, fc6_bias, fc7_weight, fc7_bias,
    cls_weight, cls_bias, box_weight, box_bias, roi_boxes, roi_level, roi_image,
    canvas_offsets, labels, target_boxes, valid,
):
    channels = p2.shape[1]
    rois = roi_level.shape[0]
    cols = lax.axis_size("col")
    rows = lax.axis_size("roi")
    piece = fc6_bias.shape[0]
    high = rows // cols
    few = channels // high
    planes = (p2, p3, p4, p5)
    pixels = rows * sum(plane.shape[2] for plane in planes)
    ring = ring_of(rows)
    per = fc7_bias.shape[0]
    classes, boxes = cls_weight.shape[1], box_weight.shape[1]
    bf16, f32 = jnp.bfloat16, jnp.float32

    block = fc6_weight.reshape(few, 7, 7, piece)
    block = jnp.pad(block, ((0, 0), (0, 0), (0, 1), (0, 0))).reshape(few, 7, 2, 4, piece)
    block = block.transpose(3, 1, 2, 0, 4).reshape(2 * len(USED), few, piece)
    block = jnp.concatenate([block[:LEADING], block[LEADING::2]])
    pairs = []
    for kappa in range(cols):
        for block_at in range(cols):
            for half in range(high):
                plane = (2 * (block_at % 2) + block_at // 2 + kappa) % cols
                source = (kappa * high + half) * cols + block_at
                pairs.append((source, (plane * high + half) * cols + kappa))
    block = lax.ppermute(block, ("roi", "col"), pairs)

    head = jnp.concatenate([cls_weight, box_weight, fc7_bias[:, None]], axis=1)
    head = jnp.pad(head, ((0, 0), (0, piece - head.shape[1])))
    bias_high = fc6_bias.astype(bf16)
    rest = fc6_bias - bias_high.astype(f32)
    bias_mid = rest.astype(bf16)
    bias_low = (rest - bias_mid.astype(f32)).astype(bf16)
    bias = jnp.concatenate([item.reshape(2, LANES) for item in (bias_high, bias_mid, bias_low)])
    bias = jnp.pad(bias, ((0, per - bias.shape[0]), (0, 0)))
    head = jnp.concatenate([head[:, :LANES], bias], axis=1)
    small = jnp.concatenate([fc7_weight, head], axis=0).reshape(SMALL, few, piece)

    def twice(vector):
        return jnp.concatenate([vector, vector])[None]

    count = jnp.sum(valid.astype(f32))
    norm_facts = jnp.concatenate(
        [twice(norm_gain), jnp.full((1, LANES), count), jnp.zeros((6, LANES), f32)]
    )
    stats = statistics(norm_facts, planes, rows, float(pixels))
    valid_total = stats[3, 0]

    picks = roi_image[None, :] == jnp.arange(4, dtype=jnp.int32)[:, None]
    shift_x = jnp.sum(jnp.where(picks, canvas_offsets[0][:, None], 0), axis=0)
    shift_y = jnp.sum(jnp.where(picks, canvas_offsets[1][:, None], 0), axis=0)
    floats, ints, order = region_tables(
        (roi_boxes[0] + shift_x).astype(f32),
        (roi_boxes[1] + shift_y).astype(f32),
        (roi_boxes[2] + shift_x).astype(f32),
        (roi_boxes[3] + shift_y).astype(f32),
        roi_level,
    )
    block = lax.optimization_barrier((block, stats, floats, order))[0]
    pieces = lax.all_gather(block, "roi", axis=0, axis_index_groups=[ring])
    pooled, centred, weight = pool_maps(
        floats, ints, order, stats[:1], stats[1:2], twice(norm_bias), planes, rois
    )
    small = gather_small(lax.optimization_barrier((small, pooled))[0], rows, cols)

    quarter = rois // cols
    first_row = lax.axis_index("col") * quarter
    mine_labels = lax.dynamic_slice_in_dim(labels, first_row, quarter)
    mine_valid = lax.dynamic_slice_in_dim(valid, first_row, quarter).astype(f32)
    mine_boxes = lax.dynamic_slice_in_dim(roi_boxes, first_row, quarter, axis=1).astype(f32)
    mine_goals = lax.dynamic_slice_in_dim(target_boxes, first_row, quarter, axis=1).astype(f32)
    foreground = mine_valid * (mine_labels > 0).astype(f32)
    loss_scale = rois * rows / valid_total
    lane = jnp.arange(LANES, dtype=jnp.int32)[None, :]
    after = LANES - classes - boxes
    facts = jnp.stack(
        [
            jnp.pad(targets_of(mine_boxes, mine_goals), ((0, 0), (classes, after))),
            (mine_labels[:, None] == lane).astype(f32),
            loss_scale
            * jnp.where(
                lane < classes,
                mine_valid[:, None],
                jnp.where(lane < classes + boxes, foreground[:, None], 0.0),
            ),
        ]
    )
    score_bias = jnp.pad(jnp.concatenate([cls_bias, box_bias]), (0, after))[None]
    g6_all, g7, hid6, hid7, gs, scores, losses = run_head(
        pooled, facts, score_bias, small, pieces, rows, cols, classes, boxes
    )
    decoded = decode(mine_boxes, scores[:, classes : classes + boxes])

    terms, g7_all, losses_all = wide_grads(
        pooled, g6_all, g7, hid6, hid7, gs, losses, rows, cols
    )
    wide_rows = terms.shape[1]
    term = lax.psum_scatter(
        terms.reshape(rows * wide_rows, piece), "roi", scatter_dimension=0, tiled=True,
        axis_index_groups=[ring],
    )
    grads, totals, base, slope = pool_grads(
        g6_all, g7_all, losses_all, centred, weight, stats, pieces, rows, cols,
        float(pixels),
    )
    input_grads = unpool_maps(floats, ints, order, base, slope, grads, planes, rois)
    term = lax.optimization_barrier((term, input_grads[3]))[0]
    back = lax.ppermute(term, ("roi", "col"), [(there, here) for here, there in pairs])
    fc6_weight_grad = restore(back, few)
    extra = [
        term[SPARES[at] * few : (SPARES[at] + 1) * few].astype(f32)
        for at in range((fc7_weight.shape[0] + per) // few)
    ]
    fc7_weight_grad = jnp.concatenate(extra[:-1], axis=0)
    cls_weight_grad = extra[-1][:, :classes]
    box_weight_grad = extra[-1][:, classes : classes + boxes]

    fc6_bias_grad = totals[1 : 1 + piece // LANES].reshape(-1)
    seven = totals[1 + piece // LANES :][: cols * piece // LANES].reshape(-1)
    place = (lax.axis_index("roi") * cols + lax.axis_index("col")) * per
    fc7_bias_grad = lax.dynamic_slice_in_dim(seven, place, per)
    line = 1 + (cols + 1) * piece // LANES
    return (
        totals[line + 1, 0] / (rois * rows),
        jnp.sum(totals[line + 2]) / (rois * rows),
        decoded,
        *input_grads,
        totals[15, :channels],
        totals[0, channels:],
        fc6_weight_grad,
        fc6_bias_grad,
        fc7_weight_grad,
        fc7_bias_grad,
        cls_weight_grad,
        totals[line, :classes],
        box_weight_grad,
        totals[line, classes : classes + boxes],
    )


def solution(mesh):
    near = mesh.shape["roi"] == 2 * mesh.shape["col"] and mesh.shape["col"] == 4
    return jax.shard_map(
        local_near if near else local,
        mesh=mesh,
        in_specs=(
            P("roi", "col", None),
            P("roi", "col", None),
            P("roi", "col", None),
            P("roi", "col", None),
            P("col"),
            P("col"),
            P("roi", "col"),
            P("col"),
            P("roi", "col"),
            P(("roi", "col")),
            P(("roi", "col"), None),
            P(),
            P(("roi", "col"), None),
            P(),
            P(None, "roi"),
            P("roi"),
            P("roi"),
            P(None, "roi"),
            P("roi"),
            P(None, "roi"),
            P("roi"),
        ),
        out_specs=(
            P(),
            P(),
            P(None, ("roi", "col")),
            P("roi", "col", None),
            P("roi", "col", None),
            P("roi", "col", None),
            P("roi", "col", None),
            P("col"),
            P("col"),
            P("roi", "col"),
            P("col"),
            P("roi", "col"),
            P(("roi", "col")),
            P(("roi", "col"), None),
            P(),
            P(("roi", "col"), None),
            P(),
        ),
        check_vma=False,
    )
```

```python
import functools
import math

import jax
import jax.numpy as jnp
from jax import lax
from jax.experimental import pallas as pl
from jax.experimental.pallas import tpu as pltpu
from jax.sharding import PartitionSpec as P

CANVAS = 1024
EPSILON = 1e-05
LANES = 128
SPAN = 10
NARROW = 8
GROUP = 16
MORE = 8
SPARE = 8
SIDES = tuple(CANVAS // (4 * 2**level) for level in range(4))
TILES = tuple(side * side // LANES for side in SIDES)
FIRST = tuple(sum(TILES[:level]) for level in range(4))
ALL_TILES = sum(TILES)
PADDED = ALL_TILES + max(SPAN - min(TILES), 0)
SLOTS = 32
USED = tuple(slot for slot in range(SLOTS) if slot % 8 < 7)
WIDE = len(USED) * LANES
F32_FIELDS = 7
I32_FIELDS = 6


def silu_slope(values):
    sigma = jax.nn.sigmoid(values)
    return sigma * (1.0 + values * (1.0 - sigma))


def contract_first(left_m, right_m):
    return lax.dot_general(
        left_m, right_m, (((0,), (0,)), ((), ())), preferred_element_type=jnp.float32
    )


def contract_last(left_m, right_m):
    return lax.dot_general(
        left_m, right_m, (((1,), (1,)), ((), ())), preferred_element_type=jnp.float32
    )


def region_tables(left, top, right, bottom, level):
    def by_level(values):
        chosen = jnp.full(level.shape, values[0])
        for at in range(1, 4):
            chosen = jnp.where(level == at, values[at], chosen)
        return chosen

    step = by_level([4.0 * 2**at for at in range(4)])
    side = by_level(list(SIDES))
    rows_log = by_level([(max(LANES // n, 1)).bit_length() - 1 for n in SIDES])
    across = by_level([max(n // LANES, 1) for n in SIDES])
    x_anchor, x_extent = left / step - 0.5, (right - left) / step
    y_anchor, y_extent = top / step - 0.5, (bottom - top) / step

    def window(anchor, extent):
        low = jnp.floor(anchor + extent * (0.5 / 14.0)).astype(jnp.int32)
        high = jnp.floor(anchor + extent * (13.5 / 14.0)).astype(jnp.int32) + 1
        return jnp.clip(low, 0, side - 1), jnp.clip(high, 0, side - 1)

    y_low, y_high = window(y_anchor, y_extent)
    x_low, x_high = window(x_anchor, x_extent)
    group_low, group_high = y_low >> rows_log, y_high >> rows_log
    tile_x = x_low // LANES
    tiles_x = x_high // LANES - tile_x + 1
    narrow = (group_high - group_low < NARROW) & (tiles_x == 1)
    chunks = jnp.where(narrow, 1, (group_high - group_low + SPAN) // SPAN)
    taken = jnp.where(narrow, NARROW, chunks * SPAN)
    group = jnp.maximum(jnp.minimum(group_low, (side >> rows_log) - taken), 0)
    first_tile = by_level(list(FIRST)) + group * across + tile_x
    mask = jnp.minimum(side, LANES) - 1
    shift = 7 - rows_log
    rows_per = (1 << rows_log).astype(jnp.float32)
    nothing = jnp.zeros((SPARE,), jnp.int32)
    parts = chunks * tiles_x
    kind = jnp.where(narrow, 0, jnp.where(parts > 1, 2, 1))
    key = jnp.where(level > 0, 3 + kind, 2 - kind)
    rois = level.shape[0]
    at = jnp.arange(rois, dtype=jnp.int32)
    before = (key[None, :] < key[:, None]) | (
        (key[None, :] == key[:, None]) & (at[None, :] < at[:, None])
    )
    rank = jnp.sum(before.astype(jnp.int32), axis=1)
    order = jnp.sum(jnp.where(rank[None, :] == at[:, None], at[None, :], 0), axis=1)
    order = jnp.concatenate([order, jnp.full((GROUP,), rois, jnp.int32)])
    ends = jnp.stack([jnp.sum((key <= last).astype(jnp.int32)) for last in range(6)])
    floats = jnp.stack(
        [
            x_anchor,
            x_extent,
            y_anchor,
            y_extent,
            (tile_x * LANES).astype(jnp.float32),
            group.astype(jnp.float32) * rows_per,
            rows_per,
        ]
    ).astype(jnp.float32)
    ints = jnp.stack([first_tile, across, mask, shift, parts, tiles_x]).astype(jnp.int32)
    away = jnp.full((F32_FIELDS, SPARE), -1e6, jnp.float32)
    floats = jnp.concatenate([floats, away], axis=1)
    ints = jnp.concatenate([ints, jnp.broadcast_to(nothing, (I32_FIELDS, SPARE))], axis=1)
    return floats.reshape(-1), ints.reshape(-1), jnp.concatenate([order, ends])


def window_weights(floats, ints, rois, region, chunk, tile_x, span=SPAN):
    rois = rois + SPARE
    x_anchor, x_extent, y_anchor, y_extent, x_origin, y_origin, rows_per = (
        floats[at * rois + region] for at in range(F32_FIELDS)
    )
    first_tile, across, mask, shift = (ints[at * rois + region] for at in range(4))
    if chunk is not None:
        first_tile = first_tile + chunk * (SPAN * across) + tile_x
        x_origin = x_origin + (tile_x * LANES).astype(jnp.float32)
        y_origin = y_origin + (chunk * SPAN).astype(jnp.float32) * rows_per
    lane = lax.broadcasted_iota(jnp.int32, (8, LANES), 1)
    bin_at = lax.broadcasted_iota(jnp.int32, (8, LANES), 0)
    x_cell = (lane & mask).astype(jnp.float32) + x_origin
    y_cell = lax.shift_right_logical(lane, jnp.broadcast_to(shift, lane.shape)).astype(
        jnp.float32
    ) + y_origin
    part = jnp.where(bin_at < 7, (2.0 * bin_at.astype(jnp.float32) + 0.5) / 14.0, -1e6)
    near = y_anchor + y_extent * part - y_cell
    far = y_anchor + y_extent * (part + 1.0 / 14.0) - y_cell

    def tent(distance):
        return jnp.maximum(1.0 - jnp.abs(distance), 0.0)

    across_w = []
    for j in range(7):
        one = x_anchor + x_extent * ((2 * j + 0.5) / 14.0)
        two = x_anchor + x_extent * ((2 * j + 1.5) / 14.0)
        across_w.append(0.25 * (tent(one - x_cell) + tent(two - x_cell)))
    across_w.append(jnp.zeros((8, LANES), jnp.float32))
    packed = [
        jnp.concatenate([across_w[2 * at], across_w[2 * at + 1]], axis=0).astype(jnp.bfloat16)
        for at in range(4)
    ]
    blocks = []
    for at in range(span):
        offset = rows_per * float(at)
        down = tent(near - offset) + tent(far - offset)
        both = jnp.concatenate([down, down], axis=0).astype(jnp.bfloat16)
        blocks.append(jnp.concatenate([both * item for item in packed], axis=0))
    return jnp.concatenate(blocks, axis=1), first_tile, across


def tile_lanes(first_tile, across, at):
    return pl.ds(pl.multiple_of((first_tile + at * across) * LANES, LANES), LANES)


def for_groups(order, start, stop, size, body):
    def step(at, carry):
        first = start + at * size
        inside = [first + index < stop for index in range(size)]
        spare = order.shape[0] - 7
        places = [
            jnp.where(good, first + index, spare) for index, good in enumerate(inside)
        ]
        body([order[place] for place in places])
        return carry

    lax.fori_loop(0, (stop - start + size - 1) // size, step, 0)


def for_parts(ints, order, rois, start, stop, size, body):
    stride = rois + SPARE

    def second(regions):
        for region in regions:
            tiles_x = ints[5 * stride + region]
            wide = (tiles_x > 1).astype(jnp.int32)
            body(region, 1 - wide, wide)

    for_groups(order, start, stop, size, second)

    def later(at, carry):
        region = order[at]
        tiles_x = ints[5 * stride + region]

        def part(index, inner):
            chunk = index // tiles_x
            body(region, chunk, index - chunk * tiles_x)
            return inner

        return lax.fori_loop(2, ints[4 * stride + region], part, carry)

    lax.fori_loop(start, stop, later, 0)


def ends_of(order):
    size = order.shape[0]
    return [order[size - 6 + at] for at in range(6)]


def pool_kernel(
    rois, floats, ints, order, stats, shift, p2, p3, p4, p5,
    pooled_out, centred_out, weight_out, maps, values, sems,
):
    channels = stats.shape[1] // 2
    stride = rois + SPARE
    copies = []
    for level, plane in enumerate((p2, p3, p4, p5)):
        cells = TILES[level] * LANES
        copies.append(
            pltpu.make_async_copy(
                plane.at[0],
                maps.at[pl.ds(0, channels), pl.ds(FIRST[level] * LANES, cells)],
                sems.at[level],
            )
        )
        copies[-1].start()
    ones = jnp.ones((16, 8 * LANES), jnp.bfloat16)

    def fill(at, carry):
        lanes = pl.ds(pl.multiple_of(at * 8 * LANES, 8 * LANES), 8 * LANES)
        maps[pl.ds(channels, 16), lanes] = ones
        return carry

    lax.fori_loop(0, ALL_TILES // 8, fill, 0)
    extra = PADDED - ALL_TILES
    if extra:
        maps[:, pl.ds(ALL_TILES * LANES, extra * LANES)] = jnp.zeros(
            (channels + 16, extra * LANES), jnp.bfloat16
        )
    for copy in copies:
        copy.wait()

    def item(region, chunk, tile_x, span=SPAN):
        kernel_w, first_tile, across = window_weights(
            floats, ints, rois, region, chunk, tile_x, span
        )
        cells = jnp.concatenate(
            [maps[:, tile_lanes(first_tile, across, at)] for at in range(span)], axis=1
        )
        return contract_last(kernel_w, cells)

    def place(region):
        return pl.ds(region, 2 * SLOTS, stride=stride)

    def narrow(regions):
        for region in regions:
            values[place(region), : channels + 16] = item(region, None, None, NARROW)

    def first(regions):
        for region in regions:
            values[place(region), : channels + 16] = item(region, None, None)

    def further(region, chunk, tile_x):
        values[place(region), : channels + 16] = values[place(region), : channels + 16] + item(region, chunk, tile_x)

    ends = ends_of(order)
    for_groups(order, 0, ends[1], MORE, first)
    for_groups(order, ends[1], ends[3], GROUP, narrow)
    for_groups(order, ends[3], ends[5], MORE, first)
    for_parts(ints, order, rois, 0, ends[0], MORE, further)
    for_parts(ints, order, rois, ends[4], ends[5], MORE, further)
    low_lane = lax.broadcasted_iota(jnp.int32, (rois, LANES), 1) < channels
    for at, slot in enumerate(USED):
        lanes = pl.ds(at * LANES, LANES)
        one = values[pl.ds(slot * stride, rois), :]
        two = values[pl.ds((slot + SLOTS) * stride, rois), :]
        value = jnp.where(low_lane, one, pltpu.roll(two, channels, 1))
        total = jnp.where(low_lane, one[:, channels : channels + 1], two[:, channels : channels + 1])
        centred = value - stats[:1] * total
        centred_out[:, lanes] = centred.astype(jnp.bfloat16)
        weight_out[:, lanes] = total.astype(jnp.bfloat16)
        pooled_out[:, lanes] = (centred * stats[1:2] + shift[...] * total).astype(jnp.bfloat16)


def unpool_kernel(
    rois, floats, ints, order, base, slope, grads, p2, p3, p4, p5,
    o2, o3, o4, o5, maps, sums, slots, sems, out_sems, finish=None,
):
    channels = base.shape[0]
    stride = rois + SPARE
    planes, outs = (p2, p3, p4, p5), (o2, o3, o4, o5)
    pieces = [(level, at) for level in range(4) for at in range(4 if level == 0 else 1)]

    def fetch(index):
        level, at = pieces[index]
        cells = TILES[level] * LANES // (4 if level == 0 else 1)
        return pltpu.make_async_copy(
            planes[level].at[0, :, pl.ds(at * cells, cells)],
            maps.at[:, pl.ds(FIRST[level] * LANES + at * cells, cells)],
            sems.at[index],
        )

    for index in range(len(pieces)):
        fetch(index).start()
    for slot in range(SLOTS):
        rows = pl.ds(slot * stride, rois)
        slots[pl.ds(slot * stride + rois, SPARE), :] = jnp.zeros((SPARE, LANES), jnp.float32)
        if slot in USED:
            lanes = pl.ds(USED.index(slot) * LANES, LANES)
            slots[rows, :] = grads[:, lanes].astype(jnp.float32)
        else:
            slots[rows, :] = jnp.zeros((rois, LANES), jnp.float32)
    base_v, slope_v = base[...], slope[...]

    def begin(at, carry):
        for part in range(4):
            lanes = pl.ds(pl.multiple_of((at * 4 + part) * LANES, LANES), LANES)
            sums[:, lanes] = base_v + slope_v * maps[:, lanes].astype(jnp.float32)
        return carry

    for index, (level, at) in enumerate(pieces):
        tiles = TILES[level] // (4 if level == 0 else 1)
        start = FIRST[level] + at * tiles
        fetch(index).wait()
        lax.fori_loop(start // 4, (start + tiles) // 4, begin, 0)
    extra = PADDED - ALL_TILES
    if extra:
        sums[:, pl.ds(ALL_TILES * LANES, extra * LANES)] = jnp.zeros(
            (channels, extra * LANES), jnp.float32
        )

    def item(region, chunk, tile_x, span=SPAN):
        kernel_w, first_tile, across = window_weights(
            floats, ints, rois, region, chunk, tile_x, span
        )
        mine = slots[pl.ds(region, SLOTS, stride=stride), :]
        stacked = jnp.concatenate([mine[:, :channels], mine[:, channels:]], axis=0)
        turned = stacked.T.astype(jnp.bfloat16)
        result = jnp.dot(turned, kernel_w, preferred_element_type=jnp.float32)
        for at in range(span):
            lanes = tile_lanes(first_tile, across, at)
            sums[:, lanes] = sums[:, lanes] + result[:, at * LANES : (at + 1) * LANES]

    def narrow(regions):
        for region in regions:
            item(region, None, None, NARROW)

    def first(regions):
        for region in regions:
            item(region, None, None)

    def send(level):
        cells = TILES[level] * LANES
        return pltpu.make_async_copy(
            sums.at[:, pl.ds(FIRST[level] * LANES, cells)], outs[level].at[0], out_sems.at[level]
        )

    ends = ends_of(order)
    for_groups(order, 0, ends[1], MORE, first)
    for_groups(order, ends[1], ends[2], GROUP, narrow)
    for_parts(ints, order, rois, 0, ends[0], MORE, item)
    send(0).start()
    if finish is not None:
        finish()
    for_groups(order, ends[2], ends[3], GROUP, narrow)
    for_groups(order, ends[3], ends[5], MORE, first)
    for_parts(ints, order, rois, ends[4], ends[5], MORE, item)
    for level in range(1, 4):
        send(level).start()
    for level in range(4):
        send(level).wait()


ANY = pl.BlockSpec(memory_space=pl.ANY)
SMEM = pl.BlockSpec(memory_space=pltpu.SMEM)
VMEM = pl.BlockSpec(memory_space=pltpu.VMEM)
LIMIT = 60 * 1024 * 1024


def pool_maps(floats, ints, order, stats, shift, planes, rois):
    channels = planes[0].shape[1]
    flat = jax.ShapeDtypeStruct((rois, WIDE), jnp.bfloat16)
    return pl.pallas_call(
        functools.partial(pool_kernel, rois),
        out_shape=(flat, flat, flat),
        in_specs=[SMEM, SMEM, SMEM, VMEM, VMEM, ANY, ANY, ANY, ANY],
        out_specs=(VMEM, VMEM, VMEM),
        scratch_shapes=[
            pltpu.VMEM((channels + 16, PADDED * LANES), jnp.bfloat16),
            pltpu.VMEM((2 * SLOTS * (rois + SPARE), LANES), jnp.float32),
            pltpu.SemaphoreType.DMA((4,)),
        ],
        compiler_params=pltpu.CompilerParams(vmem_limit_bytes=LIMIT),
        name="pool",
    )(floats, ints, order, stats, shift, *planes)


def unpool_maps(floats, ints, order, base, slope, grads, planes, rois):
    channels = planes[0].shape[1]
    return pl.pallas_call(
        functools.partial(unpool_kernel, rois),
        out_shape=tuple(jax.ShapeDtypeStruct(plane.shape, jnp.float32) for plane in planes),
        in_specs=[SMEM, SMEM, SMEM, VMEM, VMEM, VMEM, ANY, ANY, ANY, ANY],
        out_specs=(ANY, ANY, ANY, ANY),
        scratch_shapes=[
            pltpu.VMEM((channels, ALL_TILES * LANES), jnp.bfloat16),
            pltpu.VMEM((channels, PADDED * LANES), jnp.float32),
            pltpu.VMEM((SLOTS * (rois + SPARE), LANES), jnp.float32),
            pltpu.SemaphoreType.DMA((7,)),
            pltpu.SemaphoreType.DMA((4,)),
        ],
        compiler_params=pltpu.CompilerParams(vmem_limit_bytes=LIMIT),
        name="unpool",
    )(floats, ints, order, base, slope, grads, *planes)


def local(
    p2, p3, p4, p5, norm_gain, norm_bias, fc6_weight, fc6_bias, fc7_weight, fc7_bias,
    cls_weight, cls_bias, box_weight, box_bias, roi_boxes, roi_level, roi_image,
    canvas_offsets, labels, target_boxes, valid,
):
    channels = p2.shape[1]
    rois = roi_level.shape[0]
    cols = lax.axis_size("col")
    rows = lax.axis_size("roi")
    hidden = fc6_bias.shape[0] * cols
    piece = fc6_bias.shape[0]
    high = rows // cols
    few = channels // high
    planes = (p2, p3, p4, p5)

    block = fc6_weight.reshape(few, 7, 7, piece)
    block = jnp.pad(block, ((0, 0), (0, 0), (0, 1), (0, 0))).reshape(few, 7, 2, 4, piece)
    block = block.transpose(3, 1, 2, 0, 4).reshape(len(USED) * 2, few, piece)
    pairs = [
        ((kappa * high + rho // cols) * cols + rho % cols, rho * cols + kappa)
        for rho in range(rows)
        for kappa in range(cols)
    ]
    block = lax.ppermute(block, ("roi", "col"), pairs)
    wide = lax.all_gather(block, "roi", axis=0)
    wide = wide.reshape(high, cols, len(USED) * 2, few, piece)
    wide = wide.transpose(2, 0, 3, 1, 4).reshape(WIDE, hidden)

    per = fc7_bias.shape[0]
    classes, boxes = cls_weight.shape[1], box_weight.shape[1]
    head = jnp.concatenate([cls_weight, box_weight, fc7_bias[:, None]], axis=1)
    head = jnp.pad(head, ((0, 0), (0, piece - head.shape[1])))
    bias_high = fc6_bias.astype(jnp.bfloat16)
    rest = fc6_bias - bias_high.astype(jnp.float32)
    bias_mid = rest.astype(jnp.bfloat16)
    bias_low = (rest - bias_mid.astype(jnp.float32)).astype(jnp.bfloat16)
    small = jnp.concatenate(
        [fc7_weight, head, jnp.stack([bias_high, bias_mid, bias_low])], axis=0
    )
    deep_rows = fc7_weight.shape[0]
    small = jnp.pad(small, ((0, -small.shape[0] % 16), (0, 0)))
    small = lax.all_gather(small, ("roi", "col"), axis=0)
    deep = small[:, :deep_rows].reshape(rows, cols, deep_rows, piece)
    deep = deep.transpose(0, 2, 1, 3).reshape(hidden, hidden)
    head = small[:, deep_rows : deep_rows + per].reshape(hidden, piece)[:, :LANES]
    bias_seven = head[:, classes + boxes].astype(jnp.float32)
    bias_six = small[:cols, deep_rows + per : deep_rows + per + 3].astype(jnp.float32)
    bias_six = jnp.sum(bias_six, axis=1).reshape(hidden)

    values = [plane[0].astype(jnp.float32) for plane in planes]
    pixel_total = rows * sum(plane.shape[1] for plane in values)
    first_sum = sum(jnp.sum(plane, axis=1) for plane in values)
    second_sum = sum(jnp.sum(plane * plane, axis=1) for plane in values)
    local_valid = jnp.sum(valid.astype(jnp.float32))
    first_sum, second_sum, valid_total = lax.psum((first_sum, second_sum, local_valid), "roi")
    mean = first_sum / pixel_total
    variance = second_sum / pixel_total - mean * mean
    inv_std = lax.rsqrt(variance + EPSILON)
    scale = norm_gain * inv_std

    picks = roi_image[None, :] == jnp.arange(4, dtype=jnp.int32)[:, None]
    shift_x = jnp.sum(jnp.where(picks, canvas_offsets[0][:, None], 0), axis=0)
    shift_y = jnp.sum(jnp.where(picks, canvas_offsets[1][:, None], 0), axis=0)
    floats, ints, order = region_tables(
        (roi_boxes[0] + shift_x).astype(jnp.float32),
        (roi_boxes[1] + shift_y).astype(jnp.float32),
        (roi_boxes[2] + shift_x).astype(jnp.float32),
        (roi_boxes[3] + shift_y).astype(jnp.float32),
        roi_level,
    )

    def twice(vector):
        return jnp.concatenate([vector, vector])[None]

    pooled, centred, weight = pool_maps(
        floats, ints, order,
        jnp.concatenate([twice(mean), twice(scale), jnp.zeros((6, LANES), jnp.float32)]),
        twice(norm_bias), planes, rois
    )

    partial_six = jnp.dot(pooled, wide, preferred_element_type=jnp.float32).astype(jnp.bfloat16)
    pre_six = lax.psum_scatter(partial_six, "col", scatter_dimension=0, tiled=True)
    pre_six = pre_six.astype(jnp.float32) + bias_six
    hidden_six = jax.nn.silu(pre_six).astype(jnp.bfloat16)
    pre_seven = contract_last(hidden_six, deep) + bias_seven
    hidden_seven = jax.nn.silu(pre_seven).astype(jnp.bfloat16)
    scores = jnp.dot(hidden_seven, head, preferred_element_type=jnp.float32)
    logits = scores[:, :classes] + cls_bias
    deltas = scores[:, classes : classes + boxes] + box_bias

    quarter = rois // cols
    first_row = lax.axis_index("col") * quarter
    mine_labels = lax.dynamic_slice_in_dim(labels, first_row, quarter)
    mine_valid = lax.dynamic_slice_in_dim(valid, first_row, quarter).astype(jnp.float32)
    mine_boxes = lax.dynamic_slice_in_dim(roi_boxes, first_row, quarter, axis=1).astype(jnp.float32)
    mine_goals = lax.dynamic_slice_in_dim(target_boxes, first_row, quarter, axis=1).astype(
        jnp.float32
    )
    prop_width = mine_boxes[2] - mine_boxes[0]
    prop_height = mine_boxes[3] - mine_boxes[1]
    prop_cx = mine_boxes[0] + 0.5 * prop_width
    prop_cy = mine_boxes[1] + 0.5 * prop_height
    goal_width = mine_goals[2] - mine_goals[0]
    goal_height = mine_goals[3] - mine_goals[1]
    goal_cx = mine_goals[0] + 0.5 * goal_width
    goal_cy = mine_goals[1] + 0.5 * goal_height
    targets = jnp.stack(
        [
            10.0 * (goal_cx - prop_cx) / prop_width,
            10.0 * (goal_cy - prop_cy) / prop_height,
            5.0 * jnp.log(goal_width / prop_width),
            5.0 * jnp.log(goal_height / prop_height),
        ],
        axis=1,
    )
    foreground = mine_valid * (mine_labels > 0).astype(jnp.float32)
    top_logit = jnp.max(logits, axis=1, keepdims=True)
    log_total = top_logit[:, 0] + jnp.log(jnp.sum(jnp.exp(logits - top_logit), axis=1))
    onehot = (mine_labels[:, None] == jnp.arange(classes, dtype=jnp.int32)[None, :]).astype(
        jnp.float32
    )
    picked = jnp.sum(onehot * logits, axis=1)
    misfit = deltas - targets
    huber_terms = jnp.where(jnp.abs(misfit) < 1.0, 0.5 * misfit * misfit, jnp.abs(misfit) - 0.5)
    class_part = jnp.sum(mine_valid * (log_total - picked))
    box_part = jnp.sum(foreground * jnp.sum(huber_terms, axis=1))
    centre_x = prop_cx + deltas[:, 0] / 10.0 * prop_width
    centre_y = prop_cy + deltas[:, 1] / 10.0 * prop_height
    new_width = prop_width * jnp.exp(deltas[:, 2] / 5.0)
    new_height = prop_height * jnp.exp(deltas[:, 3] / 5.0)
    decoded = jnp.stack(
        [
            centre_x - 0.5 * new_width,
            centre_y - 0.5 * new_height,
            centre_x + 0.5 * new_width,
            centre_y + 0.5 * new_height,
        ]
    ) / (CANVAS // 2)
    loss_scale = rois * rows / valid_total
    softmax = jnp.exp(logits - log_total[:, None])
    logit_grads = loss_scale * mine_valid[:, None] * (softmax - onehot)
    delta_grads = loss_scale * foreground[:, None] * jnp.clip(misfit, -1.0, 1.0)
    score_grads = jnp.concatenate([logit_grads, delta_grads], axis=1)
    score_grads = jnp.pad(score_grads, ((0, 0), (0, LANES - score_grads.shape[1])))
    score_grads = score_grads.astype(jnp.bfloat16)

    head_term = contract_first(hidden_seven, score_grads)
    hidden_grads = contract_last(score_grads, head)
    pre_seven_grads = (hidden_grads * silu_slope(pre_seven)).astype(jnp.bfloat16)
    deep_term = contract_first(pre_seven_grads, hidden_six)
    six_hidden_grads = jnp.dot(pre_seven_grads, deep, preferred_element_type=jnp.float32)
    pre_six_grads = (six_hidden_grads * silu_slope(pre_six)).astype(jnp.bfloat16)
    six_grads_all = lax.all_gather(pre_six_grads, "col", axis=0, tiled=True)

    wide_term = contract_first(pooled, six_grads_all).astype(jnp.bfloat16)
    wide_term = wide_term.reshape(len(USED) * 2, high, few, cols, piece)
    wide_term = wide_term.transpose(1, 3, 0, 2, 4).reshape(rows * len(USED) * 2, few, piece)
    wide_grad = lax.psum_scatter(wide_term, "roi", scatter_dimension=0, tiled=True)
    wide_grad = lax.ppermute(wide_grad, ("roi", "col"), [(there, here) for here, there in pairs])
    wide_grad = wide_grad.reshape(4, 7, 2, few, piece).transpose(3, 1, 2, 0, 4)
    wide_grad = wide_grad.reshape(few, 7, 8, piece)[:, :, :7].reshape(few * 49, piece)
    fc6_weight_grad = wide_grad.astype(jnp.float32)

    sums = jnp.concatenate(
        [
            jnp.sum(score_grads.astype(jnp.float32), axis=0),
            jnp.stack([class_part, box_part]),
        ]
    )
    everyone = rows * cols
    deep_term = deep_term.reshape(rows, deep_rows, cols, piece).transpose(0, 2, 1, 3)
    deep_term = deep_term.reshape(everyone, deep_rows, piece)
    seven_bias_term = jnp.sum(pre_seven_grads.astype(jnp.float32), axis=0)
    head_term = jnp.concatenate(
        [head_term[:, : classes + boxes], seven_bias_term[:, None]], axis=1
    )
    head_term = jnp.pad(head_term, ((0, 0), (0, piece - head_term.shape[1])))
    head_term = head_term.reshape(everyone, per, piece)
    six_bias_term = jnp.sum(pre_six_grads.astype(jnp.float32), axis=0).reshape(cols, 1, piece)
    six_bias_term = jnp.broadcast_to(six_bias_term[None], (rows, cols, 1, piece))
    six_bias_term = six_bias_term.reshape(everyone, 1, piece)
    sums = jnp.pad(sums, (0, piece - sums.shape[0]))
    sums = jnp.broadcast_to(sums[None, None], (everyone, 1, piece))
    small_term = jnp.concatenate([deep_term, head_term, six_bias_term, sums], axis=1)
    small_term = jnp.pad(small_term, ((0, 0), (0, -small_term.shape[1] % 8), (0, 0)))
    small_grad = lax.psum_scatter(small_term, ("roi", "col"), scatter_dimension=0, tiled=True)[0]
    fc7_weight_grad = small_grad[:deep_rows]
    head_grad = small_grad[deep_rows : deep_rows + per]
    cls_weight_grad = head_grad[:, :classes]
    box_weight_grad = head_grad[:, classes : classes + boxes]
    fc7_bias_grad = head_grad[:, classes + boxes]
    fc6_bias_grad = small_grad[deep_rows + per]
    sums = small_grad[deep_rows + per + 1]
    class_bias_grad = sums[:classes]
    box_bias_grad = sums[classes : classes + boxes]
    cls_loss = sums[LANES] / valid_total
    box_loss = sums[LANES + 1] / valid_total

    pool_grads = contract_last(six_grads_all, wide)
    gain_part = jnp.sum(pool_grads * centred.astype(jnp.float32), axis=0)
    shift_part = jnp.sum(pool_grads * weight.astype(jnp.float32), axis=0)
    gain_part = jnp.sum(gain_part.reshape(-1, channels), axis=0) * inv_std
    shift_part = jnp.sum(shift_part.reshape(-1, channels), axis=0)
    norm_gain_grad, norm_bias_grad = lax.psum((gain_part, shift_part), "roi")

    scaled = (pool_grads * jnp.tile(scale, WIDE // channels)).astype(jnp.bfloat16)
    slope = -scale * inv_std * norm_gain_grad / pixel_total
    base = -scale * norm_bias_grad / pixel_total - slope * mean

    def spread(vector):
        return jnp.broadcast_to(vector[:, None], (channels, LANES))

    input_grads = unpool_maps(floats, ints, order, spread(base), spread(slope), scaled, planes, rois)
    return (
        cls_loss,
        box_loss,
        decoded,
        input_grads[0],
        input_grads[1],
        input_grads[2],
        input_grads[3],
        norm_gain_grad,
        norm_bias_grad,
        fc6_weight_grad,
        fc6_bias_grad,
        fc7_weight_grad,
        fc7_bias_grad,
        cls_weight_grad,
        class_bias_grad,
        box_weight_grad,
        box_bias_grad,
    )


MESH = pl.DeviceIdType.MESH
KEPT = tuple(at for at in range(2 * len(USED)) if at % 2 == 0 or at // 2 < 21)
LEADING = 42
SPARES = tuple(at for at in range(2 * len(USED)) if at not in KEPT)
SMALL = 5


def ring_of(rows):
    return list(range(0, rows, 2)) + list(range(rows - 1, 0, -2))


def position_of(kappa, rows, cols, block, half):
    plane = lax.rem(2 * (block % 2) + block // 2 + kappa, cols)
    return rows - 1 - plane if half else plane


def greet(axis, count):
    barrier = pltpu.get_barrier_semaphore()
    me = lax.axis_index(axis)
    for step in range(1, count):
        pl.semaphore_signal(
            barrier,
            inc=1,
            device_id={axis: lax.rem(me + step, count)},
            device_id_type=MESH,
        )


def met(count):
    pl.semaphore_wait(pltpu.get_barrier_semaphore(), count)


def remote(src, dst, sends, recvs, at, axis, peer):
    return pltpu.make_async_remote_copy(
        src_ref=src,
        dst_ref=dst,
        send_sem=sends.at[at],
        recv_sem=recvs.at[at],
        device_id={axis: peer},
        device_id_type=MESH,
    )


def share(slots, axis, count, sends, recvs, first=0):
    me = lax.axis_index(axis)
    copies = [
        remote(slots.at[me], slots.at[me], sends, recvs, first + step - 1, axis,
               lax.rem(me + step, count))
        for step in range(1, count)
    ]
    for copy in copies:
        copy.start()
    return copies


def neighbours(me):
    core, chip = lax.rem(me, 2), lax.div(me, 2)
    return me + 1 - 2 * core, me + 2 - 4 * chip


class Relay:
    def __init__(self, view, sends, recvs, first):
        me = lax.axis_index("col")
        core, chip = neighbours(me)
        self.near = remote(view(me), view(me), sends, recvs, first, "col", core)
        self.far = remote(view(me), view(me), sends, recvs, first + 1, "col", chip)
        self.passed = remote(view(chip), view(chip), sends, recvs, first + 2, "col", core)

    def start(self):
        self.far.start()
        self.near.start()

    def forward(self):
        self.far.wait_recv()
        self.passed.start()

    def wait(self):
        self.near.wait()
        self.far.wait_send()
        self.passed.wait()


def stats_kernel(
    rows, pixels, facts, small, p2, p3, p4, p5, out, small_out,
    maps, slots, sems, sends, recvs, small_sends, small_recvs,
):
    row = lax.axis_index("roi")
    depth = rows // 2
    plane, side = lax.div(row, 2), lax.rem(row, 2)
    channels = maps.shape[0]
    planes = (p2, p3, p4, p5)
    pieces = [(level, at) for level in range(4) for at in range(4 if level == 0 else 1)]
    greet("roi", rows)

    def fetch(index):
        level, at = pieces[index]
        cells = TILES[level] * LANES // (4 if level == 0 else 1)
        return pltpu.make_async_copy(
            planes[level].at[0, :, pl.ds(at * cells, cells)],
            maps.at[:, pl.ds(FIRST[level] * LANES + at * cells, cells)],
            sems.at[index],
        )

    for index in range(len(pieces)):
        fetch(index).start()
    small_out[row] = small[...]
    along = [
        remote(small, small_out.at[row], small_sends, small_recvs, step - 1, "roi",
               lax.rem(plane + step, depth) * 2 + side)
        for step in range(1, depth)
    ]
    across = []
    for step in range(depth):
        block = small_out.at[lax.rem(plane + depth - step, depth) * 2 + side]
        across.append(
            remote(block, block, small_sends, small_recvs, depth - 1 + step, "roi",
                   row + 1 - 2 * side)
        )
    met(rows - 1)
    for copy in along:
        copy.start()
    across[0].start()

    def add(at, carry):
        one, two = carry
        for part in range(4):
            lanes = pl.ds(pl.multiple_of((at * 4 + part) * LANES, LANES), LANES)
            value = maps[:, lanes].astype(jnp.float32)
            one, two = one + value, two + value * value
        return one, two

    carry = (jnp.zeros((channels, LANES), jnp.float32),) * 2
    for index, (level, at) in enumerate(pieces):
        tiles = TILES[level] // (4 if level == 0 else 1)
        start = FIRST[level] + at * tiles
        fetch(index).wait()
        carry = lax.fori_loop(start // 4, (start + tiles) // 4, add, carry)
    sums = [jnp.sum(item.T, axis=0, keepdims=True) for item in carry]
    slots[row] = jnp.concatenate(
        [jnp.concatenate(sums, axis=1), facts[1:2], jnp.zeros((6, LANES), jnp.float32)], axis=0
    )
    copies = share(slots, "roi", rows, sends, recvs)
    for step in range(1, depth):
        along[step - 1].wait_recv()
        across[step].start()
    for copy in copies:
        copy.wait()
    total = slots[0]
    for at in range(1, rows):
        total = total + slots[at]
    turned = pltpu.roll(total, channels, 1)
    low = lax.broadcasted_iota(jnp.int32, total.shape, 1) < channels
    mean = jnp.where(low, total, turned) / pixels
    inv_std = lax.rsqrt(jnp.where(low, turned, total) / pixels - mean * mean + EPSILON)
    scale = facts[...] * inv_std
    out[...] = jnp.concatenate(
        [mean[:1], scale[:1], inv_std[:1], total[1:2], jnp.zeros((4, LANES), jnp.float32)], axis=0
    )
    for copy in along:
        copy.wait_send()
    for copy in across:
        copy.wait()


def gather_small_kernel(cols, mine, out, sends, recvs, sem):
    col = lax.axis_index("col")
    greet("col", cols)
    own = pltpu.make_async_copy(mine, out.at[col], sem)
    own.start()
    own.wait()
    met(cols - 1)
    relay = Relay(lambda at: out.at[at], sends, recvs, 0)
    relay.start()
    relay.forward()
    relay.wait()


def place_wide(pieces, wide, sems, rows, cols):
    few, piece = pieces.shape[2], pieces.shape[3]
    kappa = lax.axis_index("col")
    blocks = []
    for block in range(cols):
        copies = []
        for half in range(2):
            position = position_of(kappa, rows, cols, block, half)
            span, lanes = pl.ds(half * few, few), pl.ds(block * piece, piece)
            place = 2 * block + half
            copies.append(
                pltpu.make_async_copy(
                    pieces.at[position, pl.ds(0, LEADING)],
                    wide.at[pl.ds(0, LEADING), span, lanes],
                    sems.at[place, 0],
                )
            )
            for at in range(LEADING, len(KEPT)):
                copies.append(
                    pltpu.make_async_copy(
                        pieces.at[position, at],
                        wide.at[KEPT[at], span, lanes],
                        sems.at[place, at - LEADING + 1],
                    )
                )
        blocks.append(copies)
    for copies in blocks:
        for copy in copies:
            copy.start()
    for at in SPARES:
        wide[at] = jnp.zeros(wide.shape[1:], wide.dtype)
    return blocks


def head_kernel(
    rows, cols, classes, boxes, facts, score_bias, pooled_in, small_in, pieces,
    g6_all, g7_out, hid6_out, hid7_out, gs_out, scores_out, losses_out,
    pooled, small, wide, mine, taken, in_sems, sems, sends, recvs, relay_sends, relay_recvs,
):
    me = lax.axis_index("col")
    rois, hidden = g6_all.shape
    quarter, piece = rois // cols, hidden // cols
    greet("col", cols)
    pooled_copy = pltpu.make_async_copy(pooled_in, pooled, in_sems.at[0])
    small_copy = pltpu.make_async_copy(small_in, small, in_sems.at[1])
    pooled_copy.start()
    blocks = place_wide(pieces, wide, sems, rows, cols)
    small_copy.start()
    pooled_copy.wait()
    met(cols - 1)

    def sending(part, step):
        lanes = pl.ds(part * piece, piece)
        peer = lax.rem(me + step, cols)
        return pltpu.make_async_remote_copy(
            src_ref=mine.at[peer, :, lanes],
            dst_ref=taken.at[step - 1, :, lanes],
            send_sem=sends.at[step - 1, part],
            recv_sem=recvs.at[step - 1, part],
            device_id={"col": peer},
            device_id_type=MESH,
        )

    for part in range(cols):
        for copy in blocks[part]:
            copy.wait()
        lanes = slice(part * piece, (part + 1) * piece)
        weights = wide[:, :, lanes].reshape(WIDE, piece)
        result = jnp.dot(pooled[...], weights, preferred_element_type=jnp.float32)
        result = result.astype(jnp.bfloat16)
        for at in range(cols):
            mine[at, :, lanes] = result[at * quarter : (at + 1) * quarter]
        for step in range(1, cols):
            sending(part, step).start()
    small_copy.wait()
    for part in range(cols):
        for step in range(1, cols):
            sending(part, step).wait()
    pre_six = mine[me].astype(jnp.float32)
    for step in range(1, cols):
        pre_six = pre_six + taken[step - 1].astype(jnp.float32)
    lines = [small[at, 0, 4, :16, LANES:].astype(jnp.float32) for at in range(cols)]
    bias = jnp.concatenate(
        [
            (line[part : part + 1] + line[part + 2 : part + 3]) + line[part + 4 : part + 5]
            for line in lines
            for part in range(2)
        ],
        axis=1,
    )
    pre_six = pre_six + bias
    sigma_six = jax.nn.sigmoid(pre_six)
    hidden_six = (pre_six * sigma_six).astype(jnp.bfloat16)
    hid6_out[...] = hidden_six
    deep = [small[at, :, :4].reshape(hidden, piece) for at in range(cols)]
    head = jnp.concatenate(
        [small[at, row, 4, :, :LANES] for row in range(rows) for at in range(cols)], axis=0
    )
    lane = lax.broadcasted_iota(jnp.int32, (quarter, LANES), 1)
    pick = (lane == classes + boxes).astype(jnp.bfloat16)
    pre_seven = contract_last(pick, head)
    for at in range(cols):
        pre_seven = pre_seven + contract_last(
            hidden_six[:, at * piece : (at + 1) * piece], deep[at]
        )
    sigma_seven = jax.nn.sigmoid(pre_seven)
    hidden_seven = (pre_seven * sigma_seven).astype(jnp.bfloat16)
    hid7_out[...] = hidden_seven
    scores = jnp.dot(hidden_seven, head, preferred_element_type=jnp.float32) + score_bias[...]
    scores_out[...] = scores
    targets, onehot, weights = facts[0], facts[1], facts[2]
    is_class = lane < classes
    top = jnp.max(jnp.where(is_class, scores, -jnp.inf), axis=1, keepdims=True)
    powers = jnp.where(is_class, jnp.exp(jnp.where(is_class, scores - top, 0.0)), 0.0)
    log_total = top + jnp.log(jnp.sum(powers, axis=1, keepdims=True))
    picked = jnp.sum(onehot * scores, axis=1, keepdims=True)
    softmax = jnp.where(is_class, jnp.exp(jnp.where(is_class, scores - log_total, 0.0)), 0.0)
    misfit = jnp.where(is_class, 0.0, scores - targets)
    size = jnp.abs(misfit)
    huber = jnp.where(size < 1.0, 0.5 * misfit * misfit, size - 0.5)
    class_part = jnp.sum(weights[:, :1] * (log_total - picked), axis=0, keepdims=True)
    box_part = jnp.sum(jnp.where(is_class, 0.0, weights * huber), axis=0, keepdims=True)
    grads = jnp.where(is_class, softmax - onehot, jnp.clip(misfit, -1.0, 1.0))
    score_grads = (weights * grads).astype(jnp.bfloat16)
    gs_out[...] = score_grads
    losses_out[...] = jnp.concatenate(
        [
            jnp.broadcast_to(class_part, (1, LANES)),
            box_part,
            jnp.sum(score_grads.astype(jnp.float32), axis=0, keepdims=True),
            jnp.zeros((5, LANES), jnp.float32),
        ],
        axis=0,
    )
    slope_seven = sigma_seven * (1.0 + pre_seven * (1.0 - sigma_seven))
    g7 = (contract_last(score_grads, head) * slope_seven).astype(jnp.bfloat16)
    g7_out[...] = g7
    place = pl.ds(pl.multiple_of(me * quarter, quarter), quarter)
    relays = []
    for at in range(cols):
        lanes = slice(at * piece, (at + 1) * piece)
        back = jnp.dot(g7, deep[at], preferred_element_type=jnp.float32)
        sigma, value = sigma_six[:, lanes], pre_six[:, lanes]
        back = back * (sigma * (1.0 + value * (1.0 - sigma)))
        g6_all[place, lanes] = back.astype(jnp.bfloat16)
        relays.append(
            Relay(
                lambda owner, at=at: g6_all.at[
                    pl.ds(pl.multiple_of(owner * quarter, quarter), quarter),
                    pl.ds(at * piece, piece),
                ],
                relay_sends, relay_recvs, 3 * at,
            )
        )
        relays[-1].start()
    for relay in relays:
        relay.forward()
    for relay in relays:
        relay.wait()


def wide_grad_kernel(
    rows, cols, pooled, g6_all, g7, hid6, hid7, gs, losses,
    terms, g7_all, losses_all,
    hid6_own, buffers, last, extras, head_mine, head_taken, out_sems, sends, recvs,
):
    me = lax.axis_index("col")
    rois, hidden = g6_all.shape
    quarter, piece = rois // cols, hidden // cols
    owned, per = hidden // rows, hidden // (rows * cols)
    few = buffers.shape[2] // 4
    ring = ring_of(rows)
    greet("col", cols)

    def block(at):
        return pl.ds(pl.multiple_of(at * quarter, quarter), quarter)

    g7_all[block(me), :] = g7[...]
    losses_all[me] = losses[...]
    own = pl.ds(pl.multiple_of(me * piece, piece), piece)
    hid6_own[block(me), :] = hid6[:, own]
    head_term = contract_first(hid7[...], gs[...]).astype(jnp.bfloat16)
    for row in range(rows):
        for at in range(cols):
            first = row * owned + at * per
            head_mine[at, row] = head_term[first : first + per]
    met(cols - 1)
    relay = Relay(lambda at: g7_all.at[block(at)], sends, recvs, 0)
    relay.start()
    copies = []
    for step in range(1, cols):
        peer = lax.rem(me + step, cols)
        theirs = pl.ds(pl.multiple_of(peer * piece, piece), piece)
        copies.append(
            remote(hid6.at[:, theirs], hid6_own.at[block(me)], sends, recvs, 2 + step, "col", peer)
        )
        copies.append(
            remote(head_mine.at[peer], head_taken.at[step - 1], sends, recvs, 5 + step, "col", peer)
        )
        copies.append(
            remote(losses, losses_all.at[me], sends, recvs, 8 + step, "col", peer)
        )
    for copy in copies:
        copy.start()

    def leaving(slot, at):
        size = 4 * few
        span = pl.ds(pl.multiple_of(at * size, size), size)
        return pltpu.make_async_copy(buffers.at[slot], terms.at[:, span], out_sems.at[slot])

    def put(result, target, row, parts):
        for column in range(cols):
            columns = slice(column * piece, (column + 1) * piece)
            for half in range(2):
                position = position_of(me, rows, cols, column, half)
                for index, part in enumerate(parts):
                    first = (part * 2 + half) * few
                    target[position, row + index * few : row + (index + 1) * few, :] = result[
                        first : first + few, columns
                    ]

    def step(pair, carry):
        for slot in range(2):
            at = pair * 2 + slot

            @pl.when(pair > 0)
            def _():
                leaving(slot, at - 2).wait()

            lanes = pl.ds(pl.multiple_of(at * 2 * LANES, 2 * LANES), 2 * LANES)
            result = contract_first(pooled[:, lanes], g6_all[...]).astype(jnp.bfloat16)
            put(result, buffers.at[slot], 0, range(4))
            leaving(slot, at).start()
        return carry
    pairs = LEADING // 8
    lax.fori_loop(0, pairs - 1, step, 0)
    relay.forward()
    lax.fori_loop(pairs - 1, pairs, step, 0)
    row = 0
    for at in range(2 * pairs, len(USED) // 2):
        parts = [part for part in range(4) if 4 * at + part in KEPT]
        lanes = slice(at * 2 * LANES, (at + 1) * 2 * LANES)
        result = contract_first(pooled[:, lanes], g6_all[...]).astype(jnp.bfloat16)
        put(result, last, row, parts)
        row += len(parts) * few
    first = 2 * pairs * 4 * few
    rest = pltpu.make_async_copy(last, terms.at[:, pl.ds(first, row)], out_sems.at[2])
    rest.start()
    relay.wait()
    for copy in copies:
        copy.wait()
    deep_term = contract_first(g7_all[...], hid6_own[...]).astype(jnp.bfloat16)
    nothing = jnp.zeros((per, piece - LANES), jnp.bfloat16)
    for position, owner in enumerate(ring):
        extras[position, :owned, :] = deep_term[owner * owned : (owner + 1) * owned]
        total = head_mine[me, owner].astype(jnp.float32)
        for at in range(cols - 1):
            total = total + head_taken[at, owner].astype(jnp.float32)
        extras[position, owned : owned + per, :] = jnp.concatenate(
            [total.astype(jnp.bfloat16), nothing], axis=1
        )
    more = pltpu.make_async_copy(
        extras, terms.at[:, pl.ds(first + row, owned + per)], out_sems.at[3]
    )
    more.start()
    for slot in range(2):
        leaving(slot, 2 * pairs - 2 + slot).wait()
    rest.wait()
    more.wait()


def pool_grad_kernel(
    rows, cols, pixels, g6_all, g7_all, losses_all, centred, weight, stats, pieces,
    grads, totals, base, slope, wide, slots, sems, sends, recvs,
):
    row, col = lax.axis_index("roi"), lax.axis_index("col")
    rois, hidden = g6_all.shape
    channels = base.shape[0]
    piece = hidden // cols
    greet("roi", rows)
    blocks = place_wide(pieces, wide, sems, rows, cols)
    own = pl.ds(pl.multiple_of(col * piece, piece), piece)

    def columns(values):
        return jnp.sum(values.astype(jnp.float32), axis=0, keepdims=True)

    def as_rows(vector):
        return [
            vector[:, at * LANES : (at + 1) * LANES] for at in range(vector.shape[1] // LANES)
        ]

    bias_rows = as_rows(columns(g6_all[:, own])) + as_rows(columns(g7_all[...]))
    losses = losses_all[0]
    for at in range(1, cols):
        losses = losses + losses_all[at]
    for copies in blocks:
        for copy in copies:
            copy.wait()
    scale = stats[1:2]

    def step(at, carry):
        gain, shift = carry
        lanes = pl.ds(pl.multiple_of(at * 2 * LANES, 2 * LANES), 2 * LANES)
        weights = wide[pl.ds(at * 4, 4)].reshape(2 * LANES, hidden)
        result = contract_last(g6_all[...], weights)
        with_centred = result * centred[:, lanes].astype(jnp.float32)
        with_weight = result * weight[:, lanes].astype(jnp.float32)
        both = jnp.concatenate([scale, scale], axis=1)
        grads[:, lanes] = (result * both).astype(jnp.bfloat16)
        for half in range(2):
            part = slice(half * LANES, (half + 1) * LANES)
            gain = gain + jnp.sum(with_centred[:, part].reshape(rois // 8, 8, LANES), axis=0)
            shift = shift + jnp.sum(with_weight[:, part].reshape(rois // 8, 8, LANES), axis=0)
        return gain, shift

    nothing = jnp.zeros((8, LANES), jnp.float32)
    gain, shift = lax.fori_loop(0, len(USED) // 2, step, (nothing, nothing))
    low = lax.broadcasted_iota(jnp.int32, (8, LANES), 1) < channels
    both = jnp.where(
        low, gain + pltpu.roll(gain, channels, 1), shift + pltpu.roll(shift, channels, 1)
    )
    both = jnp.sum(both, axis=0, keepdims=True)
    lines = [both] + bias_rows + [losses[2:3], losses[:2]]
    count = 1 + len(bias_rows) + 3
    lines.append(jnp.zeros((16 - count, LANES), jnp.float32))
    slots[row] = jnp.concatenate(lines, axis=0)
    met(rows - 1)
    for copy in share(slots, "roi", rows, sends, recvs):
        copy.wait()
    total = slots[0]
    for at in range(1, rows):
        total = total + slots[at]
    gain_grad = total[:1] * stats[2:3]
    totals[...] = jnp.concatenate([total[:15], gain_grad], axis=0)
    slope_row = -stats[1:2] * stats[2:3] * gain_grad / pixels
    shift_grad = pltpu.roll(jnp.broadcast_to(total[:1], (8, LANES)), channels, 1)[:1]
    base_row = -stats[1:2] * shift_grad / pixels - slope_row * stats[:1]
    slope[...] = jnp.broadcast_to(slope_row[:, :channels], (LANES, channels)).T
    base[...] = jnp.broadcast_to(base_row[:, :channels], (LANES, channels)).T


def deliver_kernel(rows, cols, few, term, out, held, taken, half, sems, sends, recvs):
    row, col = lax.axis_index("roi"), lax.axis_index("col")
    plane, side = lax.div(row, 2), lax.rem(row, 2)
    chip, core = lax.div(col, 2), lax.rem(col, 2)
    near = {"roi": row, "col": cols - 1 - col}
    crossing = lax.rem(lax.rem(plane + cols - col, cols), 2) != chip
    kappa = jnp.where(crossing, cols - 1 - col, col)
    core_there = lax.div(lax.rem(plane + cols - kappa, cols), 2)
    target = {"roi": kappa * 2 + side, "col": 2 * chip + core_there}
    alone = (kappa == plane) & (core_there == core)
    plane_from = lax.rem(2 * core + chip + plane, cols)
    core_from = jnp.where(lax.div(plane, 2) == chip, lax.rem(plane, 2), 1 - lax.rem(plane, 2))
    source = {"roi": plane_from * 2 + side, "col": 2 * chip + core_from}
    barrier = pltpu.get_barrier_semaphore()

    @pl.when(crossing)
    def _():
        pl.semaphore_signal(barrier, inc=1, device_id=near, device_id_type=MESH)

    @pl.when(jnp.logical_not(alone))
    def _():
        pl.semaphore_signal(barrier, inc=1, device_id=source, device_id_type=MESH)

    @pl.when(crossing | jnp.logical_not(alone))
    def _():
        pl.semaphore_wait(barrier, crossing.astype(jnp.int32) + 1 - alone.astype(jnp.int32))

    count = 7
    size = len(KEPT) // count
    spans = [pl.ds(at * size * few, size * few) for at in range(count)]

    def over(at):
        return pltpu.make_async_remote_copy(
            src_ref=term.at[spans[at]], dst_ref=held.at[spans[at]],
            send_sem=sends.at[0, at], recv_sem=recvs.at[0, at],
            device_id=near, device_id_type=MESH,
        )

    def along(block, at):
        return pltpu.make_async_remote_copy(
            src_ref=block.at[spans[at]], dst_ref=taken.at[spans[at]],
            send_sem=sends.at[1, at], recv_sem=recvs.at[1, at],
            device_id=target, device_id_type=MESH,
        )

    def inside(block, at):
        return pltpu.make_async_copy(block.at[spans[at]], taken.at[spans[at]], sems.at[at])

    def pass_on(block, at):
        @pl.when(alone)
        def _():
            inside(block, at).start()

        @pl.when(jnp.logical_not(alone))
        def _():
            along(block, at).start()

    @pl.when(crossing)
    def _():
        for at in range(count):
            over(at).start()
        for at in range(count):
            over(at).wait_recv()
            pass_on(held, at)

    @pl.when(jnp.logical_not(crossing))
    def _():
        for at in range(count):
            pass_on(term, at)

    for chunk in range(count):
        @pl.when(alone)
        def _():
            inside(held, chunk).wait()

        @pl.when(jnp.logical_not(alone))
        def _():
            along(held, chunk).wait_recv()

        for index in range(chunk * size, (chunk + 1) * size):
            slot = KEPT[index]
            place = pl.ds(slot // 2 % 7 * 7 + slot // 14 + 4 * (slot % 2), few, stride=49)
            for part in range(out.shape[1] // LANES):
                half[part, place, :] = taken[
                    index * few : (index + 1) * few, part * LANES : (part + 1) * LANES
                ].astype(jnp.float32)
    for part in range(out.shape[1] // LANES):
        out[:, part * LANES : (part + 1) * LANES] = half[part]

    @pl.when(crossing)
    def _():
        for at in range(count):
            over(at).wait_send()

    @pl.when(jnp.logical_not(alone))
    def _():
        for at in range(count):
            along(held, at).wait_send()


def unpool_all_kernel(
    rois, rows, cols, classes, boxes, floats, ints, order, base, slope, totals, grads, *rest
):
    planes, outs, few, scratch = rest[:4], rest[4:8], rest[8:16], rest[16:]
    gain, shift, bias_six, bias_seven, bias_cls, bias_box, cls_loss, box_loss = few
    channels, per = gain.shape[0], bias_seven.shape[0]
    row, col = lax.axis_index("roi"), lax.axis_index("col")

    def finish():
        head = totals[:8]
        turned = pltpu.roll(head, channels, 1)
        gain[...] = totals[8:][7, :channels]
        shift[...] = turned[0, :channels]
        wide_lines = bias_six.shape[0] // LANES
        for at in range(wide_lines):
            bias_six[at * LANES : (at + 1) * LANES] = head[1 + at]
        place = (row * cols + col) * per
        line = totals[pl.ds(1 + wide_lines + lax.div(place, LANES), 1), :]
        line = pltpu.roll(
            jnp.broadcast_to(line, (8, LANES)), lax.rem(LANES - lax.rem(place, LANES), LANES), 1
        )
        bias_seven[...] = line[0, :per]
        first = 1 + (cols + 1) * wide_lines
        scores = jnp.broadcast_to(totals[first : first + 1], (8, LANES))
        bias_cls[...] = scores[0, :classes]
        bias_box[...] = pltpu.roll(scores, LANES - classes, 1)[0, :boxes]
        cls_loss[...] = totals[first + 1 : first + 2, :1] / (rois * rows)
        box_loss[...] = jnp.sum(totals[first + 2 : first + 3], axis=1, keepdims=True) / (
            rois * rows
        )

    unpool_kernel(
        rois, floats, ints, order, base, slope, grads, *planes, *outs, *scratch, finish=finish
    )


def unpool_all(
    floats, ints, order, base, slope, totals, grads, planes, rois, rows, cols, classes, boxes,
    piece,
):
    channels = planes[0].shape[1]
    f32 = jnp.float32
    results = pl.pallas_call(
        functools.partial(unpool_all_kernel, rois, rows, cols, classes, boxes),
        out_shape=tuple(shaped(plane.shape, f32) for plane in planes)
        + (
            shaped((channels,), f32),
            shaped((channels,), f32),
            shaped((piece,), f32),
            shaped((piece // rows,), f32),
            shaped((classes,), f32),
            shaped((boxes,), f32),
            shaped((1, 1), f32),
            shaped((1, 1), f32),
        ),
        in_specs=[SMEM] * 3 + [VMEM] * 4 + [ANY] * 4,
        out_specs=(ANY,) * 4 + (VMEM,) * 8,
        scratch_shapes=[
            pltpu.VMEM((channels, ALL_TILES * LANES), jnp.bfloat16),
            pltpu.VMEM((channels, PADDED * LANES), f32),
            pltpu.VMEM((SLOTS * (rois + SPARE), LANES), f32),
            pltpu.SemaphoreType.DMA((7,)),
            pltpu.SemaphoreType.DMA((4,)),
        ],
        compiler_params=pltpu.CompilerParams(vmem_limit_bytes=LIMIT),
        name="unpool",
    )(floats, ints, order, base, slope, totals, grads, *planes)
    return results[:4], results[4:]


def comm_params(number):
    return pltpu.CompilerParams(
        vmem_limit_bytes=LIMIT, collective_id=number, has_side_effects=True
    )


def shaped(shape, dtype):
    return jax.ShapeDtypeStruct(shape, dtype)


def statistics(facts, small, planes, rows, pixels):
    channels = planes[0].shape[1]
    moves = rows // 2 - 1 + rows // 2
    return pl.pallas_call(
        functools.partial(stats_kernel, rows, pixels),
        out_shape=(
            shaped((8, LANES), jnp.float32),
            shaped((rows,) + small.shape, small.dtype),
        ),
        in_specs=[VMEM, VMEM, ANY, ANY, ANY, ANY],
        out_specs=(VMEM, VMEM),
        scratch_shapes=[
            pltpu.VMEM((channels, ALL_TILES * LANES), jnp.bfloat16),
            pltpu.VMEM((rows, 8, LANES), jnp.float32),
            pltpu.SemaphoreType.DMA((7,)),
            pltpu.SemaphoreType.DMA((rows - 1,)),
            pltpu.SemaphoreType.DMA((rows - 1,)),
            pltpu.SemaphoreType.DMA((moves,)),
            pltpu.SemaphoreType.DMA((moves,)),
        ],
        compiler_params=comm_params(0),
        name="statistics",
    )(facts, small, *planes)


def gather_small(mine, cols):
    return pl.pallas_call(
        functools.partial(gather_small_kernel, cols),
        out_shape=shaped((cols,) + mine.shape, mine.dtype),
        in_specs=[VMEM],
        out_specs=VMEM,
        scratch_shapes=[
            pltpu.SemaphoreType.DMA((3,)),
            pltpu.SemaphoreType.DMA((3,)),
            pltpu.SemaphoreType.DMA,
        ],
        compiler_params=comm_params(1),
        name="gather_small",
    )(mine)


def run_head(pooled, facts, score_bias, small, pieces, rows, cols, classes, boxes):
    rois, channels = pooled.shape[0], LANES // 2
    quarter, hidden = rois // cols, pieces.shape[3] * cols
    bf16, f32 = jnp.bfloat16, jnp.float32
    return pl.pallas_call(
        functools.partial(head_kernel, rows, cols, classes, boxes),
        out_shape=(
            shaped((rois, hidden), bf16),
            shaped((quarter, hidden), bf16),
            shaped((quarter, hidden), bf16),
            shaped((quarter, hidden), bf16),
            shaped((quarter, LANES), bf16),
            shaped((quarter, LANES), f32),
            shaped((8, LANES), f32),
        ),
        in_specs=[VMEM, VMEM, ANY, ANY, ANY],
        out_specs=(VMEM,) * 7,
        scratch_shapes=[
            pltpu.VMEM(pooled.shape, bf16),
            pltpu.VMEM(small.shape, bf16),
            pltpu.VMEM((2 * len(USED), channels, hidden), bf16),
            pltpu.VMEM((cols, quarter, hidden), bf16),
            pltpu.VMEM((cols - 1, quarter, hidden), bf16),
            pltpu.SemaphoreType.DMA((2,)),
            pltpu.SemaphoreType.DMA((rows, 8)),
            pltpu.SemaphoreType.DMA((cols - 1, cols)),
            pltpu.SemaphoreType.DMA((cols - 1, cols)),
            pltpu.SemaphoreType.DMA((3 * cols,)),
            pltpu.SemaphoreType.DMA((3 * cols,)),
        ],
        compiler_params=comm_params(2),
        name="head",
    )(facts, score_bias, pooled, small, pieces)


def wide_grads(pooled, g6_all, g7, hid6, hid7, gs, losses, rows, cols):
    rois, hidden = g6_all.shape
    piece, few = hidden // cols, LANES // 2 // (rows // cols)
    owned, per = hidden // rows, hidden // (rows * cols)
    bf16, f32 = jnp.bfloat16, jnp.float32
    return pl.pallas_call(
        functools.partial(wide_grad_kernel, rows, cols),
        out_shape=(
            shaped((rows, len(KEPT) * few + owned + per, piece), bf16),
            shaped((rois, hidden), bf16),
            shaped((cols, 8, LANES), f32),
        ),
        in_specs=[VMEM] * 7,
        out_specs=(ANY, VMEM, VMEM),
        scratch_shapes=[
            pltpu.VMEM((rois, piece), bf16),
            pltpu.VMEM((2, rows, 4 * few, piece), bf16),
            pltpu.VMEM((rows, (len(KEPT) - LEADING // 8 * 8) * few, piece), bf16),
            pltpu.VMEM((rows, owned + per, piece), bf16),
            pltpu.VMEM((cols, rows, per, LANES), bf16),
            pltpu.VMEM((cols - 1, rows, per, LANES), bf16),
            pltpu.SemaphoreType.DMA((4,)),
            pltpu.SemaphoreType.DMA((12,)),
            pltpu.SemaphoreType.DMA((12,)),
        ],
        compiler_params=comm_params(3),
        name="wide_grads",
    )(pooled, g6_all, g7, hid6, hid7, gs, losses)


def pool_grads(g6_all, g7_all, losses_all, centred, weight, stats, pieces, rows, cols, pixels):
    rois, hidden = g6_all.shape
    channels = LANES // 2
    bf16, f32 = jnp.bfloat16, jnp.float32
    return pl.pallas_call(
        functools.partial(pool_grad_kernel, rows, cols, pixels),
        out_shape=(
            shaped((rois, WIDE), bf16),
            shaped((16, LANES), f32),
            shaped((channels, LANES), f32),
            shaped((channels, LANES), f32),
        ),
        in_specs=[VMEM] * 6 + [ANY],
        out_specs=(VMEM,) * 4,
        scratch_shapes=[
            pltpu.VMEM((2 * len(USED), channels, hidden), bf16),
            pltpu.VMEM((rows, 16, LANES), f32),
            pltpu.SemaphoreType.DMA((rows, 8)),
            pltpu.SemaphoreType.DMA((rows - 1,)),
            pltpu.SemaphoreType.DMA((rows - 1,)),
        ],
        compiler_params=comm_params(4),
        name="pool_grads",
    )(g6_all, g7_all, losses_all, centred, weight, stats, pieces)


def deliver(term, rows, cols, few):
    piece, kept = term.shape[1], len(KEPT) * few
    return pl.pallas_call(
        functools.partial(deliver_kernel, rows, cols, few),
        out_shape=shaped((kept, piece), jnp.float32),
        in_specs=[ANY],
        out_specs=VMEM,
        scratch_shapes=[
            pltpu.VMEM((kept, piece), term.dtype),
            pltpu.VMEM((kept, piece), term.dtype),
            pltpu.VMEM((piece // LANES, kept, LANES), jnp.float32),
            pltpu.SemaphoreType.DMA((7,)),
            pltpu.SemaphoreType.DMA((2, 7)),
            pltpu.SemaphoreType.DMA((2, 7)),
        ],
        compiler_params=comm_params(5),
        name="deliver",
    )(term)


def targets_of(mine_boxes, mine_goals):
    prop_width = mine_boxes[2] - mine_boxes[0]
    prop_height = mine_boxes[3] - mine_boxes[1]
    prop_cx = mine_boxes[0] + 0.5 * prop_width
    prop_cy = mine_boxes[1] + 0.5 * prop_height
    goal_width = mine_goals[2] - mine_goals[0]
    goal_height = mine_goals[3] - mine_goals[1]
    goal_cx = mine_goals[0] + 0.5 * goal_width
    goal_cy = mine_goals[1] + 0.5 * goal_height
    return jnp.stack(
        [
            10.0 * (goal_cx - prop_cx) / prop_width,
            10.0 * (goal_cy - prop_cy) / prop_height,
            5.0 * jnp.log(goal_width / prop_width),
            5.0 * jnp.log(goal_height / prop_height),
        ],
        axis=1,
    )


def decode(mine_boxes, deltas):
    prop_width = mine_boxes[2] - mine_boxes[0]
    prop_height = mine_boxes[3] - mine_boxes[1]
    prop_cx = mine_boxes[0] + 0.5 * prop_width
    prop_cy = mine_boxes[1] + 0.5 * prop_height
    centre_x = prop_cx + deltas[:, 0] / 10.0 * prop_width
    centre_y = prop_cy + deltas[:, 1] / 10.0 * prop_height
    new_width = prop_width * jnp.exp(deltas[:, 2] / 5.0)
    new_height = prop_height * jnp.exp(deltas[:, 3] / 5.0)
    return jnp.stack(
        [
            centre_x - 0.5 * new_width,
            centre_y - 0.5 * new_height,
            centre_x + 0.5 * new_width,
            centre_y + 0.5 * new_height,
        ]
    ) / (CANVAS // 2)


def local_near(
    p2, p3, p4, p5, norm_gain, norm_bias, fc6_weight, fc6_bias, fc7_weight, fc7_bias,
    cls_weight, cls_bias, box_weight, box_bias, roi_boxes, roi_level, roi_image,
    canvas_offsets, labels, target_boxes, valid,
):
    channels = p2.shape[1]
    rois = roi_level.shape[0]
    cols = lax.axis_size("col")
    rows = lax.axis_size("roi")
    piece = fc6_bias.shape[0]
    high = rows // cols
    few = channels // high
    planes = (p2, p3, p4, p5)
    pixels = rows * sum(plane.shape[2] for plane in planes)
    ring = ring_of(rows)
    per = fc7_bias.shape[0]
    classes, boxes = cls_weight.shape[1], box_weight.shape[1]
    bf16, f32 = jnp.bfloat16, jnp.float32

    block = fc6_weight.reshape(few, 7, 7, piece)
    block = jnp.pad(block, ((0, 0), (0, 0), (0, 1), (0, 0))).reshape(few, 7, 2, 4, piece)
    block = block.transpose(3, 1, 2, 0, 4).reshape(2 * len(USED), few, piece)
    block = jnp.concatenate([block[:LEADING], block[LEADING::2]])
    pairs = []
    for kappa in range(cols):
        for block_at in range(cols):
            for half in range(high):
                plane = (2 * (block_at % 2) + block_at // 2 + kappa) % cols
                source = (kappa * high + half) * cols + block_at
                pairs.append((source, (plane * high + half) * cols + kappa))
    block = lax.ppermute(block, ("roi", "col"), pairs)

    head = jnp.concatenate([cls_weight, box_weight, fc7_bias[:, None]], axis=1)
    head = jnp.pad(head, ((0, 0), (0, piece - head.shape[1])))
    bias_high = fc6_bias.astype(bf16)
    rest = fc6_bias - bias_high.astype(f32)
    bias_mid = rest.astype(bf16)
    bias_low = (rest - bias_mid.astype(f32)).astype(bf16)
    bias = jnp.concatenate([item.reshape(2, LANES) for item in (bias_high, bias_mid, bias_low)])
    bias = jnp.pad(bias, ((0, per - bias.shape[0]), (0, 0)))
    head = jnp.concatenate([head[:, :LANES], bias], axis=1)
    small = jnp.concatenate([fc7_weight, head], axis=0).reshape(SMALL, few, piece)

    def twice(vector):
        return jnp.concatenate([vector, vector])[None]

    count = jnp.sum(valid.astype(f32))
    norm_facts = jnp.concatenate(
        [twice(norm_gain), jnp.full((1, LANES), count), jnp.zeros((6, LANES), f32)]
    )
    stats, small = statistics(norm_facts, small, planes, rows, float(pixels))
    valid_total = stats[3, 0]

    picks = roi_image[None, :] == jnp.arange(4, dtype=jnp.int32)[:, None]
    shift_x = jnp.sum(jnp.where(picks, canvas_offsets[0][:, None], 0), axis=0)
    shift_y = jnp.sum(jnp.where(picks, canvas_offsets[1][:, None], 0), axis=0)
    floats, ints, order = region_tables(
        (roi_boxes[0] + shift_x).astype(f32),
        (roi_boxes[1] + shift_y).astype(f32),
        (roi_boxes[2] + shift_x).astype(f32),
        (roi_boxes[3] + shift_y).astype(f32),
        roi_level,
    )
    block = lax.optimization_barrier((block, stats, floats, order))[0]
    pieces = lax.all_gather(block, "roi", axis=0, axis_index_groups=[ring])
    pooled, centred, weight = pool_maps(
        floats, ints, order, stats, twice(norm_bias), planes, rois
    )

    quarter = rois // cols
    first_row = lax.axis_index("col") * quarter
    mine_labels = lax.dynamic_slice_in_dim(labels, first_row, quarter)
    mine_valid = lax.dynamic_slice_in_dim(valid, first_row, quarter).astype(f32)
    mine_boxes = lax.dynamic_slice_in_dim(roi_boxes, first_row, quarter, axis=1).astype(f32)
    mine_goals = lax.dynamic_slice_in_dim(target_boxes, first_row, quarter, axis=1).astype(f32)
    foreground = mine_valid * (mine_labels > 0).astype(f32)
    loss_scale = rois * rows / valid_total
    lane = jnp.arange(LANES, dtype=jnp.int32)[None, :]
    after = LANES - classes - boxes
    facts = jnp.stack(
        [
            jnp.pad(targets_of(mine_boxes, mine_goals), ((0, 0), (classes, after))),
            (mine_labels[:, None] == lane).astype(f32),
            loss_scale
            * jnp.where(
                lane < classes,
                mine_valid[:, None],
                jnp.where(lane < classes + boxes, foreground[:, None], 0.0),
            ),
        ]
    )
    score_bias = jnp.pad(jnp.concatenate([cls_bias, box_bias]), (0, after))[None]
    small, facts, score_bias, _ = lax.optimization_barrier((small, facts, score_bias, pooled))
    small = gather_small(small, cols)
    g6_all, g7, hid6, hid7, gs, scores, losses = run_head(
        pooled, facts, score_bias, small, pieces, rows, cols, classes, boxes
    )
    decoded = decode(mine_boxes, scores[:, classes : classes + boxes])

    terms, g7_all, losses_all = wide_grads(
        pooled, g6_all, g7, hid6, hid7, gs, losses, rows, cols
    )
    wide_rows = terms.shape[1]
    term = lax.psum_scatter(
        terms.reshape(rows * wide_rows, piece), "roi", scatter_dimension=0, tiled=True,
        axis_index_groups=[ring],
    )
    grads, totals, base, slope = pool_grads(
        g6_all, g7_all, losses_all, centred, weight, stats, pieces, rows, cols,
        float(pixels),
    )
    input_grads, few_grads = unpool_all(
        floats, ints, order, base, slope, totals, grads, planes, rois, rows, cols, classes, boxes,
        piece,
    )
    term = lax.optimization_barrier((term, input_grads[3]))[0]
    fc6_weight_grad = deliver(term, rows, cols, few)
    kept = len(KEPT) * few
    deep_rows = fc7_weight.shape[0]
    extra = term[kept:].astype(f32)
    fc7_weight_grad = extra[:deep_rows]
    head_grad = extra[deep_rows:]
    cls_weight_grad = head_grad[:, :classes]
    box_weight_grad = head_grad[:, classes : classes + boxes]

    (
        norm_gain_grad, norm_bias_grad, fc6_bias_grad, fc7_bias_grad, class_bias_grad,
        box_bias_grad, cls_loss, box_loss,
    ) = few_grads
    return (
        cls_loss[0, 0],
        box_loss[0, 0],
        decoded,
        *input_grads,
        norm_gain_grad,
        norm_bias_grad,
        fc6_weight_grad,
        fc6_bias_grad,
        fc7_weight_grad,
        fc7_bias_grad,
        cls_weight_grad,
        class_bias_grad,
        box_weight_grad,
        box_bias_grad,
    )


def solution(mesh):
    near = mesh.shape["roi"] == 2 * mesh.shape["col"] and mesh.shape["col"] == 4
    return jax.shard_map(
        local_near if near else local,
        mesh=mesh,
        in_specs=(
            P("roi", "col", None),
            P("roi", "col", None),
            P("roi", "col", None),
            P("roi", "col", None),
            P("col"),
            P("col"),
            P("roi", "col"),
            P("col"),
            P("roi", "col"),
            P(("roi", "col")),
            P(("roi", "col"), None),
            P(),
            P(("roi", "col"), None),
            P(),
            P(None, "roi"),
            P("roi"),
            P("roi"),
            P(None, "roi"),
            P("roi"),
            P(None, "roi"),
            P("roi"),
        ),
        out_specs=(
            P(),
            P(),
            P(None, ("roi", "col")),
            P("roi", "col", None),
            P("roi", "col", None),
            P("roi", "col", None),
            P("roi", "col", None),
            P("col"),
            P("col"),
            P("roi", "col"),
            P("col"),
            P("roi", "col"),
            P(("roi", "col")),
            P(("roi", "col"), None),
            P(),
            P(("roi", "col"), None),
            P(),
        ),
        check_vma=False,
    )
```

```python
import functools
import math

import jax
import jax.numpy as jnp
from jax import lax
from jax.experimental import pallas as pl
from jax.experimental.pallas import tpu as pltpu
from jax.sharding import PartitionSpec as P

CANVAS = 1024
EPSILON = 1e-05
LANES = 128
SPAN = 10
NARROW = 8
GROUP = 16
MORE = 16
SPARE = 8
SIDES = tuple(CANVAS // (4 * 2**level) for level in range(4))
TILES = tuple(side * side // LANES for side in SIDES)
FIRST = tuple(sum(TILES[:level]) for level in range(4))
ALL_TILES = sum(TILES)
PADDED = ALL_TILES + max(SPAN - min(TILES), 0)
SLOTS = 32
USED = tuple(slot for slot in range(SLOTS) if slot % 8 < 7)
WIDE = len(USED) * LANES
F32_FIELDS = 7
I32_FIELDS = 6


def silu_slope(values):
    sigma = jax.nn.sigmoid(values)
    return sigma * (1.0 + values * (1.0 - sigma))


def contract_first(left_m, right_m):
    return lax.dot_general(
        left_m, right_m, (((0,), (0,)), ((), ())), preferred_element_type=jnp.float32
    )


def contract_last(left_m, right_m):
    return lax.dot_general(
        left_m, right_m, (((1,), (1,)), ((), ())), preferred_element_type=jnp.float32
    )


def region_tables(left, top, right, bottom, level):
    def by_level(values):
        chosen = jnp.full(level.shape, values[0])
        for at in range(1, 4):
            chosen = jnp.where(level == at, values[at], chosen)
        return chosen

    step = by_level([4.0 * 2**at for at in range(4)])
    side = by_level(list(SIDES))
    rows_log = by_level([(max(LANES // n, 1)).bit_length() - 1 for n in SIDES])
    across = by_level([max(n // LANES, 1) for n in SIDES])
    x_anchor, x_extent = left / step - 0.5, (right - left) / step
    y_anchor, y_extent = top / step - 0.5, (bottom - top) / step

    def window(anchor, extent):
        low = jnp.floor(anchor + extent * (0.5 / 14.0)).astype(jnp.int32)
        high = jnp.floor(anchor + extent * (13.5 / 14.0)).astype(jnp.int32) + 1
        return jnp.clip(low, 0, side - 1), jnp.clip(high, 0, side - 1)

    y_low, y_high = window(y_anchor, y_extent)
    x_low, x_high = window(x_anchor, x_extent)
    group_low, group_high = y_low >> rows_log, y_high >> rows_log
    tile_x = x_low // LANES
    tiles_x = x_high // LANES - tile_x + 1
    narrow = (group_high - group_low < NARROW) & (tiles_x == 1)
    chunks = jnp.where(narrow, 1, (group_high - group_low + SPAN) // SPAN)
    taken = jnp.where(narrow, NARROW, chunks * SPAN)
    group = jnp.maximum(jnp.minimum(group_low, (side >> rows_log) - taken), 0)
    first_tile = by_level(list(FIRST)) + group * across + tile_x
    mask = jnp.minimum(side, LANES) - 1
    shift = 7 - rows_log
    rows_per = (1 << rows_log).astype(jnp.float32)
    nothing = jnp.zeros((SPARE,), jnp.int32)
    parts = chunks * tiles_x
    kind = jnp.where(narrow, 0, jnp.where(parts > 1, 2, 1))
    key = jnp.where(level > 0, 3 + kind, 2 - kind)
    rois = level.shape[0]
    at = jnp.arange(rois, dtype=jnp.int32)
    before = (key[None, :] < key[:, None]) | (
        (key[None, :] == key[:, None]) & (at[None, :] < at[:, None])
    )
    rank = jnp.sum(before.astype(jnp.int32), axis=1)
    order = jnp.sum(jnp.where(rank[None, :] == at[:, None], at[None, :], 0), axis=1)
    order = jnp.concatenate([order, jnp.full((GROUP,), rois, jnp.int32)])
    ends = jnp.stack([jnp.sum((key <= last).astype(jnp.int32)) for last in range(6)])
    floats = jnp.stack(
        [
            x_anchor,
            x_extent,
            y_anchor,
            y_extent,
            (tile_x * LANES).astype(jnp.float32),
            group.astype(jnp.float32) * rows_per,
            rows_per,
        ]
    ).astype(jnp.float32)
    ints = jnp.stack([first_tile, across, mask, shift, parts, tiles_x]).astype(jnp.int32)
    away = jnp.full((F32_FIELDS, SPARE), -1e6, jnp.float32)
    floats = jnp.concatenate([floats, away], axis=1)
    ints = jnp.concatenate([ints, jnp.broadcast_to(nothing, (I32_FIELDS, SPARE))], axis=1)
    return floats.reshape(-1), ints.reshape(-1), jnp.concatenate([order, ends])


def window_weights(floats, ints, rois, region, chunk, tile_x, span=SPAN):
    rois = rois + SPARE
    x_anchor, x_extent, y_anchor, y_extent, x_origin, y_origin, rows_per = (
        floats[at * rois + region] for at in range(F32_FIELDS)
    )
    first_tile, across, mask, shift = (ints[at * rois + region] for at in range(4))
    if chunk is not None:
        first_tile = first_tile + chunk * (SPAN * across) + tile_x
        x_origin = x_origin + (tile_x * LANES).astype(jnp.float32)
        y_origin = y_origin + (chunk * SPAN).astype(jnp.float32) * rows_per
    lane = lax.broadcasted_iota(jnp.int32, (8, LANES), 1)
    bin_at = lax.broadcasted_iota(jnp.int32, (8, LANES), 0)
    x_cell = (lane & mask).astype(jnp.float32) + x_origin
    y_cell = lax.shift_right_logical(lane, jnp.broadcast_to(shift, lane.shape)).astype(
        jnp.float32
    ) + y_origin
    part = jnp.where(bin_at < 7, (2.0 * bin_at.astype(jnp.float32) + 0.5) / 14.0, -1e6)
    near = y_anchor + y_extent * part - y_cell
    far = y_anchor + y_extent * (part + 1.0 / 14.0) - y_cell

    def tent(distance):
        return jnp.maximum(1.0 - jnp.abs(distance), 0.0)

    across_w = []
    for j in range(7):
        one = x_anchor + x_extent * ((2 * j + 0.5) / 14.0)
        two = x_anchor + x_extent * ((2 * j + 1.5) / 14.0)
        across_w.append(0.25 * (tent(one - x_cell) + tent(two - x_cell)))
    across_w.append(jnp.zeros((8, LANES), jnp.float32))
    packed = [
        jnp.concatenate([across_w[2 * at], across_w[2 * at + 1]], axis=0).astype(jnp.bfloat16)
        for at in range(4)
    ]
    blocks = []
    for at in range(span):
        offset = rows_per * float(at)
        down = tent(near - offset) + tent(far - offset)
        both = jnp.concatenate([down, down], axis=0).astype(jnp.bfloat16)
        blocks.append(jnp.concatenate([both * item for item in packed], axis=0))
    return jnp.concatenate(blocks, axis=1), first_tile, across


def tile_lanes(first_tile, across, at):
    return pl.ds(pl.multiple_of((first_tile + at * across) * LANES, LANES), LANES)


def for_groups(order, start, stop, size, body):
    def step(at, carry):
        first = start + at * size
        inside = [first + index < stop for index in range(size)]
        spare = order.shape[0] - 7
        places = [
            jnp.where(good, first + index, spare) for index, good in enumerate(inside)
        ]
        body([order[place] for place in places])
        return carry

    lax.fori_loop(0, (stop - start + size - 1) // size, step, 0)


def for_parts(ints, order, rois, start, stop, size, body):
    stride = rois + SPARE

    def second(regions):
        for region in regions:
            tiles_x = ints[5 * stride + region]
            wide = (tiles_x > 1).astype(jnp.int32)
            body(region, 1 - wide, wide)

    for_groups(order, start, stop, size, second)

    def later(at, carry):
        region = order[at]
        tiles_x = ints[5 * stride + region]

        def part(index, inner):
            chunk = index // tiles_x
            body(region, chunk, index - chunk * tiles_x)
            return inner

        return lax.fori_loop(2, ints[4 * stride + region], part, carry)

    lax.fori_loop(start, stop, later, 0)


def ends_of(order):
    size = order.shape[0]
    return [order[size - 6 + at] for at in range(6)]


def pool_kernel(
    rois, floats, ints, order, p2, p3, p4, p5,
    centred_out, weight_out, local_out, maps, values, sems,
):
    channels = p2.shape[1]
    stride = rois + SPARE
    copies = []
    for level, plane in enumerate((p2, p3, p4, p5)):
        cells = TILES[level] * LANES
        copies.append(
            pltpu.make_async_copy(
                plane.at[0],
                maps.at[pl.ds(0, channels), pl.ds(FIRST[level] * LANES, cells)],
                sems.at[level],
            )
        )
    for copy in copies[::-1]:
        copy.start()
    ones = jnp.ones((16, 8 * LANES), jnp.bfloat16)

    def fill(at, carry):
        lanes = pl.ds(pl.multiple_of(at * 8 * LANES, 8 * LANES), 8 * LANES)
        maps[pl.ds(channels, 16), lanes] = ones
        return carry

    lax.fori_loop(0, ALL_TILES // 8, fill, 0)
    extra = PADDED - ALL_TILES
    if extra:
        maps[:, pl.ds(ALL_TILES * LANES, extra * LANES)] = jnp.zeros(
            (channels + 16, extra * LANES), jnp.bfloat16
        )
    for copy in copies[1:]:
        copy.wait()

    def item(region, chunk, tile_x, span=SPAN):
        kernel_w, first_tile, across = window_weights(
            floats, ints, rois, region, chunk, tile_x, span
        )
        cells = jnp.concatenate(
            [maps[:, tile_lanes(first_tile, across, at)] for at in range(span)], axis=1
        )
        return contract_last(kernel_w, cells)

    def place(region):
        return pl.ds(region, 2 * SLOTS, stride=stride)

    def narrow(regions):
        for region in regions:
            values[place(region), : channels + 16] = item(region, None, None, NARROW)

    def first(regions):
        for region in regions:
            values[place(region), : channels + 16] = item(region, None, None)

    def further(region, chunk, tile_x):
        values[place(region), : channels + 16] = values[place(region), : channels + 16] + item(region, chunk, tile_x)

    ends = ends_of(order)
    for_groups(order, ends[3], ends[5], MORE, first)
    for_parts(ints, order, rois, ends[4], ends[5], MORE, further)
    copies[0].wait()
    for_groups(order, 0, ends[1], MORE, first)
    for_parts(ints, order, rois, 0, ends[0], MORE, further)
    for_groups(order, ends[1], ends[3], GROUP, narrow)

    def add(at, carry):
        one, two = carry
        for part in range(4):
            lanes = pl.ds(pl.multiple_of((at * 4 + part) * LANES, LANES), LANES)
            value = maps[pl.ds(0, channels), lanes].astype(jnp.float32)
            one, two = one + value, two + value * value
        return one, two

    sums = lax.fori_loop(
        0, ALL_TILES // 4, add, (jnp.zeros((channels, LANES), jnp.float32),) * 2
    )
    sums = [jnp.sum(item.T, axis=0, keepdims=True) for item in sums]
    sums = jnp.broadcast_to(jnp.concatenate(sums, axis=1), (8, LANES))
    low = lax.broadcasted_iota(jnp.int32, (8, LANES), 1) < channels
    turned = pltpu.roll(sums, channels, 1)
    cells = float(ALL_TILES * LANES)
    mean = (jnp.where(low, sums, turned) / cells)[:1]
    square = (jnp.where(low, turned, sums) / cells)[:1]
    inverse = lax.rsqrt(jnp.maximum(square - mean * mean, 0.0) + EPSILON)
    local_out[...] = jnp.concatenate(
        [sums[:1], mean, inverse, jnp.zeros((5, LANES), jnp.float32)], axis=0
    )
    low_lane = lax.broadcasted_iota(jnp.int32, (rois, LANES), 1) < channels
    for at, slot in enumerate(USED):
        lanes = pl.ds(at * LANES, LANES)
        one = values[pl.ds(slot * stride, rois), :]
        two = values[pl.ds((slot + SLOTS) * stride, rois), :]
        value = jnp.where(low_lane, one, pltpu.roll(two, channels, 1))
        total = jnp.where(low_lane, one[:, channels : channels + 1], two[:, channels : channels + 1])
        centred_out[:, lanes] = ((value - mean * total) * inverse).astype(jnp.bfloat16)
        weight_out[:, lanes] = total.astype(jnp.bfloat16)


def unpool_kernel(
    rois, floats, ints, order, base, slope, grads, p2, p3, p4, p5,
    o2, o3, o4, o5, maps, sums, slots, sems, out_sems, finish=None,
):
    channels = base.shape[0]
    stride = rois + SPARE
    planes, outs = (p2, p3, p4, p5), (o2, o3, o4, o5)
    pieces = [(level, at) for level in range(4) for at in range(4 if level == 0 else 1)]

    def fetch(index):
        level, at = pieces[index]
        cells = TILES[level] * LANES // (4 if level == 0 else 1)
        return pltpu.make_async_copy(
            planes[level].at[0, :, pl.ds(at * cells, cells)],
            maps.at[:, pl.ds(FIRST[level] * LANES + at * cells, cells)],
            sems.at[index],
        )

    for index in range(len(pieces)):
        fetch(index).start()
    for slot in range(SLOTS):
        rows = pl.ds(slot * stride, rois)
        slots[pl.ds(slot * stride + rois, SPARE), :] = jnp.zeros((SPARE, LANES), jnp.float32)
        if slot in USED:
            lanes = pl.ds(USED.index(slot) * LANES, LANES)
            slots[rows, :] = grads[:, lanes].astype(jnp.float32)
        else:
            slots[rows, :] = jnp.zeros((rois, LANES), jnp.float32)
    base_v, slope_v = base[...], slope[...]

    def begin(at, carry):
        for part in range(4):
            lanes = pl.ds(pl.multiple_of((at * 4 + part) * LANES, LANES), LANES)
            sums[:, lanes] = base_v + slope_v * maps[:, lanes].astype(jnp.float32)
        return carry

    for index, (level, at) in enumerate(pieces):
        tiles = TILES[level] // (4 if level == 0 else 1)
        start = FIRST[level] + at * tiles
        fetch(index).wait()
        lax.fori_loop(start // 4, (start + tiles) // 4, begin, 0)
    extra = PADDED - ALL_TILES
    if extra:
        sums[:, pl.ds(ALL_TILES * LANES, extra * LANES)] = jnp.zeros(
            (channels, extra * LANES), jnp.float32
        )

    def item(region, chunk, tile_x, span=SPAN):
        kernel_w, first_tile, across = window_weights(
            floats, ints, rois, region, chunk, tile_x, span
        )
        mine = slots[pl.ds(region, SLOTS, stride=stride), :]
        stacked = jnp.concatenate([mine[:, :channels], mine[:, channels:]], axis=0)
        turned = stacked.T.astype(jnp.bfloat16)
        result = jnp.dot(turned, kernel_w, preferred_element_type=jnp.float32)
        for at in range(span):
            lanes = tile_lanes(first_tile, across, at)
            sums[:, lanes] = sums[:, lanes] + result[:, at * LANES : (at + 1) * LANES]

    def narrow(regions):
        for region in regions:
            item(region, None, None, NARROW)

    def first(regions):
        for region in regions:
            item(region, None, None)

    def send(level):
        cells = TILES[level] * LANES
        return pltpu.make_async_copy(
            sums.at[:, pl.ds(FIRST[level] * LANES, cells)], outs[level].at[0], out_sems.at[level]
        )

    ends = ends_of(order)
    for_groups(order, 0, ends[1], MORE, first)
    for_groups(order, ends[1], ends[2], GROUP, narrow)
    for_parts(ints, order, rois, 0, ends[0], MORE, item)
    send(0).start()
    if finish is not None:
        finish()
    for_groups(order, ends[2], ends[3], GROUP, narrow)
    for_groups(order, ends[3], ends[5], MORE, first)
    for_parts(ints, order, rois, ends[4], ends[5], MORE, item)
    for level in range(1, 4):
        send(level).start()
    for level in range(4):
        send(level).wait()


ANY = pl.BlockSpec(memory_space=pl.ANY)
SMEM = pl.BlockSpec(memory_space=pltpu.SMEM)
VMEM = pl.BlockSpec(memory_space=pltpu.VMEM)
LIMIT = 60 * 1024 * 1024


def pool_maps(floats, ints, order, planes, rois):
    channels = planes[0].shape[1]
    flat = jax.ShapeDtypeStruct((rois, WIDE), jnp.bfloat16)
    return pl.pallas_call(
        functools.partial(pool_kernel, rois),
        out_shape=(flat, flat, jax.ShapeDtypeStruct((8, LANES), jnp.float32)),
        in_specs=[SMEM, SMEM, SMEM, ANY, ANY, ANY, ANY],
        out_specs=(VMEM, VMEM, VMEM),
        scratch_shapes=[
            pltpu.VMEM((channels + 16, PADDED * LANES), jnp.bfloat16),
            pltpu.VMEM((2 * SLOTS * (rois + SPARE), LANES), jnp.float32),
            pltpu.SemaphoreType.DMA((4,)),
        ],
        compiler_params=pltpu.CompilerParams(vmem_limit_bytes=LIMIT),
        name="pool",
    )(floats, ints, order, *planes)


def unpool_maps(floats, ints, order, base, slope, grads, planes, rois):
    channels = planes[0].shape[1]
    return pl.pallas_call(
        functools.partial(unpool_kernel, rois),
        out_shape=tuple(jax.ShapeDtypeStruct(plane.shape, jnp.float32) for plane in planes),
        in_specs=[SMEM, SMEM, SMEM, VMEM, VMEM, VMEM, ANY, ANY, ANY, ANY],
        out_specs=(ANY, ANY, ANY, ANY),
        scratch_shapes=[
            pltpu.VMEM((channels, ALL_TILES * LANES), jnp.bfloat16),
            pltpu.VMEM((channels, PADDED * LANES), jnp.float32),
            pltpu.VMEM((SLOTS * (rois + SPARE), LANES), jnp.float32),
            pltpu.SemaphoreType.DMA((7,)),
            pltpu.SemaphoreType.DMA((4,)),
        ],
        compiler_params=pltpu.CompilerParams(vmem_limit_bytes=LIMIT),
        name="unpool",
    )(floats, ints, order, base, slope, grads, *planes)


def local(
    p2, p3, p4, p5, norm_gain, norm_bias, fc6_weight, fc6_bias, fc7_weight, fc7_bias,
    cls_weight, cls_bias, box_weight, box_bias, roi_boxes, roi_level, roi_image,
    canvas_offsets, labels, target_boxes, valid,
):
    channels = p2.shape[1]
    rois = roi_level.shape[0]
    cols = lax.axis_size("col")
    rows = lax.axis_size("roi")
    hidden = fc6_bias.shape[0] * cols
    piece = fc6_bias.shape[0]
    high = rows // cols
    few = channels // high
    planes = (p2, p3, p4, p5)

    block = fc6_weight.reshape(few, 7, 7, piece)
    block = jnp.pad(block, ((0, 0), (0, 0), (0, 1), (0, 0))).reshape(few, 7, 2, 4, piece)
    block = block.transpose(3, 1, 2, 0, 4).reshape(len(USED) * 2, few, piece)
    pairs = [
        ((kappa * high + rho // cols) * cols + rho % cols, rho * cols + kappa)
        for rho in range(rows)
        for kappa in range(cols)
    ]
    block = lax.ppermute(block, ("roi", "col"), pairs)
    wide = lax.all_gather(block, "roi", axis=0)
    wide = wide.reshape(high, cols, len(USED) * 2, few, piece)
    wide = wide.transpose(2, 0, 3, 1, 4).reshape(WIDE, hidden)

    per = fc7_bias.shape[0]
    classes, boxes = cls_weight.shape[1], box_weight.shape[1]
    head = jnp.concatenate([cls_weight, box_weight, fc7_bias[:, None]], axis=1)
    head = jnp.pad(head, ((0, 0), (0, piece - head.shape[1])))
    bias_high = fc6_bias.astype(jnp.bfloat16)
    rest = fc6_bias - bias_high.astype(jnp.float32)
    bias_mid = rest.astype(jnp.bfloat16)
    bias_low = (rest - bias_mid.astype(jnp.float32)).astype(jnp.bfloat16)
    small = jnp.concatenate(
        [fc7_weight, head, jnp.stack([bias_high, bias_mid, bias_low])], axis=0
    )
    deep_rows = fc7_weight.shape[0]
    small = jnp.pad(small, ((0, -small.shape[0] % 16), (0, 0)))
    small = lax.all_gather(small, ("roi", "col"), axis=0)
    deep = small[:, :deep_rows].reshape(rows, cols, deep_rows, piece)
    deep = deep.transpose(0, 2, 1, 3).reshape(hidden, hidden)
    head = small[:, deep_rows : deep_rows + per].reshape(hidden, piece)[:, :LANES]
    bias_seven = head[:, classes + boxes].astype(jnp.float32)
    bias_six = small[:cols, deep_rows + per : deep_rows + per + 3].astype(jnp.float32)
    bias_six = jnp.sum(bias_six, axis=1).reshape(hidden)

    values = [plane[0].astype(jnp.float32) for plane in planes]
    pixel_total = rows * sum(plane.shape[1] for plane in values)
    first_sum = sum(jnp.sum(plane, axis=1) for plane in values)
    second_sum = sum(jnp.sum(plane * plane, axis=1) for plane in values)
    local_valid = jnp.sum(valid.astype(jnp.float32))
    first_sum, second_sum, valid_total = lax.psum((first_sum, second_sum, local_valid), "roi")
    mean = first_sum / pixel_total
    variance = second_sum / pixel_total - mean * mean
    inv_std = lax.rsqrt(variance + EPSILON)
    scale = norm_gain * inv_std

    picks = roi_image[None, :] == jnp.arange(4, dtype=jnp.int32)[:, None]
    shift_x = jnp.sum(jnp.where(picks, canvas_offsets[0][:, None], 0), axis=0)
    shift_y = jnp.sum(jnp.where(picks, canvas_offsets[1][:, None], 0), axis=0)
    floats, ints, order = region_tables(
        (roi_boxes[0] + shift_x).astype(jnp.float32),
        (roi_boxes[1] + shift_y).astype(jnp.float32),
        (roi_boxes[2] + shift_x).astype(jnp.float32),
        (roi_boxes[3] + shift_y).astype(jnp.float32),
        roi_level,
    )

    centred, weight, at_home = pool_maps(floats, ints, order, planes, rois)
    times = WIDE // channels
    weight = weight.astype(jnp.float32)
    centred = centred.astype(jnp.float32) / jnp.tile(at_home[2, :channels], times)
    centred = centred + weight * jnp.tile(at_home[1, :channels] - mean, times)
    pooled = centred * jnp.tile(scale, times) + weight * jnp.tile(norm_bias, times)
    pooled = pooled.astype(jnp.bfloat16)

    partial_six = jnp.dot(pooled, wide, preferred_element_type=jnp.float32).astype(jnp.bfloat16)
    pre_six = lax.psum_scatter(partial_six, "col", scatter_dimension=0, tiled=True)
    pre_six = pre_six.astype(jnp.float32) + bias_six
    hidden_six = jax.nn.silu(pre_six).astype(jnp.bfloat16)
    pre_seven = contract_last(hidden_six, deep) + bias_seven
    hidden_seven = jax.nn.silu(pre_seven).astype(jnp.bfloat16)
    scores = jnp.dot(hidden_seven, head, preferred_element_type=jnp.float32)
    logits = scores[:, :classes] + cls_bias
    deltas = scores[:, classes : classes + boxes] + box_bias

    quarter = rois // cols
    first_row = lax.axis_index("col") * quarter
    mine_labels = lax.dynamic_slice_in_dim(labels, first_row, quarter)
    mine_valid = lax.dynamic_slice_in_dim(valid, first_row, quarter).astype(jnp.float32)
    mine_boxes = lax.dynamic_slice_in_dim(roi_boxes, first_row, quarter, axis=1).astype(jnp.float32)
    mine_goals = lax.dynamic_slice_in_dim(target_boxes, first_row, quarter, axis=1).astype(
        jnp.float32
    )
    prop_width = mine_boxes[2] - mine_boxes[0]
    prop_height = mine_boxes[3] - mine_boxes[1]
    prop_cx = mine_boxes[0] + 0.5 * prop_width
    prop_cy = mine_boxes[1] + 0.5 * prop_height
    goal_width = mine_goals[2] - mine_goals[0]
    goal_height = mine_goals[3] - mine_goals[1]
    goal_cx = mine_goals[0] + 0.5 * goal_width
    goal_cy = mine_goals[1] + 0.5 * goal_height
    targets = jnp.stack(
        [
            10.0 * (goal_cx - prop_cx) / prop_width,
            10.0 * (goal_cy - prop_cy) / prop_height,
            5.0 * jnp.log(goal_width / prop_width),
            5.0 * jnp.log(goal_height / prop_height),
        ],
        axis=1,
    )
    foreground = mine_valid * (mine_labels > 0).astype(jnp.float32)
    top_logit = jnp.max(logits, axis=1, keepdims=True)
    log_total = top_logit[:, 0] + jnp.log(jnp.sum(jnp.exp(logits - top_logit), axis=1))
    onehot = (mine_labels[:, None] == jnp.arange(classes, dtype=jnp.int32)[None, :]).astype(
        jnp.float32
    )
    picked = jnp.sum(onehot * logits, axis=1)
    misfit = deltas - targets
    huber_terms = jnp.where(jnp.abs(misfit) < 1.0, 0.5 * misfit * misfit, jnp.abs(misfit) - 0.5)
    class_part = jnp.sum(mine_valid * (log_total - picked))
    box_part = jnp.sum(foreground * jnp.sum(huber_terms, axis=1))
    centre_x = prop_cx + deltas[:, 0] / 10.0 * prop_width
    centre_y = prop_cy + deltas[:, 1] / 10.0 * prop_height
    new_width = prop_width * jnp.exp(deltas[:, 2] / 5.0)
    new_height = prop_height * jnp.exp(deltas[:, 3] / 5.0)
    decoded = jnp.stack(
        [
            centre_x - 0.5 * new_width,
            centre_y - 0.5 * new_height,
            centre_x + 0.5 * new_width,
            centre_y + 0.5 * new_height,
        ]
    ) / (CANVAS // 2)
    loss_scale = rois * rows / valid_total
    softmax = jnp.exp(logits - log_total[:, None])
    logit_grads = loss_scale * mine_valid[:, None] * (softmax - onehot)
    delta_grads = loss_scale * foreground[:, None] * jnp.clip(misfit, -1.0, 1.0)
    score_grads = jnp.concatenate([logit_grads, delta_grads], axis=1)
    score_grads = jnp.pad(score_grads, ((0, 0), (0, LANES - score_grads.shape[1])))
    score_grads = score_grads.astype(jnp.bfloat16)

    head_term = contract_first(hidden_seven, score_grads)
    hidden_grads = contract_last(score_grads, head)
    pre_seven_grads = (hidden_grads * silu_slope(pre_seven)).astype(jnp.bfloat16)
    deep_term = contract_first(pre_seven_grads, hidden_six)
    six_hidden_grads = jnp.dot(pre_seven_grads, deep, preferred_element_type=jnp.float32)
    pre_six_grads = (six_hidden_grads * silu_slope(pre_six)).astype(jnp.bfloat16)
    six_grads_all = lax.all_gather(pre_six_grads, "col", axis=0, tiled=True)

    wide_term = contract_first(pooled, six_grads_all).astype(jnp.bfloat16)
    wide_term = wide_term.reshape(len(USED) * 2, high, few, cols, piece)
    wide_term = wide_term.transpose(1, 3, 0, 2, 4).reshape(rows * len(USED) * 2, few, piece)
    wide_grad = lax.psum_scatter(wide_term, "roi", scatter_dimension=0, tiled=True)
    wide_grad = lax.ppermute(wide_grad, ("roi", "col"), [(there, here) for here, there in pairs])
    wide_grad = wide_grad.reshape(4, 7, 2, few, piece).transpose(3, 1, 2, 0, 4)
    wide_grad = wide_grad.reshape(few, 7, 8, piece)[:, :, :7].reshape(few * 49, piece)
    fc6_weight_grad = wide_grad.astype(jnp.float32)

    sums = jnp.concatenate(
        [
            jnp.sum(score_grads.astype(jnp.float32), axis=0),
            jnp.stack([class_part, box_part]),
        ]
    )
    everyone = rows * cols
    deep_term = deep_term.reshape(rows, deep_rows, cols, piece).transpose(0, 2, 1, 3)
    deep_term = deep_term.reshape(everyone, deep_rows, piece)
    seven_bias_term = jnp.sum(pre_seven_grads.astype(jnp.float32), axis=0)
    head_term = jnp.concatenate(
        [head_term[:, : classes + boxes], seven_bias_term[:, None]], axis=1
    )
    head_term = jnp.pad(head_term, ((0, 0), (0, piece - head_term.shape[1])))
    head_term = head_term.reshape(everyone, per, piece)
    six_bias_term = jnp.sum(pre_six_grads.astype(jnp.float32), axis=0).reshape(cols, 1, piece)
    six_bias_term = jnp.broadcast_to(six_bias_term[None], (rows, cols, 1, piece))
    six_bias_term = six_bias_term.reshape(everyone, 1, piece)
    sums = jnp.pad(sums, (0, piece - sums.shape[0]))
    sums = jnp.broadcast_to(sums[None, None], (everyone, 1, piece))
    small_term = jnp.concatenate([deep_term, head_term, six_bias_term, sums], axis=1)
    small_term = jnp.pad(small_term, ((0, 0), (0, -small_term.shape[1] % 8), (0, 0)))
    small_grad = lax.psum_scatter(small_term, ("roi", "col"), scatter_dimension=0, tiled=True)[0]
    fc7_weight_grad = small_grad[:deep_rows]
    head_grad = small_grad[deep_rows : deep_rows + per]
    cls_weight_grad = head_grad[:, :classes]
    box_weight_grad = head_grad[:, classes : classes + boxes]
    fc7_bias_grad = head_grad[:, classes + boxes]
    fc6_bias_grad = small_grad[deep_rows + per]
    sums = small_grad[deep_rows + per + 1]
    class_bias_grad = sums[:classes]
    box_bias_grad = sums[classes : classes + boxes]
    cls_loss = sums[LANES] / valid_total
    box_loss = sums[LANES + 1] / valid_total

    pool_grads = contract_last(six_grads_all, wide)
    gain_part = jnp.sum(pool_grads * centred.astype(jnp.float32), axis=0)
    shift_part = jnp.sum(pool_grads * weight.astype(jnp.float32), axis=0)
    gain_part = jnp.sum(gain_part.reshape(-1, channels), axis=0) * inv_std
    shift_part = jnp.sum(shift_part.reshape(-1, channels), axis=0)
    norm_gain_grad, norm_bias_grad = lax.psum((gain_part, shift_part), "roi")

    scaled = (pool_grads * jnp.tile(scale, WIDE // channels)).astype(jnp.bfloat16)
    slope = -scale * inv_std * norm_gain_grad / pixel_total
    base = -scale * norm_bias_grad / pixel_total - slope * mean

    def spread(vector):
        return jnp.broadcast_to(vector[:, None], (channels, LANES))

    input_grads = unpool_maps(floats, ints, order, spread(base), spread(slope), scaled, planes, rois)
    return (
        cls_loss,
        box_loss,
        decoded,
        input_grads[0],
        input_grads[1],
        input_grads[2],
        input_grads[3],
        norm_gain_grad,
        norm_bias_grad,
        fc6_weight_grad,
        fc6_bias_grad,
        fc7_weight_grad,
        fc7_bias_grad,
        cls_weight_grad,
        class_bias_grad,
        box_weight_grad,
        box_bias_grad,
    )


MESH = pl.DeviceIdType.MESH
KEPT = tuple(at for at in range(2 * len(USED)) if at % 2 == 0 or at // 2 < 21)
LEADING = 42
SPARES = tuple(at for at in range(2 * len(USED)) if at not in KEPT)
SMALL = 5


def ring_of(rows):
    return list(range(0, rows, 2)) + list(range(rows - 1, 0, -2))


def position_of(kappa, rows, cols, block, half):
    plane = lax.rem(2 * (block % 2) + block // 2 + kappa, cols)
    return rows - 1 - plane if half else plane


def greet(axis, count):
    barrier = pltpu.get_barrier_semaphore()
    me = lax.axis_index(axis)
    for step in range(1, count):
        pl.semaphore_signal(
            barrier,
            inc=1,
            device_id={axis: lax.rem(me + step, count)},
            device_id_type=MESH,
        )


def met(count):
    pl.semaphore_wait(pltpu.get_barrier_semaphore(), count)


def remote(src, dst, sends, recvs, at, axis, peer):
    return pltpu.make_async_remote_copy(
        src_ref=src,
        dst_ref=dst,
        send_sem=sends.at[at],
        recv_sem=recvs.at[at],
        device_id={axis: peer},
        device_id_type=MESH,
    )


def share(slots, axis, count, sends, recvs, first=0):
    me = lax.axis_index(axis)
    copies = [
        remote(slots.at[me], slots.at[me], sends, recvs, first + step - 1, axis,
               lax.rem(me + step, count))
        for step in range(1, count)
    ]
    for copy in copies:
        copy.start()
    return copies


def neighbours(me):
    core, chip = lax.rem(me, 2), lax.div(me, 2)
    return me + 1 - 2 * core, me + 2 - 4 * chip


class Relay:
    def __init__(self, view, sends, recvs, first):
        me = lax.axis_index("col")
        core, chip = neighbours(me)
        self.near = remote(view(me), view(me), sends, recvs, first, "col", core)
        self.far = remote(view(me), view(me), sends, recvs, first + 1, "col", chip)
        self.passed = remote(view(chip), view(chip), sends, recvs, first + 2, "col", core)

    def start(self):
        self.far.start()
        self.near.start()

    def forward(self):
        self.far.wait_recv()
        self.passed.start()

    def wait(self):
        self.near.wait()
        self.far.wait_send()
        self.passed.wait()


def gather_small_kernel(
    rows, cols, pixels, mine, norms, at_home, out, stats,
    slots, sends, recvs, x_sends, x_recvs, s_sends, s_recvs, sem,
):
    row, col = lax.axis_index("roi"), lax.axis_index("col")
    depth, channels = rows // 2, LANES // 2
    plane, side = lax.div(row, 2), lax.rem(row, 2)
    greet("roi", rows)
    greet("col", cols)
    slots[row] = jnp.concatenate([at_home[:1], norms[1:2], at_home[2:]], axis=0)
    own = pltpu.make_async_copy(mine, out.at[col, plane, side], sem)
    own.start()
    own.wait()
    met(rows + cols - 2)
    sums = share(slots, "roi", rows, s_sends, s_recvs)
    along = [
        remote(mine, out.at[col, plane, side], x_sends, x_recvs, step - 1, "roi",
               lax.rem(plane + step, depth) * 2 + side)
        for step in range(1, depth)
    ]
    across = []
    for step in range(depth):
        block = out.at[col, lax.rem(plane + depth - step, depth), side]
        across.append(
            remote(block, block, x_sends, x_recvs, depth - 1 + step, "roi", row + 1 - 2 * side)
        )
    for copy in along:
        copy.start()
    across[0].start()
    for step in range(1, depth):
        along[step - 1].wait_recv()
        across[step].start()
    relays = [
        Relay(lambda at: out.at[at, :, side], sends, recvs, 0),
        Relay(lambda at: out.at[at, :, 1 - side], sends, recvs, 3),
    ]
    relays[0].start()
    for copy in across:
        copy.wait_recv()
    relays[1].start()
    for copy in sums:
        copy.wait()
    total = slots[0]
    for at in range(1, rows):
        total = total + slots[at]
    turned = pltpu.roll(total, channels, 1)
    low = lax.broadcasted_iota(jnp.int32, total.shape, 1) < channels
    mean = (jnp.where(low, total, turned) / pixels)[:1]
    square = (jnp.where(low, turned, total) / pixels)[:1]
    inv_std = lax.rsqrt(square - mean * mean + EPSILON)
    scale = norms[:1] * inv_std
    spread = 1.0 / at_home[2:3]
    offset = at_home[1:2] - mean
    stats[...] = jnp.concatenate(
        [mean, scale, inv_std, total[1:2], scale * spread, scale * offset + norms[2:3],
         spread, offset],
        axis=0,
    )
    for relay in relays:
        relay.forward()
    for relay in relays:
        relay.wait()
    for copy in along + across:
        copy.wait_send()


def place_wide(pieces, wide, sems, rows, cols):
    few, piece = pieces.shape[2], pieces.shape[3]
    kappa = lax.axis_index("col")
    blocks = []
    for block in range(cols):
        copies = []
        for half in range(2):
            position = position_of(kappa, rows, cols, block, half)
            span, lanes = pl.ds(half * few, few), pl.ds(block * piece, piece)
            place = 2 * block + half
            copies.append(
                pltpu.make_async_copy(
                    pieces.at[position, pl.ds(0, LEADING)],
                    wide.at[pl.ds(0, LEADING), span, lanes],
                    sems.at[place, 0],
                )
            )
            for at in range(LEADING, len(KEPT)):
                copies.append(
                    pltpu.make_async_copy(
                        pieces.at[position, at],
                        wide.at[KEPT[at], span, lanes],
                        sems.at[place, at - LEADING + 1],
                    )
                )
        blocks.append(copies)
    for copies in blocks:
        for copy in copies:
            copy.start()
    for at in SPARES:
        wide[at] = jnp.zeros(wide.shape[1:], wide.dtype)
    return blocks


def head_kernel(
    rows, cols, classes, boxes, facts, score_bias, stats, centred_in, weight_in, small_in, pieces,
    pooled, g6_all, g7_out, hid6_out, hid7_out, gs_out, scores_out, losses_out,
    centred, weight, small, wide, mine, taken, in_sems, sems, sends, recvs, relay_sends, relay_recvs,
):
    me = lax.axis_index("col")
    rois, hidden = g6_all.shape
    quarter, piece = rois // cols, hidden // cols
    greet("col", cols)
    centred_copy = pltpu.make_async_copy(centred_in, centred, in_sems.at[0])
    weight_copy = pltpu.make_async_copy(weight_in, weight, in_sems.at[1])
    small_copy = pltpu.make_async_copy(small_in, small, in_sems.at[2])
    centred_copy.start()
    weight_copy.start()
    blocks = place_wide(pieces, wide, sems, rows, cols)
    small_copy.start()
    centred_copy.wait()
    weight_copy.wait()
    for at in range(len(USED)):
        lanes = slice(at * LANES, (at + 1) * LANES)
        value = centred[:, lanes].astype(jnp.float32) * stats[4:5]
        value = value + weight[:, lanes].astype(jnp.float32) * stats[5:6]
        pooled[:, lanes] = value.astype(jnp.bfloat16)
    met(cols - 1)

    def sending(part, step):
        lanes = pl.ds(part * piece, piece)
        peer = lax.rem(me + step, cols)
        return pltpu.make_async_remote_copy(
            src_ref=mine.at[peer, :, lanes],
            dst_ref=taken.at[step - 1, :, lanes],
            send_sem=sends.at[step - 1, part],
            recv_sem=recvs.at[step - 1, part],
            device_id={"col": peer},
            device_id_type=MESH,
        )

    for part in range(cols):
        for copy in blocks[part]:
            copy.wait()
        lanes = slice(part * piece, (part + 1) * piece)
        weights = wide[:, :, lanes].reshape(WIDE, piece)
        result = jnp.dot(pooled[...], weights, preferred_element_type=jnp.float32)
        result = result.astype(jnp.bfloat16)
        for at in range(cols):
            mine[at, :, lanes] = result[at * quarter : (at + 1) * quarter]
        for step in range(1, cols):
            sending(part, step).start()
    small_copy.wait()
    for part in range(cols):
        for step in range(1, cols):
            sending(part, step).wait()
    pre_six = mine[me].astype(jnp.float32)
    for step in range(1, cols):
        pre_six = pre_six + taken[step - 1].astype(jnp.float32)
    lines = [small[at, 0, 4, :16, LANES:].astype(jnp.float32) for at in range(cols)]
    bias = jnp.concatenate(
        [
            (line[part : part + 1] + line[part + 2 : part + 3]) + line[part + 4 : part + 5]
            for line in lines
            for part in range(2)
        ],
        axis=1,
    )
    pre_six = pre_six + bias
    sigma_six = jax.nn.sigmoid(pre_six)
    hidden_six = (pre_six * sigma_six).astype(jnp.bfloat16)
    hid6_out[...] = hidden_six
    deep = [small[at, :, :4].reshape(hidden, piece) for at in range(cols)]
    head = jnp.concatenate(
        [small[at, row, 4, :, :LANES] for row in range(rows) for at in range(cols)], axis=0
    )
    lane = lax.broadcasted_iota(jnp.int32, (quarter, LANES), 1)
    pick = (lane == classes + boxes).astype(jnp.bfloat16)
    pre_seven = contract_last(pick, head)
    for at in range(cols):
        pre_seven = pre_seven + contract_last(
            hidden_six[:, at * piece : (at + 1) * piece], deep[at]
        )
    sigma_seven = jax.nn.sigmoid(pre_seven)
    hidden_seven = (pre_seven * sigma_seven).astype(jnp.bfloat16)
    hid7_out[...] = hidden_seven
    scores = jnp.dot(hidden_seven, head, preferred_element_type=jnp.float32) + score_bias[...]
    scores_out[...] = scores
    loss_scale = float(rois * rows) / stats[3:4, :1]
    targets, onehot, weights = facts[0], facts[1], facts[2] * loss_scale
    is_class = lane < classes
    top = jnp.max(jnp.where(is_class, scores, -jnp.inf), axis=1, keepdims=True)
    powers = jnp.where(is_class, jnp.exp(jnp.where(is_class, scores - top, 0.0)), 0.0)
    log_total = top + jnp.log(jnp.sum(powers, axis=1, keepdims=True))
    picked = jnp.sum(onehot * scores, axis=1, keepdims=True)
    softmax = jnp.where(is_class, jnp.exp(jnp.where(is_class, scores - log_total, 0.0)), 0.0)
    misfit = jnp.where(is_class, 0.0, scores - targets)
    size = jnp.abs(misfit)
    huber = jnp.where(size < 1.0, 0.5 * misfit * misfit, size - 0.5)
    class_part = jnp.sum(weights[:, :1] * (log_total - picked), axis=0, keepdims=True)
    box_part = jnp.sum(jnp.where(is_class, 0.0, weights * huber), axis=0, keepdims=True)
    grads = jnp.where(is_class, softmax - onehot, jnp.clip(misfit, -1.0, 1.0))
    score_grads = (weights * grads).astype(jnp.bfloat16)
    gs_out[...] = score_grads
    losses_out[...] = jnp.concatenate(
        [
            jnp.broadcast_to(class_part, (1, LANES)),
            box_part,
            jnp.sum(score_grads.astype(jnp.float32), axis=0, keepdims=True),
            jnp.zeros((5, LANES), jnp.float32),
        ],
        axis=0,
    )
    slope_seven = sigma_seven * (1.0 + pre_seven * (1.0 - sigma_seven))
    g7 = (contract_last(score_grads, head) * slope_seven).astype(jnp.bfloat16)
    g7_out[...] = g7
    place = pl.ds(pl.multiple_of(me * quarter, quarter), quarter)
    relays = []
    for at in range(cols):
        lanes = slice(at * piece, (at + 1) * piece)
        back = jnp.dot(g7, deep[at], preferred_element_type=jnp.float32)
        sigma, value = sigma_six[:, lanes], pre_six[:, lanes]
        back = back * (sigma * (1.0 + value * (1.0 - sigma)))
        g6_all[place, lanes] = back.astype(jnp.bfloat16)
        relays.append(
            Relay(
                lambda owner, at=at: g6_all.at[
                    pl.ds(pl.multiple_of(owner * quarter, quarter), quarter),
                    pl.ds(at * piece, piece),
                ],
                relay_sends, relay_recvs, 3 * at,
            )
        )
        relays[-1].start()
    for relay in relays:
        relay.forward()
    for relay in relays:
        relay.wait()


def wide_grad_kernel(
    rows, cols, pooled, g6_all, g7, hid6, hid7, gs, losses,
    terms, g7_all, losses_all,
    hid6_own, buffers, last, extras, head_mine, head_taken, out_sems, sends, recvs,
):
    me = lax.axis_index("col")
    rois, hidden = g6_all.shape
    quarter, piece = rois // cols, hidden // cols
    owned, per = hidden // rows, hidden // (rows * cols)
    few = buffers.shape[2] // 4
    ring = ring_of(rows)
    greet("col", cols)

    def block(at):
        return pl.ds(pl.multiple_of(at * quarter, quarter), quarter)

    g7_all[block(me), :] = g7[...]
    losses_all[me] = losses[...]
    own = pl.ds(pl.multiple_of(me * piece, piece), piece)
    hid6_own[block(me), :] = hid6[:, own]
    head_term = contract_first(hid7[...], gs[...]).astype(jnp.bfloat16)
    for row in range(rows):
        for at in range(cols):
            first = row * owned + at * per
            head_mine[at, row] = head_term[first : first + per]
    met(cols - 1)
    relay = Relay(lambda at: g7_all.at[block(at)], sends, recvs, 0)
    relay.start()
    copies = []
    for step in range(1, cols):
        peer = lax.rem(me + step, cols)
        theirs = pl.ds(pl.multiple_of(peer * piece, piece), piece)
        copies.append(
            remote(hid6.at[:, theirs], hid6_own.at[block(me)], sends, recvs, 2 + step, "col", peer)
        )
        copies.append(
            remote(head_mine.at[peer], head_taken.at[step - 1], sends, recvs, 5 + step, "col", peer)
        )
        copies.append(
            remote(losses, losses_all.at[me], sends, recvs, 8 + step, "col", peer)
        )
    for copy in copies:
        copy.start()

    def leaving(slot, at):
        size = 4 * few
        span = pl.ds(pl.multiple_of(at * size, size), size)
        return pltpu.make_async_copy(buffers.at[slot], terms.at[:, span], out_sems.at[slot])

    def put(result, target, row, parts):
        for column in range(cols):
            columns = slice(column * piece, (column + 1) * piece)
            for half in range(2):
                position = position_of(me, rows, cols, column, half)
                for index, part in enumerate(parts):
                    first = (part * 2 + half) * few
                    target[position, row + index * few : row + (index + 1) * few, :] = result[
                        first : first + few, columns
                    ]

    def step(pair, carry):
        for slot in range(2):
            at = pair * 2 + slot

            @pl.when(pair > 0)
            def _():
                leaving(slot, at - 2).wait()

            lanes = pl.ds(pl.multiple_of(at * 2 * LANES, 2 * LANES), 2 * LANES)
            result = contract_first(pooled[:, lanes], g6_all[...]).astype(jnp.bfloat16)
            put(result, buffers.at[slot], 0, range(4))
            leaving(slot, at).start()
        return carry
    pairs = LEADING // 8
    lax.fori_loop(0, pairs - 1, step, 0)
    relay.forward()
    lax.fori_loop(pairs - 1, pairs, step, 0)
    row = 0
    for at in range(2 * pairs, len(USED) // 2):
        parts = [part for part in range(4) if 4 * at + part in KEPT]
        lanes = slice(at * 2 * LANES, (at + 1) * 2 * LANES)
        result = contract_first(pooled[:, lanes], g6_all[...]).astype(jnp.bfloat16)
        put(result, last, row, parts)
        row += len(parts) * few
    first = 2 * pairs * 4 * few
    rest = pltpu.make_async_copy(last, terms.at[:, pl.ds(first, row)], out_sems.at[2])
    rest.start()
    relay.wait()
    for copy in copies:
        copy.wait()
    deep_term = contract_first(g7_all[...], hid6_own[...]).astype(jnp.bfloat16)
    nothing = jnp.zeros((per, piece - LANES), jnp.bfloat16)
    for position, owner in enumerate(ring):
        extras[position, :owned, :] = deep_term[owner * owned : (owner + 1) * owned]
        total = head_mine[me, owner].astype(jnp.float32)
        for at in range(cols - 1):
            total = total + head_taken[at, owner].astype(jnp.float32)
        extras[position, owned : owned + per, :] = jnp.concatenate(
            [total.astype(jnp.bfloat16), nothing], axis=1
        )
    more = pltpu.make_async_copy(
        extras, terms.at[:, pl.ds(first + row, owned + per)], out_sems.at[3]
    )
    more.start()
    for slot in range(2):
        leaving(slot, 2 * pairs - 2 + slot).wait()
    rest.wait()
    more.wait()


def pool_grad_kernel(
    rows, cols, pixels, g6_all, g7_all, losses_all, centred, weight, stats, pieces,
    grads, totals, base, slope, wide, slots, sems, sends, recvs,
):
    row, col = lax.axis_index("roi"), lax.axis_index("col")
    rois, hidden = g6_all.shape
    channels = base.shape[0]
    piece = hidden // cols
    greet("roi", rows)
    blocks = place_wide(pieces, wide, sems, rows, cols)
    own = pl.ds(pl.multiple_of(col * piece, piece), piece)

    def columns(values):
        return jnp.sum(values.astype(jnp.float32), axis=0, keepdims=True)

    def as_rows(vector):
        return [
            vector[:, at * LANES : (at + 1) * LANES] for at in range(vector.shape[1] // LANES)
        ]

    bias_rows = as_rows(columns(g6_all[:, own])) + as_rows(columns(g7_all[...]))
    losses = losses_all[0]
    for at in range(1, cols):
        losses = losses + losses_all[at]
    for copies in blocks:
        for copy in copies:
            copy.wait()
    scale = stats[1:2]

    def step(at, carry):
        gain, shift = carry
        lanes = pl.ds(pl.multiple_of(at * 2 * LANES, 2 * LANES), 2 * LANES)
        weights = wide[pl.ds(at * 4, 4)].reshape(2 * LANES, hidden)
        result = contract_last(g6_all[...], weights)
        with_centred = result * centred[:, lanes].astype(jnp.float32)
        with_weight = result * weight[:, lanes].astype(jnp.float32)
        both = jnp.concatenate([scale, scale], axis=1)
        grads[:, lanes] = (result * both).astype(jnp.bfloat16)
        for half in range(2):
            part = slice(half * LANES, (half + 1) * LANES)
            gain = gain + jnp.sum(with_centred[:, part].reshape(rois // 8, 8, LANES), axis=0)
            shift = shift + jnp.sum(with_weight[:, part].reshape(rois // 8, 8, LANES), axis=0)
        return gain, shift

    nothing = jnp.zeros((8, LANES), jnp.float32)
    gain, shift = lax.fori_loop(0, len(USED) // 2, step, (nothing, nothing))
    low = lax.broadcasted_iota(jnp.int32, (8, LANES), 1) < channels
    gain = jnp.sum(gain + pltpu.roll(gain, channels, 1), axis=0, keepdims=True)
    shift = jnp.sum(shift + pltpu.roll(shift, channels, 1), axis=0, keepdims=True)
    both = jnp.where(low[:1], stats[6:7] * gain + stats[7:8] * shift, shift)
    lines = [both] + bias_rows + [losses[2:3], losses[:2]]
    count = 1 + len(bias_rows) + 3
    lines.append(jnp.zeros((16 - count, LANES), jnp.float32))
    slots[row] = jnp.concatenate(lines, axis=0)
    met(rows - 1)
    for copy in share(slots, "roi", rows, sends, recvs):
        copy.wait()
    total = slots[0]
    for at in range(1, rows):
        total = total + slots[at]
    gain_grad = total[:1] * stats[2:3]
    totals[...] = jnp.concatenate([total[:15], gain_grad], axis=0)
    slope_row = -stats[1:2] * stats[2:3] * gain_grad / pixels
    shift_grad = pltpu.roll(jnp.broadcast_to(total[:1], (8, LANES)), channels, 1)[:1]
    base_row = -stats[1:2] * shift_grad / pixels - slope_row * stats[:1]
    slope[...] = jnp.broadcast_to(slope_row[:, :channels], (LANES, channels)).T
    base[...] = jnp.broadcast_to(base_row[:, :channels], (LANES, channels)).T


def deliver_kernel(rows, cols, few, term, taken, held, sems, sends, recvs):
    row, col = lax.axis_index("roi"), lax.axis_index("col")
    plane, side = lax.div(row, 2), lax.rem(row, 2)
    chip, core = lax.div(col, 2), lax.rem(col, 2)
    near = {"roi": row, "col": cols - 1 - col}
    crossing = lax.rem(lax.rem(plane + cols - col, cols), 2) != chip
    kappa = jnp.where(crossing, cols - 1 - col, col)
    core_there = lax.div(lax.rem(plane + cols - kappa, cols), 2)
    target = {"roi": kappa * 2 + side, "col": 2 * chip + core_there}
    alone = (kappa == plane) & (core_there == core)
    plane_from = lax.rem(2 * core + chip + plane, cols)
    core_from = jnp.where(lax.div(plane, 2) == chip, lax.rem(plane, 2), 1 - lax.rem(plane, 2))
    source = {"roi": plane_from * 2 + side, "col": 2 * chip + core_from}
    barrier = pltpu.get_barrier_semaphore()

    @pl.when(crossing)
    def _():
        pl.semaphore_signal(barrier, inc=1, device_id=near, device_id_type=MESH)

    @pl.when(jnp.logical_not(alone))
    def _():
        pl.semaphore_signal(barrier, inc=1, device_id=source, device_id_type=MESH)

    @pl.when(crossing | jnp.logical_not(alone))
    def _():
        pl.semaphore_wait(barrier, crossing.astype(jnp.int32) + 1 - alone.astype(jnp.int32))

    count = 7
    size = len(KEPT) // count
    spans = [pl.ds(at * size * few, size * few) for at in range(count)]

    def over(at):
        return pltpu.make_async_remote_copy(
            src_ref=term.at[spans[at]], dst_ref=held.at[spans[at]],
            send_sem=sends.at[0, at], recv_sem=recvs.at[0, at],
            device_id=near, device_id_type=MESH,
        )

    def along(block, at):
        return pltpu.make_async_remote_copy(
            src_ref=block.at[spans[at]], dst_ref=taken.at[spans[at]],
            send_sem=sends.at[1, at], recv_sem=recvs.at[1, at],
            device_id=target, device_id_type=MESH,
        )

    def inside(block, at):
        return pltpu.make_async_copy(block.at[spans[at]], taken.at[spans[at]], sems.at[at])

    def pass_on(block, at):
        @pl.when(alone)
        def _():
            inside(block, at).start()

        @pl.when(jnp.logical_not(alone))
        def _():
            along(block, at).start()

    @pl.when(crossing)
    def _():
        for at in range(count):
            over(at).start()
        for at in range(count):
            over(at).wait_recv()
            pass_on(held, at)

    @pl.when(jnp.logical_not(crossing))
    def _():
        for at in range(count):
            pass_on(term, at)

    for chunk in range(count):
        @pl.when(alone)
        def _():
            inside(held, chunk).wait()

        @pl.when(jnp.logical_not(alone))
        def _():
            along(held, chunk).wait_recv()


    @pl.when(crossing)
    def _():
        for at in range(count):
            over(at).wait_send()

    @pl.when(jnp.logical_not(alone))
    def _():
        for at in range(count):
            along(held, at).wait_send()


def restore_kernel(few, classes, boxes, taken, term, out, deep, scores, deltas, half):
    for part in range(out.shape[1] // LANES):
        lanes = slice(part * LANES, (part + 1) * LANES)
        for index, slot in enumerate(KEPT):
            place = pl.ds(slot // 2 % 7 * 7 + slot // 14 + 4 * (slot % 2), few, stride=49)
            half[part, place, :] = taken[index * few : (index + 1) * few, lanes].astype(
                jnp.float32
            )
        out[:, lanes] = half[part]
    rows = deep.shape[0]
    kept = out.shape[0]
    deep[...] = term[kept : kept + rows, :].astype(jnp.float32)
    head = term[kept + rows :, :LANES].astype(jnp.float32)
    scores[...] = head[:, :classes]
    deltas[...] = pltpu.roll(head, LANES - classes, 1)[:, :boxes]


def unpool_all_kernel(
    rois, rows, cols, classes, boxes, floats, ints, order, base, slope, totals, grads, *rest
):
    planes, outs, few, scratch = rest[:4], rest[4:8], rest[8:16], rest[16:]
    gain, shift, bias_six, bias_seven, bias_cls, bias_box, cls_loss, box_loss = few
    channels, per = gain.shape[0], bias_seven.shape[0]
    row, col = lax.axis_index("roi"), lax.axis_index("col")

    def finish():
        head = totals[:8]
        turned = pltpu.roll(head, channels, 1)
        gain[...] = totals[8:][7, :channels]
        shift[...] = turned[0, :channels]
        wide_lines = bias_six.shape[0] // LANES
        for at in range(wide_lines):
            bias_six[at * LANES : (at + 1) * LANES] = head[1 + at]
        place = (row * cols + col) * per
        line = totals[pl.ds(1 + wide_lines + lax.div(place, LANES), 1), :]
        line = pltpu.roll(
            jnp.broadcast_to(line, (8, LANES)), lax.rem(LANES - lax.rem(place, LANES), LANES), 1
        )
        bias_seven[...] = line[0, :per]
        first = 1 + (cols + 1) * wide_lines
        scores = jnp.broadcast_to(totals[first : first + 1], (8, LANES))
        bias_cls[...] = scores[0, :classes]
        bias_box[...] = pltpu.roll(scores, LANES - classes, 1)[0, :boxes]
        cls_loss[...] = totals[first + 1 : first + 2, :1] / (rois * rows)
        box_loss[...] = jnp.sum(totals[first + 2 : first + 3], axis=1, keepdims=True) / (
            rois * rows
        )

    unpool_kernel(
        rois, floats, ints, order, base, slope, grads, *planes, *outs, *scratch, finish=finish
    )


def unpool_all(
    floats, ints, order, base, slope, totals, grads, planes, rois, rows, cols, classes, boxes,
    piece,
):
    channels = planes[0].shape[1]
    f32 = jnp.float32
    results = pl.pallas_call(
        functools.partial(unpool_all_kernel, rois, rows, cols, classes, boxes),
        out_shape=tuple(shaped(plane.shape, f32) for plane in planes)
        + (
            shaped((channels,), f32),
            shaped((channels,), f32),
            shaped((piece,), f32),
            shaped((piece // rows,), f32),
            shaped((classes,), f32),
            shaped((boxes,), f32),
            shaped((1, 1), f32),
            shaped((1, 1), f32),
        ),
        in_specs=[SMEM] * 3 + [VMEM] * 4 + [ANY] * 4,
        out_specs=(ANY,) * 4 + (VMEM,) * 8,
        scratch_shapes=[
            pltpu.VMEM((channels, ALL_TILES * LANES), jnp.bfloat16),
            pltpu.VMEM((channels, PADDED * LANES), f32),
            pltpu.VMEM((SLOTS * (rois + SPARE), LANES), f32),
            pltpu.SemaphoreType.DMA((7,)),
            pltpu.SemaphoreType.DMA((4,)),
        ],
        compiler_params=pltpu.CompilerParams(vmem_limit_bytes=LIMIT),
        name="unpool",
    )(floats, ints, order, base, slope, totals, grads, *planes)
    return results[:4], results[4:]


def comm_params(number):
    return pltpu.CompilerParams(
        vmem_limit_bytes=LIMIT, collective_id=number, has_side_effects=True
    )


def shaped(shape, dtype):
    return jax.ShapeDtypeStruct(shape, dtype)


def gather_small(mine, norms, at_home, rows, cols, pixels):
    out, stats = pl.pallas_call(
        functools.partial(gather_small_kernel, rows, cols, pixels),
        out_shape=(
            shaped((cols, rows // 2, 2) + mine.shape, mine.dtype),
            shaped((8, LANES), jnp.float32),
        ),
        in_specs=[VMEM] * 3,
        out_specs=(VMEM, VMEM),
        scratch_shapes=[
            pltpu.VMEM((rows, 8, LANES), jnp.float32),
            pltpu.SemaphoreType.DMA((6,)),
            pltpu.SemaphoreType.DMA((6,)),
            pltpu.SemaphoreType.DMA((rows - 1,)),
            pltpu.SemaphoreType.DMA((rows - 1,)),
            pltpu.SemaphoreType.DMA((rows - 1,)),
            pltpu.SemaphoreType.DMA((rows - 1,)),
            pltpu.SemaphoreType.DMA,
        ],
        compiler_params=comm_params(1),
        name="gather_small",
    )(mine, norms, at_home)
    return out.reshape((cols, rows) + mine.shape), stats


def run_head(centred, weight, stats, facts, score_bias, small, pieces, rows, cols, classes, boxes):
    rois, channels = centred.shape[0], LANES // 2
    quarter, hidden = rois // cols, pieces.shape[3] * cols
    bf16, f32 = jnp.bfloat16, jnp.float32
    return pl.pallas_call(
        functools.partial(head_kernel, rows, cols, classes, boxes),
        out_shape=(
            shaped(centred.shape, bf16),
            shaped((rois, hidden), bf16),
            shaped((quarter, hidden), bf16),
            shaped((quarter, hidden), bf16),
            shaped((quarter, hidden), bf16),
            shaped((quarter, LANES), bf16),
            shaped((quarter, LANES), f32),
            shaped((8, LANES), f32),
        ),
        in_specs=[VMEM, VMEM, VMEM, ANY, ANY, ANY, ANY],
        out_specs=(VMEM,) * 8,
        scratch_shapes=[
            pltpu.VMEM(centred.shape, bf16),
            pltpu.VMEM(centred.shape, bf16),
            pltpu.VMEM(small.shape, bf16),
            pltpu.VMEM((2 * len(USED), channels, hidden), bf16),
            pltpu.VMEM((cols, quarter, hidden), bf16),
            pltpu.VMEM((cols - 1, quarter, hidden), bf16),
            pltpu.SemaphoreType.DMA((3,)),
            pltpu.SemaphoreType.DMA((rows, 8)),
            pltpu.SemaphoreType.DMA((cols - 1, cols)),
            pltpu.SemaphoreType.DMA((cols - 1, cols)),
            pltpu.SemaphoreType.DMA((3 * cols,)),
            pltpu.SemaphoreType.DMA((3 * cols,)),
        ],
        compiler_params=comm_params(2),
        name="head",
    )(facts, score_bias, stats, centred, weight, small, pieces)


def wide_grads(pooled, g6_all, g7, hid6, hid7, gs, losses, rows, cols):
    rois, hidden = g6_all.shape
    piece, few = hidden // cols, LANES // 2 // (rows // cols)
    owned, per = hidden // rows, hidden // (rows * cols)
    bf16, f32 = jnp.bfloat16, jnp.float32
    return pl.pallas_call(
        functools.partial(wide_grad_kernel, rows, cols),
        out_shape=(
            shaped((rows, len(KEPT) * few + owned + per, piece), bf16),
            shaped((rois, hidden), bf16),
            shaped((cols, 8, LANES), f32),
        ),
        in_specs=[VMEM] * 7,
        out_specs=(ANY, VMEM, VMEM),
        scratch_shapes=[
            pltpu.VMEM((rois, piece), bf16),
            pltpu.VMEM((2, rows, 4 * few, piece), bf16),
            pltpu.VMEM((rows, (len(KEPT) - LEADING // 8 * 8) * few, piece), bf16),
            pltpu.VMEM((rows, owned + per, piece), bf16),
            pltpu.VMEM((cols, rows, per, LANES), bf16),
            pltpu.VMEM((cols - 1, rows, per, LANES), bf16),
            pltpu.SemaphoreType.DMA((4,)),
            pltpu.SemaphoreType.DMA((12,)),
            pltpu.SemaphoreType.DMA((12,)),
        ],
        compiler_params=comm_params(3),
        name="wide_grads",
    )(pooled, g6_all, g7, hid6, hid7, gs, losses)


def pool_grads(g6_all, g7_all, losses_all, centred, weight, stats, pieces, rows, cols, pixels):
    rois, hidden = g6_all.shape
    channels = LANES // 2
    bf16, f32 = jnp.bfloat16, jnp.float32
    return pl.pallas_call(
        functools.partial(pool_grad_kernel, rows, cols, pixels),
        out_shape=(
            shaped((rois, WIDE), bf16),
            shaped((16, LANES), f32),
            shaped((channels, LANES), f32),
            shaped((channels, LANES), f32),
        ),
        in_specs=[VMEM] * 6 + [ANY],
        out_specs=(VMEM,) * 4,
        scratch_shapes=[
            pltpu.VMEM((2 * len(USED), channels, hidden), bf16),
            pltpu.VMEM((rows, 16, LANES), f32),
            pltpu.SemaphoreType.DMA((rows, 8)),
            pltpu.SemaphoreType.DMA((rows - 1,)),
            pltpu.SemaphoreType.DMA((rows - 1,)),
        ],
        compiler_params=comm_params(4),
        name="pool_grads",
    )(g6_all, g7_all, losses_all, centred, weight, stats, pieces)


def deliver(term, rows, cols, few):
    piece, kept = term.shape[1], len(KEPT) * few
    return pl.pallas_call(
        functools.partial(deliver_kernel, rows, cols, few),
        out_shape=shaped((kept, piece), term.dtype),
        in_specs=[ANY],
        out_specs=VMEM,
        scratch_shapes=[
            pltpu.VMEM((kept, piece), term.dtype),
            pltpu.SemaphoreType.DMA((7,)),
            pltpu.SemaphoreType.DMA((2, 7)),
            pltpu.SemaphoreType.DMA((2, 7)),
        ],
        compiler_params=comm_params(5),
        name="deliver",
    )(term)


def restore(taken, term, few, deep_rows, per, classes, boxes):
    kept, piece = taken.shape
    f32 = jnp.float32
    return pl.pallas_call(
        functools.partial(restore_kernel, few, classes, boxes),
        out_shape=(
            shaped((kept, piece), f32),
            shaped((deep_rows, piece), f32),
            shaped((per, classes), f32),
            shaped((per, boxes), f32),
        ),
        in_specs=[VMEM, VMEM],
        out_specs=(VMEM,) * 4,
        scratch_shapes=[pltpu.VMEM((piece // LANES, kept, LANES), f32)],
        compiler_params=pltpu.CompilerParams(vmem_limit_bytes=LIMIT),
        name="restore",
    )(taken, term)


def targets_of(mine_boxes, mine_goals):
    prop_width = mine_boxes[2] - mine_boxes[0]
    prop_height = mine_boxes[3] - mine_boxes[1]
    prop_cx = mine_boxes[0] + 0.5 * prop_width
    prop_cy = mine_boxes[1] + 0.5 * prop_height
    goal_width = mine_goals[2] - mine_goals[0]
    goal_height = mine_goals[3] - mine_goals[1]
    goal_cx = mine_goals[0] + 0.5 * goal_width
    goal_cy = mine_goals[1] + 0.5 * goal_height
    return jnp.stack(
        [
            10.0 * (goal_cx - prop_cx) / prop_width,
            10.0 * (goal_cy - prop_cy) / prop_height,
            5.0 * jnp.log(goal_width / prop_width),
            5.0 * jnp.log(goal_height / prop_height),
        ],
        axis=1,
    )


def decode(mine_boxes, deltas):
    prop_width = mine_boxes[2] - mine_boxes[0]
    prop_height = mine_boxes[3] - mine_boxes[1]
    prop_cx = mine_boxes[0] + 0.5 * prop_width
    prop_cy = mine_boxes[1] + 0.5 * prop_height
    centre_x = prop_cx + deltas[:, 0] / 10.0 * prop_width
    centre_y = prop_cy + deltas[:, 1] / 10.0 * prop_height
    new_width = prop_width * jnp.exp(deltas[:, 2] / 5.0)
    new_height = prop_height * jnp.exp(deltas[:, 3] / 5.0)
    return jnp.stack(
        [
            centre_x - 0.5 * new_width,
            centre_y - 0.5 * new_height,
            centre_x + 0.5 * new_width,
            centre_y + 0.5 * new_height,
        ]
    ) / (CANVAS // 2)


def local_near(
    p2, p3, p4, p5, norm_gain, norm_bias, fc6_weight, fc6_bias, fc7_weight, fc7_bias,
    cls_weight, cls_bias, box_weight, box_bias, roi_boxes, roi_level, roi_image,
    canvas_offsets, labels, target_boxes, valid,
):
    channels = p2.shape[1]
    rois = roi_level.shape[0]
    cols = lax.axis_size("col")
    rows = lax.axis_size("roi")
    piece = fc6_bias.shape[0]
    high = rows // cols
    few = channels // high
    planes = (p2, p3, p4, p5)
    pixels = rows * sum(plane.shape[2] for plane in planes)
    ring = ring_of(rows)
    per = fc7_bias.shape[0]
    classes, boxes = cls_weight.shape[1], box_weight.shape[1]
    bf16, f32 = jnp.bfloat16, jnp.float32

    block = fc6_weight.reshape(few, 7, 7, piece)
    block = jnp.pad(block, ((0, 0), (0, 0), (0, 1), (0, 0))).reshape(few, 7, 2, 4, piece)
    block = block.transpose(3, 1, 2, 0, 4).reshape(2 * len(USED), few, piece)
    block = jnp.concatenate([block[:LEADING], block[LEADING::2]])
    pairs = []
    for kappa in range(cols):
        for block_at in range(cols):
            for half in range(high):
                plane = (2 * (block_at % 2) + block_at // 2 + kappa) % cols
                source = (kappa * high + half) * cols + block_at
                pairs.append((source, (plane * high + half) * cols + kappa))
    block = lax.ppermute(block, ("roi", "col"), pairs)

    head = jnp.concatenate([cls_weight, box_weight, fc7_bias[:, None]], axis=1)
    head = jnp.pad(head, ((0, 0), (0, piece - head.shape[1])))
    bias_high = fc6_bias.astype(bf16)
    rest = fc6_bias - bias_high.astype(f32)
    bias_mid = rest.astype(bf16)
    bias_low = (rest - bias_mid.astype(f32)).astype(bf16)
    bias = jnp.concatenate([item.reshape(2, LANES) for item in (bias_high, bias_mid, bias_low)])
    bias = jnp.pad(bias, ((0, per - bias.shape[0]), (0, 0)))
    head = jnp.concatenate([head[:, :LANES], bias], axis=1)
    small = jnp.concatenate([fc7_weight, head], axis=0).reshape(SMALL, few, piece)

    def twice(vector):
        return jnp.concatenate([vector, vector])[None]

    count = jnp.sum(valid.astype(f32))
    norms = jnp.concatenate(
        [twice(norm_gain), jnp.full((1, LANES), count), twice(norm_bias), jnp.zeros((5, LANES), f32)]
    )

    picks = roi_image[None, :] == jnp.arange(4, dtype=jnp.int32)[:, None]
    shift_x = jnp.sum(jnp.where(picks, canvas_offsets[0][:, None], 0), axis=0)
    shift_y = jnp.sum(jnp.where(picks, canvas_offsets[1][:, None], 0), axis=0)
    floats, ints, order = region_tables(
        (roi_boxes[0] + shift_x).astype(f32),
        (roi_boxes[1] + shift_y).astype(f32),
        (roi_boxes[2] + shift_x).astype(f32),
        (roi_boxes[3] + shift_y).astype(f32),
        roi_level,
    )
    block = lax.optimization_barrier((block, floats, order))[0]
    pieces = lax.all_gather(block, "roi", axis=0, axis_index_groups=[ring])
    centred, weight, at_home = pool_maps(floats, ints, order, planes, rois)

    quarter = rois // cols
    first_row = lax.axis_index("col") * quarter
    mine_labels = lax.dynamic_slice_in_dim(labels, first_row, quarter)
    mine_valid = lax.dynamic_slice_in_dim(valid, first_row, quarter).astype(f32)
    mine_boxes = lax.dynamic_slice_in_dim(roi_boxes, first_row, quarter, axis=1).astype(f32)
    mine_goals = lax.dynamic_slice_in_dim(target_boxes, first_row, quarter, axis=1).astype(f32)
    foreground = mine_valid * (mine_labels > 0).astype(f32)
    lane = jnp.arange(LANES, dtype=jnp.int32)[None, :]
    after = LANES - classes - boxes
    facts = jnp.stack(
        [
            jnp.pad(targets_of(mine_boxes, mine_goals), ((0, 0), (classes, after))),
            (mine_labels[:, None] == lane).astype(f32),
            jnp.where(
                lane < classes,
                mine_valid[:, None],
                jnp.where(lane < classes + boxes, foreground[:, None], 0.0),
            ),
        ]
    )
    score_bias = jnp.pad(jnp.concatenate([cls_bias, box_bias]), (0, after))[None]
    small, facts, score_bias, _ = lax.optimization_barrier((small, facts, score_bias, at_home))
    small, stats = gather_small(small, norms, at_home, rows, cols, float(pixels))
    pooled, g6_all, g7, hid6, hid7, gs, scores, losses = run_head(
        centred, weight, stats, facts, score_bias, small, pieces, rows, cols, classes, boxes
    )
    decoded = decode(mine_boxes, scores[:, classes : classes + boxes])

    terms, g7_all, losses_all = wide_grads(
        pooled, g6_all, g7, hid6, hid7, gs, losses, rows, cols
    )
    wide_rows = terms.shape[1]
    term = lax.psum_scatter(
        terms.reshape(rows * wide_rows, piece), "roi", scatter_dimension=0, tiled=True,
        axis_index_groups=[ring],
    )
    grads, totals, base, slope = pool_grads(
        g6_all, g7_all, losses_all, centred, weight, stats, pieces, rows, cols,
        float(pixels),
    )
    input_grads, few_grads = unpool_all(
        floats, ints, order, base, slope, totals, grads, planes, rois, rows, cols, classes, boxes,
        piece,
    )
    term = lax.optimization_barrier((term, input_grads[3]))[0]
    fc6_weight_grad, fc7_weight_grad, cls_weight_grad, box_weight_grad = restore(
        deliver(term, rows, cols, few), term, few, fc7_weight.shape[0], per, classes, boxes
    )
    (
        norm_gain_grad, norm_bias_grad, fc6_bias_grad, fc7_bias_grad, class_bias_grad,
        box_bias_grad, cls_loss, box_loss,
    ) = few_grads
    return (
        cls_loss[0, 0],
        box_loss[0, 0],
        decoded,
        *input_grads,
        norm_gain_grad,
        norm_bias_grad,
        fc6_weight_grad,
        fc6_bias_grad,
        fc7_weight_grad,
        fc7_bias_grad,
        cls_weight_grad,
        class_bias_grad,
        box_weight_grad,
        box_bias_grad,
    )


def solution(mesh):
    near = mesh.shape["roi"] == 2 * mesh.shape["col"] and mesh.shape["col"] == 4
    return jax.shard_map(
        local_near if near else local,
        mesh=mesh,
        in_specs=(
            P("roi", "col", None),
            P("roi", "col", None),
            P("roi", "col", None),
            P("roi", "col", None),
            P("col"),
            P("col"),
            P("roi", "col"),
            P("col"),
            P("roi", "col"),
            P(("roi", "col")),
            P(("roi", "col"), None),
            P(),
            P(("roi", "col"), None),
            P(),
            P(None, "roi"),
            P("roi"),
            P("roi"),
            P(None, "roi"),
            P("roi"),
            P(None, "roi"),
            P("roi"),
        ),
        out_specs=(
            P(),
            P(),
            P(None, ("roi", "col")),
            P("roi", "col", None),
            P("roi", "col", None),
            P("roi", "col", None),
            P("roi", "col", None),
            P("col"),
            P("col"),
            P("roi", "col"),
            P("col"),
            P("roi", "col"),
            P(("roi", "col")),
            P(("roi", "col"), None),
            P(),
            P(("roi", "col"), None),
            P(),
        ),
        check_vma=False,
    )
```

```python
import functools
import math

import jax
import jax.numpy as jnp
from jax import lax
from jax.experimental import pallas as pl
from jax.experimental.pallas import tpu as pltpu
from jax.sharding import PartitionSpec as P

CANVAS = 1024
EPSILON = 1e-05
LANES = 128
SPAN = 10
NARROW = 8
GROUP = 16
MORE = 16
SPARE = 8
SIDES = tuple(CANVAS // (4 * 2**level) for level in range(4))
TILES = tuple(side * side // LANES for side in SIDES)
FIRST = tuple(sum(TILES[:level]) for level in range(4))
ALL_TILES = sum(TILES)
PADDED = ALL_TILES + max(SPAN - min(TILES), 0)
SLOTS = 32
USED = tuple(slot for slot in range(SLOTS) if slot % 8 < 7)
WIDE = len(USED) * LANES
F32_FIELDS = 7
I32_FIELDS = 6


def silu_slope(values):
    sigma = jax.nn.sigmoid(values)
    return sigma * (1.0 + values * (1.0 - sigma))


def contract_first(left_m, right_m):
    return lax.dot_general(
        left_m, right_m, (((0,), (0,)), ((), ())), preferred_element_type=jnp.float32
    )


def contract_last(left_m, right_m):
    return lax.dot_general(
        left_m, right_m, (((1,), (1,)), ((), ())), preferred_element_type=jnp.float32
    )


def region_tables(left, top, right, bottom, level):
    def by_level(values):
        chosen = jnp.full(level.shape, values[0])
        for at in range(1, 4):
            chosen = jnp.where(level == at, values[at], chosen)
        return chosen

    step = by_level([4.0 * 2**at for at in range(4)])
    side = by_level(list(SIDES))
    rows_log = by_level([(max(LANES // n, 1)).bit_length() - 1 for n in SIDES])
    across = by_level([max(n // LANES, 1) for n in SIDES])
    x_anchor, x_extent = left / step - 0.5, (right - left) / step
    y_anchor, y_extent = top / step - 0.5, (bottom - top) / step

    def window(anchor, extent):
        low = jnp.floor(anchor + extent * (0.5 / 14.0)).astype(jnp.int32)
        high = jnp.floor(anchor + extent * (13.5 / 14.0)).astype(jnp.int32) + 1
        return jnp.clip(low, 0, side - 1), jnp.clip(high, 0, side - 1)

    y_low, y_high = window(y_anchor, y_extent)
    x_low, x_high = window(x_anchor, x_extent)
    group_low, group_high = y_low >> rows_log, y_high >> rows_log
    tile_x = x_low // LANES
    tiles_x = x_high // LANES - tile_x + 1
    narrow = (group_high - group_low < NARROW) & (tiles_x == 1)
    chunks = jnp.where(narrow, 1, (group_high - group_low + SPAN) // SPAN)
    taken = jnp.where(narrow, NARROW, chunks * SPAN)
    group = jnp.maximum(jnp.minimum(group_low, (side >> rows_log) - taken), 0)
    first_tile = by_level(list(FIRST)) + group * across + tile_x
    mask = jnp.minimum(side, LANES) - 1
    shift = 7 - rows_log
    rows_per = (1 << rows_log).astype(jnp.float32)
    nothing = jnp.zeros((SPARE,), jnp.int32)
    parts = chunks * tiles_x
    kind = jnp.where(narrow, 0, jnp.where(parts > 1, 2, 1))
    key = jnp.where(level > 0, 3 + kind, 2 - kind)
    rois = level.shape[0]
    at = jnp.arange(rois, dtype=jnp.int32)
    before = (key[None, :] < key[:, None]) | (
        (key[None, :] == key[:, None]) & (at[None, :] < at[:, None])
    )
    rank = jnp.sum(before.astype(jnp.int32), axis=1)
    order = jnp.sum(jnp.where(rank[None, :] == at[:, None], at[None, :], 0), axis=1)
    order = jnp.concatenate([order, jnp.full((GROUP,), rois, jnp.int32)])
    ends = jnp.stack([jnp.sum((key <= last).astype(jnp.int32)) for last in range(6)])
    floats = jnp.stack(
        [
            x_anchor,
            x_extent,
            y_anchor,
            y_extent,
            (tile_x * LANES).astype(jnp.float32),
            group.astype(jnp.float32) * rows_per,
            rows_per,
        ]
    ).astype(jnp.float32)
    ints = jnp.stack([first_tile, across, mask, shift, parts, tiles_x]).astype(jnp.int32)
    away = jnp.full((F32_FIELDS, SPARE), -1e6, jnp.float32)
    floats = jnp.concatenate([floats, away], axis=1)
    ints = jnp.concatenate([ints, jnp.broadcast_to(nothing, (I32_FIELDS, SPARE))], axis=1)
    return floats.reshape(-1), ints.reshape(-1), jnp.concatenate([order, ends])


def window_weights(floats, ints, rois, region, chunk, tile_x, span=SPAN):
    rois = rois + SPARE
    x_anchor, x_extent, y_anchor, y_extent, x_origin, y_origin, rows_per = (
        floats[at * rois + region] for at in range(F32_FIELDS)
    )
    first_tile, across, mask, shift = (ints[at * rois + region] for at in range(4))
    if chunk is not None:
        first_tile = first_tile + chunk * (SPAN * across) + tile_x
        x_origin = x_origin + (tile_x * LANES).astype(jnp.float32)
        y_origin = y_origin + (chunk * SPAN).astype(jnp.float32) * rows_per
    lane = lax.broadcasted_iota(jnp.int32, (8, LANES), 1)
    bin_at = lax.broadcasted_iota(jnp.int32, (8, LANES), 0)
    x_cell = (lane & mask).astype(jnp.float32) + x_origin
    y_cell = lax.shift_right_logical(lane, jnp.broadcast_to(shift, lane.shape)).astype(
        jnp.float32
    ) + y_origin
    part = jnp.where(bin_at < 7, (2.0 * bin_at.astype(jnp.float32) + 0.5) / 14.0, -1e6)
    near = y_anchor + y_extent * part - y_cell
    far = y_anchor + y_extent * (part + 1.0 / 14.0) - y_cell

    def tent(distance):
        return jnp.maximum(1.0 - jnp.abs(distance), 0.0)

    across_w = []
    for j in range(7):
        one = x_anchor + x_extent * ((2 * j + 0.5) / 14.0)
        two = x_anchor + x_extent * ((2 * j + 1.5) / 14.0)
        across_w.append(0.25 * (tent(one - x_cell) + tent(two - x_cell)))
    across_w.append(jnp.zeros((8, LANES), jnp.float32))
    packed = [
        jnp.concatenate([across_w[2 * at], across_w[2 * at + 1]], axis=0).astype(jnp.bfloat16)
        for at in range(4)
    ]
    blocks = []
    for at in range(span):
        offset = rows_per * float(at)
        down = tent(near - offset) + tent(far - offset)
        both = jnp.concatenate([down, down], axis=0).astype(jnp.bfloat16)
        blocks.append(jnp.concatenate([both * item for item in packed], axis=0))
    return jnp.concatenate(blocks, axis=1), first_tile, across


def tile_lanes(first_tile, across, at):
    return pl.ds(pl.multiple_of((first_tile + at * across) * LANES, LANES), LANES)


def for_groups(order, start, stop, size, body):
    def step(at, carry):
        first = start + at * size
        inside = [first + index < stop for index in range(size)]
        spare = order.shape[0] - 7
        places = [
            jnp.where(good, first + index, spare) for index, good in enumerate(inside)
        ]
        body([order[place] for place in places])
        return carry

    lax.fori_loop(0, (stop - start + size - 1) // size, step, 0)


def for_parts(ints, order, rois, start, stop, size, body):
    stride = rois + SPARE

    def second(regions):
        for region in regions:
            tiles_x = ints[5 * stride + region]
            wide = (tiles_x > 1).astype(jnp.int32)
            body(region, 1 - wide, wide)

    for_groups(order, start, stop, size, second)

    def later(at, carry):
        region = order[at]
        tiles_x = ints[5 * stride + region]

        def part(index, inner):
            chunk = index // tiles_x
            body(region, chunk, index - chunk * tiles_x)
            return inner

        return lax.fori_loop(2, ints[4 * stride + region], part, carry)

    lax.fori_loop(start, stop, later, 0)


def ends_of(order):
    size = order.shape[0]
    return [order[size - 6 + at] for at in range(6)]


def pool_kernel(
    rois, floats, ints, order, p2, p3, p4, p5,
    centred_out, weight_out, local_out, maps, values, sems,
):
    channels = p2.shape[1]
    stride = rois + SPARE
    copies = []
    for level, plane in enumerate((p2, p3, p4, p5)):
        cells = TILES[level] * LANES
        copies.append(
            pltpu.make_async_copy(
                plane.at[0],
                maps.at[pl.ds(0, channels), pl.ds(FIRST[level] * LANES, cells)],
                sems.at[level],
            )
        )
    for copy in copies[::-1]:
        copy.start()
    ones = jnp.ones((16, 8 * LANES), jnp.bfloat16)

    def fill(at, carry):
        lanes = pl.ds(pl.multiple_of(at * 8 * LANES, 8 * LANES), 8 * LANES)
        maps[pl.ds(channels, 16), lanes] = ones
        return carry

    lax.fori_loop(0, ALL_TILES // 8, fill, 0)
    extra = PADDED - ALL_TILES
    if extra:
        maps[:, pl.ds(ALL_TILES * LANES, extra * LANES)] = jnp.zeros(
            (channels + 16, extra * LANES), jnp.bfloat16
        )
    for copy in copies[1:]:
        copy.wait()

    def item(region, chunk, tile_x, span=SPAN):
        kernel_w, first_tile, across = window_weights(
            floats, ints, rois, region, chunk, tile_x, span
        )
        cells = jnp.concatenate(
            [maps[:, tile_lanes(first_tile, across, at)] for at in range(span)], axis=1
        )
        return contract_last(kernel_w, cells)

    def place(region):
        return pl.ds(region, 2 * SLOTS, stride=stride)

    def narrow(regions):
        for region in regions:
            values[place(region), : channels + 16] = item(region, None, None, NARROW)

    def first(regions):
        for region in regions:
            values[place(region), : channels + 16] = item(region, None, None)

    def further(region, chunk, tile_x):
        values[place(region), : channels + 16] = values[place(region), : channels + 16] + item(region, chunk, tile_x)

    ends = ends_of(order)
    for_groups(order, ends[3], ends[5], MORE, first)
    for_parts(ints, order, rois, ends[4], ends[5], MORE, further)
    copies[0].wait()
    for_groups(order, 0, ends[1], MORE, first)
    for_parts(ints, order, rois, 0, ends[0], MORE, further)
    for_groups(order, ends[1], ends[3], GROUP, narrow)

    def add(at, carry):
        one, two = carry
        for part in range(4):
            lanes = pl.ds(pl.multiple_of((at * 4 + part) * LANES, LANES), LANES)
            value = maps[pl.ds(0, channels), lanes].astype(jnp.float32)
            one, two = one + value, two + value * value
        return one, two

    sums = lax.fori_loop(
        0, ALL_TILES // 4, add, (jnp.zeros((channels, LANES), jnp.float32),) * 2
    )
    sums = [jnp.sum(item.T, axis=0, keepdims=True) for item in sums]
    sums = jnp.broadcast_to(jnp.concatenate(sums, axis=1), (8, LANES))
    low = lax.broadcasted_iota(jnp.int32, (8, LANES), 1) < channels
    turned = pltpu.roll(sums, channels, 1)
    cells = float(ALL_TILES * LANES)
    mean = (jnp.where(low, sums, turned) / cells)[:1]
    square = (jnp.where(low, turned, sums) / cells)[:1]
    inverse = lax.rsqrt(jnp.maximum(square - mean * mean, 0.0) + EPSILON)
    local_out[...] = jnp.concatenate(
        [sums[:1], mean, inverse, jnp.zeros((5, LANES), jnp.float32)], axis=0
    )
    low_lane = lax.broadcasted_iota(jnp.int32, (rois, LANES), 1) < channels
    for at, slot in enumerate(USED):
        lanes = pl.ds(at * LANES, LANES)
        one = values[pl.ds(slot * stride, rois), :]
        two = values[pl.ds((slot + SLOTS) * stride, rois), :]
        value = jnp.where(low_lane, one, pltpu.roll(two, channels, 1))
        total = jnp.where(low_lane, one[:, channels : channels + 1], two[:, channels : channels + 1])
        centred_out[:, lanes] = ((value - mean * total) * inverse).astype(jnp.bfloat16)
        weight_out[:, lanes] = total.astype(jnp.bfloat16)


def unpool_kernel(
    rois, floats, ints, order, base, slope, grads, p2, p3, p4, p5,
    o2, o3, o4, o5, maps, sums, slots, sems, out_sems, finish=None,
):
    channels = base.shape[0]
    stride = rois + SPARE
    planes, outs = (p2, p3, p4, p5), (o2, o3, o4, o5)
    pieces = [(level, at) for level in range(4) for at in range(4 if level == 0 else 1)]

    def fetch(index):
        level, at = pieces[index]
        cells = TILES[level] * LANES // (4 if level == 0 else 1)
        return pltpu.make_async_copy(
            planes[level].at[0, :, pl.ds(at * cells, cells)],
            maps.at[:, pl.ds(FIRST[level] * LANES + at * cells, cells)],
            sems.at[index],
        )

    for index in range(len(pieces)):
        fetch(index).start()
    for slot in range(SLOTS):
        rows = pl.ds(slot * stride, rois)
        slots[pl.ds(slot * stride + rois, SPARE), :] = jnp.zeros((SPARE, LANES), jnp.float32)
        if slot in USED:
            lanes = pl.ds(USED.index(slot) * LANES, LANES)
            slots[rows, :] = grads[:, lanes].astype(jnp.float32)
        else:
            slots[rows, :] = jnp.zeros((rois, LANES), jnp.float32)
    base_v, slope_v = base[...], slope[...]

    def begin(at, carry):
        for part in range(4):
            lanes = pl.ds(pl.multiple_of((at * 4 + part) * LANES, LANES), LANES)
            sums[:, lanes] = base_v + slope_v * maps[:, lanes].astype(jnp.float32)
        return carry

    for index, (level, at) in enumerate(pieces):
        tiles = TILES[level] // (4 if level == 0 else 1)
        start = FIRST[level] + at * tiles
        fetch(index).wait()
        lax.fori_loop(start // 4, (start + tiles) // 4, begin, 0)
    extra = PADDED - ALL_TILES
    if extra:
        sums[:, pl.ds(ALL_TILES * LANES, extra * LANES)] = jnp.zeros(
            (channels, extra * LANES), jnp.float32
        )

    def item(region, chunk, tile_x, span=SPAN):
        kernel_w, first_tile, across = window_weights(
            floats, ints, rois, region, chunk, tile_x, span
        )
        mine = slots[pl.ds(region, SLOTS, stride=stride), :]
        stacked = jnp.concatenate([mine[:, :channels], mine[:, channels:]], axis=0)
        turned = stacked.T.astype(jnp.bfloat16)
        result = jnp.dot(turned, kernel_w, preferred_element_type=jnp.float32)
        for at in range(span):
            lanes = tile_lanes(first_tile, across, at)
            sums[:, lanes] = sums[:, lanes] + result[:, at * LANES : (at + 1) * LANES]

    def narrow(regions):
        for region in regions:
            item(region, None, None, NARROW)

    def first(regions):
        for region in regions:
            item(region, None, None)

    def send(level):
        cells = TILES[level] * LANES
        return pltpu.make_async_copy(
            sums.at[:, pl.ds(FIRST[level] * LANES, cells)], outs[level].at[0], out_sems.at[level]
        )

    ends = ends_of(order)
    for_groups(order, 0, ends[1], MORE, first)
    for_groups(order, ends[1], ends[2], GROUP, narrow)
    for_parts(ints, order, rois, 0, ends[0], MORE, item)
    send(0).start()
    if finish is not None:
        finish()
    for_groups(order, ends[2], ends[3], GROUP, narrow)
    for_groups(order, ends[3], ends[5], MORE, first)
    for_parts(ints, order, rois, ends[4], ends[5], MORE, item)
    for level in range(1, 4):
        send(level).start()
    for level in range(4):
        send(level).wait()


ANY = pl.BlockSpec(memory_space=pl.ANY)
SMEM = pl.BlockSpec(memory_space=pltpu.SMEM)
VMEM = pl.BlockSpec(memory_space=pltpu.VMEM)
LIMIT = 60 * 1024 * 1024


def pool_maps(floats, ints, order, planes, rois):
    channels = planes[0].shape[1]
    flat = jax.ShapeDtypeStruct((rois, WIDE), jnp.bfloat16)
    return pl.pallas_call(
        functools.partial(pool_kernel, rois),
        out_shape=(flat, flat, jax.ShapeDtypeStruct((8, LANES), jnp.float32)),
        in_specs=[SMEM, SMEM, SMEM, ANY, ANY, ANY, ANY],
        out_specs=(VMEM, VMEM, VMEM),
        scratch_shapes=[
            pltpu.VMEM((channels + 16, PADDED * LANES), jnp.bfloat16),
            pltpu.VMEM((2 * SLOTS * (rois + SPARE), LANES), jnp.float32),
            pltpu.SemaphoreType.DMA((4,)),
        ],
        compiler_params=pltpu.CompilerParams(vmem_limit_bytes=LIMIT),
        name="pool",
    )(floats, ints, order, *planes)


def unpool_maps(floats, ints, order, base, slope, grads, planes, rois):
    channels = planes[0].shape[1]
    return pl.pallas_call(
        functools.partial(unpool_kernel, rois),
        out_shape=tuple(jax.ShapeDtypeStruct(plane.shape, jnp.float32) for plane in planes),
        in_specs=[SMEM, SMEM, SMEM, VMEM, VMEM, VMEM, ANY, ANY, ANY, ANY],
        out_specs=(ANY, ANY, ANY, ANY),
        scratch_shapes=[
            pltpu.VMEM((channels, ALL_TILES * LANES), jnp.bfloat16),
            pltpu.VMEM((channels, PADDED * LANES), jnp.float32),
            pltpu.VMEM((SLOTS * (rois + SPARE), LANES), jnp.float32),
            pltpu.SemaphoreType.DMA((7,)),
            pltpu.SemaphoreType.DMA((4,)),
        ],
        compiler_params=pltpu.CompilerParams(vmem_limit_bytes=LIMIT),
        name="unpool",
    )(floats, ints, order, base, slope, grads, *planes)


def local(
    p2, p3, p4, p5, norm_gain, norm_bias, fc6_weight, fc6_bias, fc7_weight, fc7_bias,
    cls_weight, cls_bias, box_weight, box_bias, roi_boxes, roi_level, roi_image,
    canvas_offsets, labels, target_boxes, valid,
):
    channels = p2.shape[1]
    rois = roi_level.shape[0]
    cols = lax.axis_size("col")
    rows = lax.axis_size("roi")
    hidden = fc6_bias.shape[0] * cols
    piece = fc6_bias.shape[0]
    high = rows // cols
    few = channels // high
    planes = (p2, p3, p4, p5)

    block = fc6_weight.reshape(few, 7, 7, piece)
    block = jnp.pad(block, ((0, 0), (0, 0), (0, 1), (0, 0))).reshape(few, 7, 2, 4, piece)
    block = block.transpose(3, 1, 2, 0, 4).reshape(len(USED) * 2, few, piece)
    pairs = [
        ((kappa * high + rho // cols) * cols + rho % cols, rho * cols + kappa)
        for rho in range(rows)
        for kappa in range(cols)
    ]
    block = lax.ppermute(block, ("roi", "col"), pairs)
    wide = lax.all_gather(block, "roi", axis=0)
    wide = wide.reshape(high, cols, len(USED) * 2, few, piece)
    wide = wide.transpose(2, 0, 3, 1, 4).reshape(WIDE, hidden)

    per = fc7_bias.shape[0]
    classes, boxes = cls_weight.shape[1], box_weight.shape[1]
    head = jnp.concatenate([cls_weight, box_weight, fc7_bias[:, None]], axis=1)
    head = jnp.pad(head, ((0, 0), (0, piece - head.shape[1])))
    bias_high = fc6_bias.astype(jnp.bfloat16)
    rest = fc6_bias - bias_high.astype(jnp.float32)
    bias_mid = rest.astype(jnp.bfloat16)
    bias_low = (rest - bias_mid.astype(jnp.float32)).astype(jnp.bfloat16)
    small = jnp.concatenate(
        [fc7_weight, head, jnp.stack([bias_high, bias_mid, bias_low])], axis=0
    )
    deep_rows = fc7_weight.shape[0]
    small = jnp.pad(small, ((0, -small.shape[0] % 16), (0, 0)))
    small = lax.all_gather(small, ("roi", "col"), axis=0)
    deep = small[:, :deep_rows].reshape(rows, cols, deep_rows, piece)
    deep = deep.transpose(0, 2, 1, 3).reshape(hidden, hidden)
    head = small[:, deep_rows : deep_rows + per].reshape(hidden, piece)[:, :LANES]
    bias_seven = head[:, classes + boxes].astype(jnp.float32)
    bias_six = small[:cols, deep_rows + per : deep_rows + per + 3].astype(jnp.float32)
    bias_six = jnp.sum(bias_six, axis=1).reshape(hidden)

    values = [plane[0].astype(jnp.float32) for plane in planes]
    pixel_total = rows * sum(plane.shape[1] for plane in values)
    first_sum = sum(jnp.sum(plane, axis=1) for plane in values)
    second_sum = sum(jnp.sum(plane * plane, axis=1) for plane in values)
    local_valid = jnp.sum(valid.astype(jnp.float32))
    first_sum, second_sum, valid_total = lax.psum((first_sum, second_sum, local_valid), "roi")
    mean = first_sum / pixel_total
    variance = second_sum / pixel_total - mean * mean
    inv_std = lax.rsqrt(variance + EPSILON)
    scale = norm_gain * inv_std

    picks = roi_image[None, :] == jnp.arange(4, dtype=jnp.int32)[:, None]
    shift_x = jnp.sum(jnp.where(picks, canvas_offsets[0][:, None], 0), axis=0)
    shift_y = jnp.sum(jnp.where(picks, canvas_offsets[1][:, None], 0), axis=0)
    floats, ints, order = region_tables(
        (roi_boxes[0] + shift_x).astype(jnp.float32),
        (roi_boxes[1] + shift_y).astype(jnp.float32),
        (roi_boxes[2] + shift_x).astype(jnp.float32),
        (roi_boxes[3] + shift_y).astype(jnp.float32),
        roi_level,
    )

    centred, weight, at_home = pool_maps(floats, ints, order, planes, rois)
    times = WIDE // channels
    weight = weight.astype(jnp.float32)
    centred = centred.astype(jnp.float32) / jnp.tile(at_home[2, :channels], times)
    centred = centred + weight * jnp.tile(at_home[1, :channels] - mean, times)
    pooled = centred * jnp.tile(scale, times) + weight * jnp.tile(norm_bias, times)
    pooled = pooled.astype(jnp.bfloat16)

    partial_six = jnp.dot(pooled, wide, preferred_element_type=jnp.float32).astype(jnp.bfloat16)
    pre_six = lax.psum_scatter(partial_six, "col", scatter_dimension=0, tiled=True)
    pre_six = pre_six.astype(jnp.float32) + bias_six
    hidden_six = jax.nn.silu(pre_six).astype(jnp.bfloat16)
    pre_seven = contract_last(hidden_six, deep) + bias_seven
    hidden_seven = jax.nn.silu(pre_seven).astype(jnp.bfloat16)
    scores = jnp.dot(hidden_seven, head, preferred_element_type=jnp.float32)
    logits = scores[:, :classes] + cls_bias
    deltas = scores[:, classes : classes + boxes] + box_bias

    quarter = rois // cols
    first_row = lax.axis_index("col") * quarter
    mine_labels = lax.dynamic_slice_in_dim(labels, first_row, quarter)
    mine_valid = lax.dynamic_slice_in_dim(valid, first_row, quarter).astype(jnp.float32)
    mine_boxes = lax.dynamic_slice_in_dim(roi_boxes, first_row, quarter, axis=1).astype(jnp.float32)
    mine_goals = lax.dynamic_slice_in_dim(target_boxes, first_row, quarter, axis=1).astype(
        jnp.float32
    )
    prop_width = mine_boxes[2] - mine_boxes[0]
    prop_height = mine_boxes[3] - mine_boxes[1]
    prop_cx = mine_boxes[0] + 0.5 * prop_width
    prop_cy = mine_boxes[1] + 0.5 * prop_height
    goal_width = mine_goals[2] - mine_goals[0]
    goal_height = mine_goals[3] - mine_goals[1]
    goal_cx = mine_goals[0] + 0.5 * goal_width
    goal_cy = mine_goals[1] + 0.5 * goal_height
    targets = jnp.stack(
        [
            10.0 * (goal_cx - prop_cx) / prop_width,
            10.0 * (goal_cy - prop_cy) / prop_height,
            5.0 * jnp.log(goal_width / prop_width),
            5.0 * jnp.log(goal_height / prop_height),
        ],
        axis=1,
    )
    foreground = mine_valid * (mine_labels > 0).astype(jnp.float32)
    top_logit = jnp.max(logits, axis=1, keepdims=True)
    log_total = top_logit[:, 0] + jnp.log(jnp.sum(jnp.exp(logits - top_logit), axis=1))
    onehot = (mine_labels[:, None] == jnp.arange(classes, dtype=jnp.int32)[None, :]).astype(
        jnp.float32
    )
    picked = jnp.sum(onehot * logits, axis=1)
    misfit = deltas - targets
    huber_terms = jnp.where(jnp.abs(misfit) < 1.0, 0.5 * misfit * misfit, jnp.abs(misfit) - 0.5)
    class_part = jnp.sum(mine_valid * (log_total - picked))
    box_part = jnp.sum(foreground * jnp.sum(huber_terms, axis=1))
    centre_x = prop_cx + deltas[:, 0] / 10.0 * prop_width
    centre_y = prop_cy + deltas[:, 1] / 10.0 * prop_height
    new_width = prop_width * jnp.exp(deltas[:, 2] / 5.0)
    new_height = prop_height * jnp.exp(deltas[:, 3] / 5.0)
    decoded = jnp.stack(
        [
            centre_x - 0.5 * new_width,
            centre_y - 0.5 * new_height,
            centre_x + 0.5 * new_width,
            centre_y + 0.5 * new_height,
        ]
    ) / (CANVAS // 2)
    loss_scale = rois * rows / valid_total
    softmax = jnp.exp(logits - log_total[:, None])
    logit_grads = loss_scale * mine_valid[:, None] * (softmax - onehot)
    delta_grads = loss_scale * foreground[:, None] * jnp.clip(misfit, -1.0, 1.0)
    score_grads = jnp.concatenate([logit_grads, delta_grads], axis=1)
    score_grads = jnp.pad(score_grads, ((0, 0), (0, LANES - score_grads.shape[1])))
    score_grads = score_grads.astype(jnp.bfloat16)

    head_term = contract_first(hidden_seven, score_grads)
    hidden_grads = contract_last(score_grads, head)
    pre_seven_grads = (hidden_grads * silu_slope(pre_seven)).astype(jnp.bfloat16)
    deep_term = contract_first(pre_seven_grads, hidden_six)
    six_hidden_grads = jnp.dot(pre_seven_grads, deep, preferred_element_type=jnp.float32)
    pre_six_grads = (six_hidden_grads * silu_slope(pre_six)).astype(jnp.bfloat16)
    six_grads_all = lax.all_gather(pre_six_grads, "col", axis=0, tiled=True)

    wide_term = contract_first(pooled, six_grads_all).astype(jnp.bfloat16)
    wide_term = wide_term.reshape(len(USED) * 2, high, few, cols, piece)
    wide_term = wide_term.transpose(1, 3, 0, 2, 4).reshape(rows * len(USED) * 2, few, piece)
    wide_grad = lax.psum_scatter(wide_term, "roi", scatter_dimension=0, tiled=True)
    wide_grad = lax.ppermute(wide_grad, ("roi", "col"), [(there, here) for here, there in pairs])
    wide_grad = wide_grad.reshape(4, 7, 2, few, piece).transpose(3, 1, 2, 0, 4)
    wide_grad = wide_grad.reshape(few, 7, 8, piece)[:, :, :7].reshape(few * 49, piece)
    fc6_weight_grad = wide_grad.astype(jnp.float32)

    sums = jnp.concatenate(
        [
            jnp.sum(score_grads.astype(jnp.float32), axis=0),
            jnp.stack([class_part, box_part]),
        ]
    )
    everyone = rows * cols
    deep_term = deep_term.reshape(rows, deep_rows, cols, piece).transpose(0, 2, 1, 3)
    deep_term = deep_term.reshape(everyone, deep_rows, piece)
    seven_bias_term = jnp.sum(pre_seven_grads.astype(jnp.float32), axis=0)
    head_term = jnp.concatenate(
        [head_term[:, : classes + boxes], seven_bias_term[:, None]], axis=1
    )
    head_term = jnp.pad(head_term, ((0, 0), (0, piece - head_term.shape[1])))
    head_term = head_term.reshape(everyone, per, piece)
    six_bias_term = jnp.sum(pre_six_grads.astype(jnp.float32), axis=0).reshape(cols, 1, piece)
    six_bias_term = jnp.broadcast_to(six_bias_term[None], (rows, cols, 1, piece))
    six_bias_term = six_bias_term.reshape(everyone, 1, piece)
    sums = jnp.pad(sums, (0, piece - sums.shape[0]))
    sums = jnp.broadcast_to(sums[None, None], (everyone, 1, piece))
    small_term = jnp.concatenate([deep_term, head_term, six_bias_term, sums], axis=1)
    small_term = jnp.pad(small_term, ((0, 0), (0, -small_term.shape[1] % 8), (0, 0)))
    small_grad = lax.psum_scatter(small_term, ("roi", "col"), scatter_dimension=0, tiled=True)[0]
    fc7_weight_grad = small_grad[:deep_rows]
    head_grad = small_grad[deep_rows : deep_rows + per]
    cls_weight_grad = head_grad[:, :classes]
    box_weight_grad = head_grad[:, classes : classes + boxes]
    fc7_bias_grad = head_grad[:, classes + boxes]
    fc6_bias_grad = small_grad[deep_rows + per]
    sums = small_grad[deep_rows + per + 1]
    class_bias_grad = sums[:classes]
    box_bias_grad = sums[classes : classes + boxes]
    cls_loss = sums[LANES] / valid_total
    box_loss = sums[LANES + 1] / valid_total

    pool_grads = contract_last(six_grads_all, wide)
    gain_part = jnp.sum(pool_grads * centred.astype(jnp.float32), axis=0)
    shift_part = jnp.sum(pool_grads * weight.astype(jnp.float32), axis=0)
    gain_part = jnp.sum(gain_part.reshape(-1, channels), axis=0) * inv_std
    shift_part = jnp.sum(shift_part.reshape(-1, channels), axis=0)
    norm_gain_grad, norm_bias_grad = lax.psum((gain_part, shift_part), "roi")

    scaled = (pool_grads * jnp.tile(scale, WIDE // channels)).astype(jnp.bfloat16)
    slope = -scale * inv_std * norm_gain_grad / pixel_total
    base = -scale * norm_bias_grad / pixel_total - slope * mean

    def spread(vector):
        return jnp.broadcast_to(vector[:, None], (channels, LANES))

    input_grads = unpool_maps(floats, ints, order, spread(base), spread(slope), scaled, planes, rois)
    return (
        cls_loss,
        box_loss,
        decoded,
        input_grads[0],
        input_grads[1],
        input_grads[2],
        input_grads[3],
        norm_gain_grad,
        norm_bias_grad,
        fc6_weight_grad,
        fc6_bias_grad,
        fc7_weight_grad,
        fc7_bias_grad,
        cls_weight_grad,
        class_bias_grad,
        box_weight_grad,
        box_bias_grad,
    )


MESH = pl.DeviceIdType.MESH
KEPT = tuple(at for at in range(2 * len(USED)) if at % 2 == 0 or at // 2 < 21)
LEADING = 42
SPARES = tuple(at for at in range(2 * len(USED)) if at not in KEPT)
SMALL = 5


def ring_of(rows):
    return list(range(0, rows, 2)) + list(range(rows - 1, 0, -2))


def position_of(kappa, rows, cols, block, half):
    plane = lax.rem(2 * (block % 2) + block // 2 + kappa, cols)
    return rows - 1 - plane if half else plane


def greet(axis, count):
    barrier = pltpu.get_barrier_semaphore()
    me = lax.axis_index(axis)
    for step in range(1, count):
        pl.semaphore_signal(
            barrier,
            inc=1,
            device_id={axis: lax.rem(me + step, count)},
            device_id_type=MESH,
        )


def met(count):
    pl.semaphore_wait(pltpu.get_barrier_semaphore(), count)


def remote(src, dst, sends, recvs, at, axis, peer):
    return pltpu.make_async_remote_copy(
        src_ref=src,
        dst_ref=dst,
        send_sem=sends.at[at],
        recv_sem=recvs.at[at],
        device_id={axis: peer},
        device_id_type=MESH,
    )


def share(slots, axis, count, sends, recvs, first=0):
    me = lax.axis_index(axis)
    copies = [
        remote(slots.at[me], slots.at[me], sends, recvs, first + step - 1, axis,
               lax.rem(me + step, count))
        for step in range(1, count)
    ]
    for copy in copies:
        copy.start()
    return copies


def neighbours(me):
    core, chip = lax.rem(me, 2), lax.div(me, 2)
    return me + 1 - 2 * core, me + 2 - 4 * chip


class Relay:
    def __init__(self, view, sends, recvs, first):
        me = lax.axis_index("col")
        core, chip = neighbours(me)
        self.near = remote(view(me), view(me), sends, recvs, first, "col", core)
        self.far = remote(view(me), view(me), sends, recvs, first + 1, "col", chip)
        self.passed = remote(view(chip), view(chip), sends, recvs, first + 2, "col", core)

    def start(self):
        self.far.start()
        self.near.start()

    def forward(self):
        self.far.wait_recv()
        self.passed.start()

    def wait(self):
        self.near.wait()
        self.far.wait_send()
        self.passed.wait()


def gather_small_kernel(
    rows, cols, pixels, mine, norms, at_home, out, stats,
    slots, sends, recvs, x_sends, x_recvs, s_sends, s_recvs, sem,
):
    row, col = lax.axis_index("roi"), lax.axis_index("col")
    depth, channels = rows // 2, LANES // 2
    plane, side = lax.div(row, 2), lax.rem(row, 2)
    greet("roi", rows)
    greet("col", cols)
    slots[row] = jnp.concatenate([at_home[:1], norms[1:2], at_home[2:]], axis=0)
    own = pltpu.make_async_copy(mine, out.at[col, plane, side], sem)
    own.start()
    own.wait()
    met(rows + cols - 2)
    sums = share(slots, "roi", rows, s_sends, s_recvs)
    along = [
        remote(mine, out.at[col, plane, side], x_sends, x_recvs, step - 1, "roi",
               lax.rem(plane + step, depth) * 2 + side)
        for step in range(1, depth)
    ]
    across = []
    for step in range(depth):
        block = out.at[col, lax.rem(plane + depth - step, depth), side]
        across.append(
            remote(block, block, x_sends, x_recvs, depth - 1 + step, "roi", row + 1 - 2 * side)
        )
    for copy in along:
        copy.start()
    across[0].start()
    for step in range(1, depth):
        along[step - 1].wait_recv()
        across[step].start()
    relays = [
        Relay(lambda at: out.at[at, :, side], sends, recvs, 0),
        Relay(lambda at: out.at[at, :, 1 - side], sends, recvs, 3),
    ]
    relays[0].start()
    for copy in across:
        copy.wait_recv()
    relays[1].start()
    for copy in sums:
        copy.wait()
    total = slots[0]
    for at in range(1, rows):
        total = total + slots[at]
    turned = pltpu.roll(total, channels, 1)
    low = lax.broadcasted_iota(jnp.int32, total.shape, 1) < channels
    mean = (jnp.where(low, total, turned) / pixels)[:1]
    square = (jnp.where(low, turned, total) / pixels)[:1]
    inv_std = lax.rsqrt(square - mean * mean + EPSILON)
    scale = norms[:1] * inv_std
    spread = 1.0 / at_home[2:3]
    offset = at_home[1:2] - mean
    stats[...] = jnp.concatenate(
        [mean, scale, inv_std, total[1:2], scale * spread, scale * offset + norms[2:3],
         spread, offset],
        axis=0,
    )
    for relay in relays:
        relay.forward()
    for relay in relays:
        relay.wait()
    for copy in along + across:
        copy.wait_send()


def place_wide(pieces, wide, sems, rows, cols):
    few, piece = pieces.shape[2], pieces.shape[3]
    kappa = lax.axis_index("col")
    blocks = []
    for block in range(cols):
        copies = []
        for half in range(2):
            position = position_of(kappa, rows, cols, block, half)
            span, lanes = pl.ds(half * few, few), pl.ds(block * piece, piece)
            place = 2 * block + half
            copies.append(
                pltpu.make_async_copy(
                    pieces.at[position, pl.ds(0, LEADING)],
                    wide.at[pl.ds(0, LEADING), span, lanes],
                    sems.at[place, 0],
                )
            )
            for at in range(LEADING, len(KEPT)):
                copies.append(
                    pltpu.make_async_copy(
                        pieces.at[position, at],
                        wide.at[KEPT[at], span, lanes],
                        sems.at[place, at - LEADING + 1],
                    )
                )
        blocks.append(copies)
    for copies in blocks:
        for copy in copies:
            copy.start()
    for at in SPARES:
        wide[at] = jnp.zeros(wide.shape[1:], wide.dtype)
    return blocks


def head_kernel(
    rows, cols, classes, boxes, facts, score_bias, stats, centred_in, weight_in, small_in, pieces,
    pooled, g6_all, g7_out, hid6_out, hid7_out, gs_out, scores_out, losses_out,
    centred, weight, small, wide, mine, taken, in_sems, sems, sends, recvs, relay_sends, relay_recvs,
):
    me = lax.axis_index("col")
    rois, hidden = g6_all.shape
    quarter, piece = rois // cols, hidden // cols
    greet("col", cols)
    centred_copy = pltpu.make_async_copy(centred_in, centred, in_sems.at[0])
    weight_copy = pltpu.make_async_copy(weight_in, weight, in_sems.at[1])
    small_copy = pltpu.make_async_copy(small_in, small, in_sems.at[2])
    centred_copy.start()
    weight_copy.start()
    blocks = place_wide(pieces, wide, sems, rows, cols)
    small_copy.start()
    centred_copy.wait()
    weight_copy.wait()
    for at in range(len(USED)):
        lanes = slice(at * LANES, (at + 1) * LANES)
        value = centred[:, lanes].astype(jnp.float32) * stats[4:5]
        value = value + weight[:, lanes].astype(jnp.float32) * stats[5:6]
        pooled[:, lanes] = value.astype(jnp.bfloat16)
    met(cols - 1)

    def sending(part, step):
        lanes = pl.ds(part * piece, piece)
        peer = lax.rem(me + step, cols)
        return pltpu.make_async_remote_copy(
            src_ref=mine.at[peer, :, lanes],
            dst_ref=taken.at[step - 1, :, lanes],
            send_sem=sends.at[step - 1, part],
            recv_sem=recvs.at[step - 1, part],
            device_id={"col": peer},
            device_id_type=MESH,
        )

    for part in range(cols):
        for copy in blocks[part]:
            copy.wait()
        lanes = slice(part * piece, (part + 1) * piece)
        weights = wide[:, :, lanes].reshape(WIDE, piece)
        result = jnp.dot(pooled[...], weights, preferred_element_type=jnp.float32)
        result = result.astype(jnp.bfloat16)
        for at in range(cols):
            mine[at, :, lanes] = result[at * quarter : (at + 1) * quarter]
        for step in range(1, cols):
            sending(part, step).start()
    small_copy.wait()
    for part in range(cols):
        for step in range(1, cols):
            sending(part, step).wait()
    pre_six = mine[me].astype(jnp.float32)
    for step in range(1, cols):
        pre_six = pre_six + taken[step - 1].astype(jnp.float32)
    lines = [small[at, 0, 4, :16, LANES:].astype(jnp.float32) for at in range(cols)]
    bias = jnp.concatenate(
        [
            (line[part : part + 1] + line[part + 2 : part + 3]) + line[part + 4 : part + 5]
            for line in lines
            for part in range(2)
        ],
        axis=1,
    )
    pre_six = pre_six + bias
    sigma_six = jax.nn.sigmoid(pre_six)
    hidden_six = (pre_six * sigma_six).astype(jnp.bfloat16)
    hid6_out[...] = hidden_six
    deep = [small[at, :, :4].reshape(hidden, piece) for at in range(cols)]
    head = jnp.concatenate(
        [small[at, row, 4, :, :LANES] for row in range(rows) for at in range(cols)], axis=0
    )
    lane = lax.broadcasted_iota(jnp.int32, (quarter, LANES), 1)
    pick = (lane == classes + boxes).astype(jnp.bfloat16)
    pre_seven = contract_last(pick, head)
    for at in range(cols):
        pre_seven = pre_seven + contract_last(
            hidden_six[:, at * piece : (at + 1) * piece], deep[at]
        )
    sigma_seven = jax.nn.sigmoid(pre_seven)
    hidden_seven = (pre_seven * sigma_seven).astype(jnp.bfloat16)
    hid7_out[...] = hidden_seven
    scores = jnp.dot(hidden_seven, head, preferred_element_type=jnp.float32) + score_bias[...]
    scores_out[...] = scores
    loss_scale = float(rois * rows) / stats[3:4, :1]
    targets, onehot, weights = facts[0], facts[1], facts[2] * loss_scale
    is_class = lane < classes
    top = jnp.max(jnp.where(is_class, scores, -jnp.inf), axis=1, keepdims=True)
    powers = jnp.where(is_class, jnp.exp(jnp.where(is_class, scores - top, 0.0)), 0.0)
    log_total = top + jnp.log(jnp.sum(powers, axis=1, keepdims=True))
    picked = jnp.sum(onehot * scores, axis=1, keepdims=True)
    softmax = jnp.where(is_class, jnp.exp(jnp.where(is_class, scores - log_total, 0.0)), 0.0)
    misfit = jnp.where(is_class, 0.0, scores - targets)
    size = jnp.abs(misfit)
    huber = jnp.where(size < 1.0, 0.5 * misfit * misfit, size - 0.5)
    class_part = jnp.sum(weights[:, :1] * (log_total - picked), axis=0, keepdims=True)
    box_part = jnp.sum(jnp.where(is_class, 0.0, weights * huber), axis=0, keepdims=True)
    grads = jnp.where(is_class, softmax - onehot, jnp.clip(misfit, -1.0, 1.0))
    score_grads = (weights * grads).astype(jnp.bfloat16)
    gs_out[...] = score_grads
    losses_out[...] = jnp.concatenate(
        [
            jnp.broadcast_to(class_part, (1, LANES)),
            box_part,
            jnp.sum(score_grads.astype(jnp.float32), axis=0, keepdims=True),
            jnp.zeros((5, LANES), jnp.float32),
        ],
        axis=0,
    )
    slope_seven = sigma_seven * (1.0 + pre_seven * (1.0 - sigma_seven))
    g7 = (contract_last(score_grads, head) * slope_seven).astype(jnp.bfloat16)
    g7_out[...] = g7
    place = pl.ds(pl.multiple_of(me * quarter, quarter), quarter)
    relays = []
    for at in range(cols):
        lanes = slice(at * piece, (at + 1) * piece)
        back = jnp.dot(g7, deep[at], preferred_element_type=jnp.float32)
        sigma, value = sigma_six[:, lanes], pre_six[:, lanes]
        back = back * (sigma * (1.0 + value * (1.0 - sigma)))
        g6_all[place, lanes] = back.astype(jnp.bfloat16)
        relays.append(
            Relay(
                lambda owner, at=at: g6_all.at[
                    pl.ds(pl.multiple_of(owner * quarter, quarter), quarter),
                    pl.ds(at * piece, piece),
                ],
                relay_sends, relay_recvs, 3 * at,
            )
        )
        relays[-1].start()
    for relay in relays:
        relay.forward()
    for relay in relays:
        relay.wait()


def wide_grad_kernel(
    rows, cols, pooled_in, g6_all, g7, hid6, hid7, gs, losses,
    terms, g7_all, losses_all,
    pooled, hid6_own, buffers, last, extras, head_mine, head_taken, in_sem, out_sems, sends, recvs,
):
    me = lax.axis_index("col")
    rois, hidden = g6_all.shape
    quarter, piece = rois // cols, hidden // cols
    owned, per = hidden // rows, hidden // (rows * cols)
    few = buffers.shape[2] // 4
    ring = ring_of(rows)
    greet("col", cols)
    fetch = pltpu.make_async_copy(pooled_in, pooled, in_sem)
    fetch.start()

    def block(at):
        return pl.ds(pl.multiple_of(at * quarter, quarter), quarter)

    g7_all[block(me), :] = g7[...]
    losses_all[me] = losses[...]
    own = pl.ds(pl.multiple_of(me * piece, piece), piece)
    hid6_own[block(me), :] = hid6[:, own]
    head_term = contract_first(hid7[...], gs[...]).astype(jnp.bfloat16)
    for row in range(rows):
        for at in range(cols):
            first = row * owned + at * per
            head_mine[at, row] = head_term[first : first + per]
    met(cols - 1)
    relay = Relay(lambda at: g7_all.at[block(at)], sends, recvs, 0)
    relay.start()
    copies = []
    for step in range(1, cols):
        peer = lax.rem(me + step, cols)
        theirs = pl.ds(pl.multiple_of(peer * piece, piece), piece)
        copies.append(
            remote(hid6.at[:, theirs], hid6_own.at[block(me)], sends, recvs, 2 + step, "col", peer)
        )
        copies.append(
            remote(head_mine.at[peer], head_taken.at[step - 1], sends, recvs, 5 + step, "col", peer)
        )
        copies.append(
            remote(losses, losses_all.at[me], sends, recvs, 8 + step, "col", peer)
        )
    for copy in copies:
        copy.start()

    def leaving(slot, at):
        size = 4 * few
        span = pl.ds(pl.multiple_of(at * size, size), size)
        return pltpu.make_async_copy(buffers.at[slot], terms.at[:, span], out_sems.at[slot])

    def put(result, target, row, parts):
        for column in range(cols):
            columns = slice(column * piece, (column + 1) * piece)
            for half in range(2):
                position = position_of(me, rows, cols, column, half)
                for index, part in enumerate(parts):
                    first = (part * 2 + half) * few
                    target[position, row + index * few : row + (index + 1) * few, :] = result[
                        first : first + few, columns
                    ]

    def step(pair, carry):
        for slot in range(2):
            at = pair * 2 + slot

            @pl.when(pair > 0)
            def _():
                leaving(slot, at - 2).wait()

            lanes = pl.ds(pl.multiple_of(at * 2 * LANES, 2 * LANES), 2 * LANES)
            result = contract_first(pooled[:, lanes], g6_all[...]).astype(jnp.bfloat16)
            put(result, buffers.at[slot], 0, range(4))
            leaving(slot, at).start()
        return carry
    fetch.wait()
    pairs = LEADING // 8
    lax.fori_loop(0, pairs - 1, step, 0)
    relay.forward()
    lax.fori_loop(pairs - 1, pairs, step, 0)
    row = 0
    for at in range(2 * pairs, len(USED) // 2):
        parts = [part for part in range(4) if 4 * at + part in KEPT]
        lanes = slice(at * 2 * LANES, (at + 1) * 2 * LANES)
        result = contract_first(pooled[:, lanes], g6_all[...]).astype(jnp.bfloat16)
        put(result, last, row, parts)
        row += len(parts) * few
    first = 2 * pairs * 4 * few
    rest = pltpu.make_async_copy(last, terms.at[:, pl.ds(first, row)], out_sems.at[2])
    rest.start()
    relay.wait()
    for copy in copies:
        copy.wait()
    deep_term = contract_first(g7_all[...], hid6_own[...]).astype(jnp.bfloat16)
    nothing = jnp.zeros((per, piece - LANES), jnp.bfloat16)
    for position, owner in enumerate(ring):
        extras[position, :owned, :] = deep_term[owner * owned : (owner + 1) * owned]
        total = head_mine[me, owner].astype(jnp.float32)
        for at in range(cols - 1):
            total = total + head_taken[at, owner].astype(jnp.float32)
        extras[position, owned : owned + per, :] = jnp.concatenate(
            [total.astype(jnp.bfloat16), nothing], axis=1
        )
    more = pltpu.make_async_copy(
        extras, terms.at[:, pl.ds(first + row, owned + per)], out_sems.at[3]
    )
    more.start()
    for slot in range(2):
        leaving(slot, 2 * pairs - 2 + slot).wait()
    rest.wait()
    more.wait()


def pool_grad_kernel(
    rows, cols, pixels, g6_all, g7_all, losses_all, centred, weight, stats, pieces,
    grads, totals, base, slope, wide, slots, sems, sends, recvs,
):
    row, col = lax.axis_index("roi"), lax.axis_index("col")
    rois, hidden = g6_all.shape
    channels = base.shape[0]
    piece = hidden // cols
    greet("roi", rows)
    blocks = place_wide(pieces, wide, sems, rows, cols)
    own = pl.ds(pl.multiple_of(col * piece, piece), piece)

    def columns(values):
        return jnp.sum(values.astype(jnp.float32), axis=0, keepdims=True)

    def as_rows(vector):
        return [
            vector[:, at * LANES : (at + 1) * LANES] for at in range(vector.shape[1] // LANES)
        ]

    bias_rows = as_rows(columns(g6_all[:, own])) + as_rows(columns(g7_all[...]))
    losses = losses_all[0]
    for at in range(1, cols):
        losses = losses + losses_all[at]
    for copies in blocks:
        for copy in copies:
            copy.wait()
    scale = stats[1:2]

    def step(at, carry):
        gain, shift = carry
        lanes = pl.ds(pl.multiple_of(at * 2 * LANES, 2 * LANES), 2 * LANES)
        weights = wide[pl.ds(at * 4, 4)].reshape(2 * LANES, hidden)
        result = contract_last(g6_all[...], weights)
        with_centred = result * centred[:, lanes].astype(jnp.float32)
        with_weight = result * weight[:, lanes].astype(jnp.float32)
        both = jnp.concatenate([scale, scale], axis=1)
        grads[:, lanes] = (result * both).astype(jnp.bfloat16)
        for half in range(2):
            part = slice(half * LANES, (half + 1) * LANES)
            gain = gain + jnp.sum(with_centred[:, part].reshape(rois // 8, 8, LANES), axis=0)
            shift = shift + jnp.sum(with_weight[:, part].reshape(rois // 8, 8, LANES), axis=0)
        return gain, shift

    nothing = jnp.zeros((8, LANES), jnp.float32)
    gain, shift = lax.fori_loop(0, len(USED) // 2, step, (nothing, nothing))
    low = lax.broadcasted_iota(jnp.int32, (8, LANES), 1) < channels
    gain = jnp.sum(gain + pltpu.roll(gain, channels, 1), axis=0, keepdims=True)
    shift = jnp.sum(shift + pltpu.roll(shift, channels, 1), axis=0, keepdims=True)
    both = jnp.where(low[:1], stats[6:7] * gain + stats[7:8] * shift, shift)
    lines = [both] + bias_rows + [losses[2:3], losses[:2]]
    count = 1 + len(bias_rows) + 3
    lines.append(jnp.zeros((16 - count, LANES), jnp.float32))
    slots[row] = jnp.concatenate(lines, axis=0)
    met(rows - 1)
    for copy in share(slots, "roi", rows, sends, recvs):
        copy.wait()
    total = slots[0]
    for at in range(1, rows):
        total = total + slots[at]
    gain_grad = total[:1] * stats[2:3]
    totals[...] = jnp.concatenate([total[:15], gain_grad], axis=0)
    slope_row = -stats[1:2] * stats[2:3] * gain_grad / pixels
    shift_grad = pltpu.roll(jnp.broadcast_to(total[:1], (8, LANES)), channels, 1)[:1]
    base_row = -stats[1:2] * shift_grad / pixels - slope_row * stats[:1]
    slope[...] = jnp.broadcast_to(slope_row[:, :channels], (LANES, channels)).T
    base[...] = jnp.broadcast_to(base_row[:, :channels], (LANES, channels)).T


def deliver_kernel(rows, cols, few, term, taken, held, sems, sends, recvs):
    row, col = lax.axis_index("roi"), lax.axis_index("col")
    plane, side = lax.div(row, 2), lax.rem(row, 2)
    chip, core = lax.div(col, 2), lax.rem(col, 2)
    near = {"roi": row, "col": cols - 1 - col}
    crossing = lax.rem(lax.rem(plane + cols - col, cols), 2) != chip
    kappa = jnp.where(crossing, cols - 1 - col, col)
    core_there = lax.div(lax.rem(plane + cols - kappa, cols), 2)
    target = {"roi": kappa * 2 + side, "col": 2 * chip + core_there}
    alone = (kappa == plane) & (core_there == core)
    plane_from = lax.rem(2 * core + chip + plane, cols)
    core_from = jnp.where(lax.div(plane, 2) == chip, lax.rem(plane, 2), 1 - lax.rem(plane, 2))
    source = {"roi": plane_from * 2 + side, "col": 2 * chip + core_from}
    barrier = pltpu.get_barrier_semaphore()

    @pl.when(crossing)
    def _():
        pl.semaphore_signal(barrier, inc=1, device_id=near, device_id_type=MESH)

    @pl.when(jnp.logical_not(alone))
    def _():
        pl.semaphore_signal(barrier, inc=1, device_id=source, device_id_type=MESH)

    @pl.when(crossing | jnp.logical_not(alone))
    def _():
        pl.semaphore_wait(barrier, crossing.astype(jnp.int32) + 1 - alone.astype(jnp.int32))

    count = 7
    size = len(KEPT) // count
    spans = [pl.ds(at * size * few, size * few) for at in range(count)]

    def over(at):
        return pltpu.make_async_remote_copy(
            src_ref=term.at[spans[at]], dst_ref=held.at[spans[at]],
            send_sem=sends.at[0, at], recv_sem=recvs.at[0, at],
            device_id=near, device_id_type=MESH,
        )

    def along(block, at):
        return pltpu.make_async_remote_copy(
            src_ref=block.at[spans[at]], dst_ref=taken.at[spans[at]],
            send_sem=sends.at[1, at], recv_sem=recvs.at[1, at],
            device_id=target, device_id_type=MESH,
        )

    def inside(block, at):
        return pltpu.make_async_copy(block.at[spans[at]], taken.at[spans[at]], sems.at[at])

    def pass_on(block, at):
        @pl.when(alone)
        def _():
            inside(block, at).start()

        @pl.when(jnp.logical_not(alone))
        def _():
            along(block, at).start()

    @pl.when(crossing)
    def _():
        for at in range(count):
            over(at).start()
        for at in range(count):
            over(at).wait_recv()
            pass_on(held, at)

    @pl.when(jnp.logical_not(crossing))
    def _():
        for at in range(count):
            pass_on(term, at)

    for chunk in range(count):
        @pl.when(alone)
        def _():
            inside(held, chunk).wait()

        @pl.when(jnp.logical_not(alone))
        def _():
            along(held, chunk).wait_recv()


    @pl.when(crossing)
    def _():
        for at in range(count):
            over(at).wait_send()

    @pl.when(jnp.logical_not(alone))
    def _():
        for at in range(count):
            along(held, at).wait_send()


def restore_kernel(few, classes, boxes, taken, term, out, deep, scores, deltas, half):
    for part in range(out.shape[1] // LANES):
        lanes = slice(part * LANES, (part + 1) * LANES)
        for index, slot in enumerate(KEPT):
            place = pl.ds(slot // 2 % 7 * 7 + slot // 14 + 4 * (slot % 2), few, stride=49)
            half[part, place, :] = taken[index * few : (index + 1) * few, lanes].astype(
                jnp.float32
            )
        out[:, lanes] = half[part]
    rows = deep.shape[0]
    kept = out.shape[0]
    deep[...] = term[kept : kept + rows, :].astype(jnp.float32)
    head = term[kept + rows :, :LANES].astype(jnp.float32)
    scores[...] = head[:, :classes]
    deltas[...] = pltpu.roll(head, LANES - classes, 1)[:, :boxes]


def unpool_all_kernel(
    rois, rows, cols, classes, boxes, floats, ints, order, base, slope, totals, grads, *rest
):
    planes, outs, few, scratch = rest[:4], rest[4:8], rest[8:16], rest[16:]
    gain, shift, bias_six, bias_seven, bias_cls, bias_box, cls_loss, box_loss = few
    channels, per = gain.shape[0], bias_seven.shape[0]
    row, col = lax.axis_index("roi"), lax.axis_index("col")

    def finish():
        head = totals[:8]
        turned = pltpu.roll(head, channels, 1)
        gain[...] = totals[8:][7, :channels]
        shift[...] = turned[0, :channels]
        wide_lines = bias_six.shape[0] // LANES
        for at in range(wide_lines):
            bias_six[at * LANES : (at + 1) * LANES] = head[1 + at]
        place = (row * cols + col) * per
        line = totals[pl.ds(1 + wide_lines + lax.div(place, LANES), 1), :]
        line = pltpu.roll(
            jnp.broadcast_to(line, (8, LANES)), lax.rem(LANES - lax.rem(place, LANES), LANES), 1
        )
        bias_seven[...] = line[0, :per]
        first = 1 + (cols + 1) * wide_lines
        scores = jnp.broadcast_to(totals[first : first + 1], (8, LANES))
        bias_cls[...] = scores[0, :classes]
        bias_box[...] = pltpu.roll(scores, LANES - classes, 1)[0, :boxes]
        cls_loss[...] = totals[first + 1 : first + 2, :1] / (rois * rows)
        box_loss[...] = jnp.sum(totals[first + 2 : first + 3], axis=1, keepdims=True) / (
            rois * rows
        )

    unpool_kernel(
        rois, floats, ints, order, base, slope, grads, *planes, *outs, *scratch, finish=finish
    )


def unpool_all(
    floats, ints, order, base, slope, totals, grads, planes, rois, rows, cols, classes, boxes,
    piece,
):
    channels = planes[0].shape[1]
    f32 = jnp.float32
    results = pl.pallas_call(
        functools.partial(unpool_all_kernel, rois, rows, cols, classes, boxes),
        out_shape=tuple(shaped(plane.shape, f32) for plane in planes)
        + (
            shaped((channels,), f32),
            shaped((channels,), f32),
            shaped((piece,), f32),
            shaped((piece // rows,), f32),
            shaped((classes,), f32),
            shaped((boxes,), f32),
            shaped((1, 1), f32),
            shaped((1, 1), f32),
        ),
        in_specs=[SMEM] * 3 + [VMEM] * 4 + [ANY] * 4,
        out_specs=(ANY,) * 4 + (VMEM,) * 8,
        scratch_shapes=[
            pltpu.VMEM((channels, ALL_TILES * LANES), jnp.bfloat16),
            pltpu.VMEM((channels, PADDED * LANES), f32),
            pltpu.VMEM((SLOTS * (rois + SPARE), LANES), f32),
            pltpu.SemaphoreType.DMA((7,)),
            pltpu.SemaphoreType.DMA((4,)),
        ],
        compiler_params=pltpu.CompilerParams(vmem_limit_bytes=LIMIT),
        name="unpool",
    )(floats, ints, order, base, slope, totals, grads, *planes)
    return results[:4], results[4:]


def comm_params(number):
    return pltpu.CompilerParams(
        vmem_limit_bytes=LIMIT, collective_id=number, has_side_effects=True
    )


def shaped(shape, dtype):
    return jax.ShapeDtypeStruct(shape, dtype)


def gather_small(mine, norms, at_home, rows, cols, pixels):
    out, stats = pl.pallas_call(
        functools.partial(gather_small_kernel, rows, cols, pixels),
        out_shape=(
            shaped((cols, rows // 2, 2) + mine.shape, mine.dtype),
            shaped((8, LANES), jnp.float32),
        ),
        in_specs=[VMEM] * 3,
        out_specs=(VMEM, VMEM),
        scratch_shapes=[
            pltpu.VMEM((rows, 8, LANES), jnp.float32),
            pltpu.SemaphoreType.DMA((6,)),
            pltpu.SemaphoreType.DMA((6,)),
            pltpu.SemaphoreType.DMA((rows - 1,)),
            pltpu.SemaphoreType.DMA((rows - 1,)),
            pltpu.SemaphoreType.DMA((rows - 1,)),
            pltpu.SemaphoreType.DMA((rows - 1,)),
            pltpu.SemaphoreType.DMA,
        ],
        compiler_params=comm_params(1),
        name="gather_small",
    )(mine, norms, at_home)
    return out.reshape((cols, rows) + mine.shape), stats


def run_head(centred, weight, stats, facts, score_bias, small, pieces, rows, cols, classes, boxes):
    rois, channels = centred.shape[0], LANES // 2
    quarter, hidden = rois // cols, pieces.shape[3] * cols
    bf16, f32 = jnp.bfloat16, jnp.float32
    return pl.pallas_call(
        functools.partial(head_kernel, rows, cols, classes, boxes),
        out_shape=(
            shaped(centred.shape, bf16),
            shaped((rois, hidden), bf16),
            shaped((quarter, hidden), bf16),
            shaped((quarter, hidden), bf16),
            shaped((quarter, hidden), bf16),
            shaped((quarter, LANES), bf16),
            shaped((quarter, LANES), f32),
            shaped((8, LANES), f32),
        ),
        in_specs=[VMEM, VMEM, VMEM, ANY, ANY, ANY, ANY],
        out_specs=(VMEM,) * 8,
        scratch_shapes=[
            pltpu.VMEM(centred.shape, bf16),
            pltpu.VMEM(centred.shape, bf16),
            pltpu.VMEM(small.shape, bf16),
            pltpu.VMEM((2 * len(USED), channels, hidden), bf16),
            pltpu.VMEM((cols, quarter, hidden), bf16),
            pltpu.VMEM((cols - 1, quarter, hidden), bf16),
            pltpu.SemaphoreType.DMA((3,)),
            pltpu.SemaphoreType.DMA((rows, 8)),
            pltpu.SemaphoreType.DMA((cols - 1, cols)),
            pltpu.SemaphoreType.DMA((cols - 1, cols)),
            pltpu.SemaphoreType.DMA((3 * cols,)),
            pltpu.SemaphoreType.DMA((3 * cols,)),
        ],
        compiler_params=comm_params(2),
        name="head",
    )(facts, score_bias, stats, centred, weight, small, pieces)


def wide_grads(pooled, g6_all, g7, hid6, hid7, gs, losses, rows, cols):
    rois, hidden = g6_all.shape
    piece, few = hidden // cols, LANES // 2 // (rows // cols)
    owned, per = hidden // rows, hidden // (rows * cols)
    bf16, f32 = jnp.bfloat16, jnp.float32
    return pl.pallas_call(
        functools.partial(wide_grad_kernel, rows, cols),
        out_shape=(
            shaped((rows, len(KEPT) * few + owned + per, piece), bf16),
            shaped((rois, hidden), bf16),
            shaped((cols, 8, LANES), f32),
        ),
        in_specs=[ANY] + [VMEM] * 6,
        out_specs=(ANY, VMEM, VMEM),
        scratch_shapes=[
            pltpu.VMEM(pooled.shape, bf16),
            pltpu.VMEM((rois, piece), bf16),
            pltpu.VMEM((2, rows, 4 * few, piece), bf16),
            pltpu.VMEM((rows, (len(KEPT) - LEADING // 8 * 8) * few, piece), bf16),
            pltpu.VMEM((rows, owned + per, piece), bf16),
            pltpu.VMEM((cols, rows, per, LANES), bf16),
            pltpu.VMEM((cols - 1, rows, per, LANES), bf16),
            pltpu.SemaphoreType.DMA,
            pltpu.SemaphoreType.DMA((4,)),
            pltpu.SemaphoreType.DMA((12,)),
            pltpu.SemaphoreType.DMA((12,)),
        ],
        compiler_params=comm_params(3),
        name="wide_grads",
    )(pooled, g6_all, g7, hid6, hid7, gs, losses)


def pool_grads(g6_all, g7_all, losses_all, centred, weight, stats, pieces, rows, cols, pixels):
    rois, hidden = g6_all.shape
    channels = LANES // 2
    bf16, f32 = jnp.bfloat16, jnp.float32
    return pl.pallas_call(
        functools.partial(pool_grad_kernel, rows, cols, pixels),
        out_shape=(
            shaped((rois, WIDE), bf16),
            shaped((16, LANES), f32),
            shaped((channels, LANES), f32),
            shaped((channels, LANES), f32),
        ),
        in_specs=[VMEM] * 6 + [ANY],
        out_specs=(VMEM,) * 4,
        scratch_shapes=[
            pltpu.VMEM((2 * len(USED), channels, hidden), bf16),
            pltpu.VMEM((rows, 16, LANES), f32),
            pltpu.SemaphoreType.DMA((rows, 8)),
            pltpu.SemaphoreType.DMA((rows - 1,)),
            pltpu.SemaphoreType.DMA((rows - 1,)),
        ],
        compiler_params=comm_params(4),
        name="pool_grads",
    )(g6_all, g7_all, losses_all, centred, weight, stats, pieces)


def deliver(term, rows, cols, few):
    piece, kept = term.shape[1], len(KEPT) * few
    return pl.pallas_call(
        functools.partial(deliver_kernel, rows, cols, few),
        out_shape=shaped((kept, piece), term.dtype),
        in_specs=[ANY],
        out_specs=VMEM,
        scratch_shapes=[
            pltpu.VMEM((kept, piece), term.dtype),
            pltpu.SemaphoreType.DMA((7,)),
            pltpu.SemaphoreType.DMA((2, 7)),
            pltpu.SemaphoreType.DMA((2, 7)),
        ],
        compiler_params=comm_params(5),
        name="deliver",
    )(term)


def restore(taken, term, few, deep_rows, per, classes, boxes):
    kept, piece = taken.shape
    f32 = jnp.float32
    return pl.pallas_call(
        functools.partial(restore_kernel, few, classes, boxes),
        out_shape=(
            shaped((kept, piece), f32),
            shaped((deep_rows, piece), f32),
            shaped((per, classes), f32),
            shaped((per, boxes), f32),
        ),
        in_specs=[VMEM, VMEM],
        out_specs=(VMEM,) * 4,
        scratch_shapes=[pltpu.VMEM((piece // LANES, kept, LANES), f32)],
        compiler_params=pltpu.CompilerParams(vmem_limit_bytes=LIMIT),
        name="restore",
    )(taken, term)


def targets_of(mine_boxes, mine_goals):
    prop_width = mine_boxes[2] - mine_boxes[0]
    prop_height = mine_boxes[3] - mine_boxes[1]
    prop_cx = mine_boxes[0] + 0.5 * prop_width
    prop_cy = mine_boxes[1] + 0.5 * prop_height
    goal_width = mine_goals[2] - mine_goals[0]
    goal_height = mine_goals[3] - mine_goals[1]
    goal_cx = mine_goals[0] + 0.5 * goal_width
    goal_cy = mine_goals[1] + 0.5 * goal_height
    return jnp.stack(
        [
            10.0 * (goal_cx - prop_cx) / prop_width,
            10.0 * (goal_cy - prop_cy) / prop_height,
            5.0 * jnp.log(goal_width / prop_width),
            5.0 * jnp.log(goal_height / prop_height),
        ],
        axis=1,
    )


def decode(mine_boxes, deltas):
    prop_width = mine_boxes[2] - mine_boxes[0]
    prop_height = mine_boxes[3] - mine_boxes[1]
    prop_cx = mine_boxes[0] + 0.5 * prop_width
    prop_cy = mine_boxes[1] + 0.5 * prop_height
    centre_x = prop_cx + deltas[:, 0] / 10.0 * prop_width
    centre_y = prop_cy + deltas[:, 1] / 10.0 * prop_height
    new_width = prop_width * jnp.exp(deltas[:, 2] / 5.0)
    new_height = prop_height * jnp.exp(deltas[:, 3] / 5.0)
    return jnp.stack(
        [
            centre_x - 0.5 * new_width,
            centre_y - 0.5 * new_height,
            centre_x + 0.5 * new_width,
            centre_y + 0.5 * new_height,
        ]
    ) / (CANVAS // 2)


def local_near(
    p2, p3, p4, p5, norm_gain, norm_bias, fc6_weight, fc6_bias, fc7_weight, fc7_bias,
    cls_weight, cls_bias, box_weight, box_bias, roi_boxes, roi_level, roi_image,
    canvas_offsets, labels, target_boxes, valid,
):
    channels = p2.shape[1]
    rois = roi_level.shape[0]
    cols = lax.axis_size("col")
    rows = lax.axis_size("roi")
    piece = fc6_bias.shape[0]
    high = rows // cols
    few = channels // high
    planes = (p2, p3, p4, p5)
    pixels = rows * sum(plane.shape[2] for plane in planes)
    ring = ring_of(rows)
    per = fc7_bias.shape[0]
    classes, boxes = cls_weight.shape[1], box_weight.shape[1]
    bf16, f32 = jnp.bfloat16, jnp.float32

    block = fc6_weight.reshape(few, 7, 7, piece)
    block = jnp.pad(block, ((0, 0), (0, 0), (0, 1), (0, 0))).reshape(few, 7, 2, 4, piece)
    block = block.transpose(3, 1, 2, 0, 4).reshape(2 * len(USED), few, piece)
    block = jnp.concatenate([block[:LEADING], block[LEADING::2]])
    pairs = []
    for kappa in range(cols):
        for block_at in range(cols):
            for half in range(high):
                plane = (2 * (block_at % 2) + block_at // 2 + kappa) % cols
                source = (kappa * high + half) * cols + block_at
                pairs.append((source, (plane * high + half) * cols + kappa))
    block = lax.ppermute(block, ("roi", "col"), pairs)

    head = jnp.concatenate([cls_weight, box_weight, fc7_bias[:, None]], axis=1)
    head = jnp.pad(head, ((0, 0), (0, piece - head.shape[1])))
    bias_high = fc6_bias.astype(bf16)
    rest = fc6_bias - bias_high.astype(f32)
    bias_mid = rest.astype(bf16)
    bias_low = (rest - bias_mid.astype(f32)).astype(bf16)
    bias = jnp.concatenate([item.reshape(2, LANES) for item in (bias_high, bias_mid, bias_low)])
    bias = jnp.pad(bias, ((0, per - bias.shape[0]), (0, 0)))
    head = jnp.concatenate([head[:, :LANES], bias], axis=1)
    small = jnp.concatenate([fc7_weight, head], axis=0).reshape(SMALL, few, piece)

    def twice(vector):
        return jnp.concatenate([vector, vector])[None]

    count = jnp.sum(valid.astype(f32))
    norms = jnp.concatenate(
        [twice(norm_gain), jnp.full((1, LANES), count), twice(norm_bias), jnp.zeros((5, LANES), f32)]
    )

    picks = roi_image[None, :] == jnp.arange(4, dtype=jnp.int32)[:, None]
    shift_x = jnp.sum(jnp.where(picks, canvas_offsets[0][:, None], 0), axis=0)
    shift_y = jnp.sum(jnp.where(picks, canvas_offsets[1][:, None], 0), axis=0)
    floats, ints, order = region_tables(
        (roi_boxes[0] + shift_x).astype(f32),
        (roi_boxes[1] + shift_y).astype(f32),
        (roi_boxes[2] + shift_x).astype(f32),
        (roi_boxes[3] + shift_y).astype(f32),
        roi_level,
    )
    block = lax.optimization_barrier((block, floats, order))[0]
    pieces = lax.all_gather(block, "roi", axis=0, axis_index_groups=[ring])
    centred, weight, at_home = pool_maps(floats, ints, order, planes, rois)

    quarter = rois // cols
    first_row = lax.axis_index("col") * quarter
    mine_labels = lax.dynamic_slice_in_dim(labels, first_row, quarter)
    mine_valid = lax.dynamic_slice_in_dim(valid, first_row, quarter).astype(f32)
    mine_boxes = lax.dynamic_slice_in_dim(roi_boxes, first_row, quarter, axis=1).astype(f32)
    mine_goals = lax.dynamic_slice_in_dim(target_boxes, first_row, quarter, axis=1).astype(f32)
    foreground = mine_valid * (mine_labels > 0).astype(f32)
    lane = jnp.arange(LANES, dtype=jnp.int32)[None, :]
    after = LANES - classes - boxes
    facts = jnp.stack(
        [
            jnp.pad(targets_of(mine_boxes, mine_goals), ((0, 0), (classes, after))),
            (mine_labels[:, None] == lane).astype(f32),
            jnp.where(
                lane < classes,
                mine_valid[:, None],
                jnp.where(lane < classes + boxes, foreground[:, None], 0.0),
            ),
        ]
    )
    score_bias = jnp.pad(jnp.concatenate([cls_bias, box_bias]), (0, after))[None]
    small, facts, score_bias, _ = lax.optimization_barrier((small, facts, score_bias, at_home))
    small, stats = gather_small(small, norms, at_home, rows, cols, float(pixels))
    pooled, g6_all, g7, hid6, hid7, gs, scores, losses = run_head(
        centred, weight, stats, facts, score_bias, small, pieces, rows, cols, classes, boxes
    )
    decoded = decode(mine_boxes, scores[:, classes : classes + boxes])

    terms, g7_all, losses_all = wide_grads(
        pooled, g6_all, g7, hid6, hid7, gs, losses, rows, cols
    )
    wide_rows = terms.shape[1]
    term = lax.psum_scatter(
        terms.reshape(rows * wide_rows, piece), "roi", scatter_dimension=0, tiled=True,
        axis_index_groups=[ring],
    )
    grads, totals, base, slope = pool_grads(
        g6_all, g7_all, losses_all, centred, weight, stats, pieces, rows, cols,
        float(pixels),
    )
    input_grads, few_grads = unpool_all(
        floats, ints, order, base, slope, totals, grads, planes, rois, rows, cols, classes, boxes,
        piece,
    )
    term = lax.optimization_barrier((term, input_grads[3]))[0]
    fc6_weight_grad, fc7_weight_grad, cls_weight_grad, box_weight_grad = restore(
        deliver(term, rows, cols, few), term, few, fc7_weight.shape[0], per, classes, boxes
    )
    (
        norm_gain_grad, norm_bias_grad, fc6_bias_grad, fc7_bias_grad, class_bias_grad,
        box_bias_grad, cls_loss, box_loss,
    ) = few_grads
    return (
        cls_loss[0, 0],
        box_loss[0, 0],
        decoded,
        *input_grads,
        norm_gain_grad,
        norm_bias_grad,
        fc6_weight_grad,
        fc6_bias_grad,
        fc7_weight_grad,
        fc7_bias_grad,
        cls_weight_grad,
        class_bias_grad,
        box_weight_grad,
        box_bias_grad,
    )


def solution(mesh):
    near = mesh.shape["roi"] == 2 * mesh.shape["col"] and mesh.shape["col"] == 4
    return jax.shard_map(
        local_near if near else local,
        mesh=mesh,
        in_specs=(
            P("roi", "col", None),
            P("roi", "col", None),
            P("roi", "col", None),
            P("roi", "col", None),
            P("col"),
            P("col"),
            P("roi", "col"),
            P("col"),
            P("roi", "col"),
            P(("roi", "col")),
            P(("roi", "col"), None),
            P(),
            P(("roi", "col"), None),
            P(),
            P(None, "roi"),
            P("roi"),
            P("roi"),
            P(None, "roi"),
            P("roi"),
            P(None, "roi"),
            P("roi"),
        ),
        out_specs=(
            P(),
            P(),
            P(None, ("roi", "col")),
            P("roi", "col", None),
            P("roi", "col", None),
            P("roi", "col", None),
            P("roi", "col", None),
            P("col"),
            P("col"),
            P("roi", "col"),
            P("col"),
            P("roi", "col"),
            P(("roi", "col")),
            P(("roi", "col"), None),
            P(),
            P(("roi", "col"), None),
            P(),
        ),
        check_vma=False,
    )
```
